32 devices in a mesh: seq: 2 (over x), dp: 16 (over z, y, core).
Axes of the slice: x: 2, y: 2, z: 4, core: 2. Of those that a mesh axis runs over, the one named last changes fastest.
Arguments:
- tokens: bfloat16 [16384, 1536], P(('dp', 'seq')), may hold values from -6 to 6
- cotangent: bfloat16 [16384, 1536], P(('dp', 'seq')), may hold values from -6 to 6
- in_weight: float32 [1536, 6448], P(('seq', 'dp')), may hold values from -0.15625 to 0.15625
- in_moment: float32 [1536, 6448], P(('seq', 'dp')), may hold values from -24 to 24
- in_square: float32 [1536, 6448], P(('seq', 'dp')), may hold values from 1.47456 to 5.89824
- out_weight: float32 [3072, 1536], P(('seq', 'dp')), may hold values from -0.109375 to 0.109375
- out_moment: float32 [3072, 1536], P(('seq', 'dp')), may hold values from -80 to 80
- out_square: float32 [3072, 1536], P(('seq', 'dp')), may hold values from 16.384 to 65.536
- conv_table: float32 [5, 3328], P(None, ('seq', 'dp')), may hold values from -3 to 3
- conv_moment: float32 [5, 3328], P(None, ('seq', 'dp')), may hold values from -24 to 24
- conv_square: float32 [5, 3328], P(None, ('seq', 'dp')), may hold values from 1.47456 to 5.89824
- norm_gains: float32 [4608], P(('seq', 'dp')), may hold values from 0.5 to 1.5
- gain_moment: float32 [4608], P(('seq', 'dp')), may hold values from -48 to 48
- gain_square: float32 [4608], P(('seq', 'dp')), may hold values from 5.89824 to 23.59296
- head_table: float32 [3, 48], replicated, may hold values from -10 to 1.5, as said below
- head_moment: float32 [3, 48], replicated, may hold values from -80 to 80
- head_square: float32 [3, 48], replicated, may hold values from 16.384 to 65.536
Outputs:
- layer_out: float32 [16384, 1536], P(('dp', 'seq'))
- tokens_grad: float32 [16384, 1536], P(('dp', 'seq'))
- in_weight_new: float32 [1536, 6448], P(('seq', 'dp'))
- in_moment_new: float32 [1536, 6448], P(('seq', 'dp'))
- in_square_new: float32 [1536, 6448], P(('seq', 'dp'))
- out_weight_new: float32 [3072, 1536], P(('seq', 'dp'))
- out_moment_new: float32 [3072, 1536], P(('seq', 'dp'))
- out_square_new: float32 [3072, 1536], P(('seq', 'dp'))
- conv_table_new: float32 [5, 3328], P(None, ('seq', 'dp'))
- conv_moment_new: float32 [5, 3328], P(None, ('seq', 'dp'))
- conv_square_new: float32 [5, 3328], P(None, ('seq', 'dp'))
- norm_gains_new: float32 [4608], P(('seq', 'dp'))
- gain_moment_new: float32 [4608], P(('seq', 'dp'))
- gain_square_new: float32 [4608], P(('seq', 'dp'))
- head_table_new: float32 [3, 48], replicated
- head_moment_new: float32 [3, 48], replicated
- head_square_new: float32 [3, 48], replicated
The draws below stay inside these ranges and needn't reach their ends.
Inputs may be any that keep to these rules, and one draw needn't show every extreme that they name: `head_table`: row 0 holds the logarithm of each head's decay rate, row 1 its step bias, row 2 its skip factor, which lies between 0.5 and 1.5.
All inputs are finite; a program needn't handle non-finite values.
Results may differ from the reference program's by a relative error of at most 0.012.
The reference program's roundings to bfloat16 on the way count: a program that leaves them out, or rounds other values in their place, can miss the bound.
Values may be sent and summed in bfloat16 or wider, within the bound.
No kernel may reach another device: no remote copies, remote signals or barrier semaphores. Data moves between devices by JAX's collectives and lax.ppermute only.
A program may use at most 160 MiB of HBM per device.

```python
import math
import jax
import jax.numpy as jnp
from jax import lax

D = 1536
HEADS = 48
HEAD_DIM = 64
STATE = 128
CONV = 4
BLOCK = 256
STEP = 10
DI = 3072
CH = 3328
PROJ = 6448
SEQ_LEN = 1024
TOKENS = 16384
N_DP = 16


def draw_head_table(key, part):
    key = jax.random.fold_in(key, 7)
    rate_key, bias_key, skip_key = jax.random.split(key, 3)
    low_rate = 0.2 / SEQ_LEN
    high_rate = 0.03
    exponents = jax.random.uniform(rate_key, (HEADS,), jnp.float32, math.log(low_rate), math.log(high_rate))
    biases = jax.random.uniform(bias_key, (HEADS,), jnp.float32, 0.3, 0.8)
    skips = jax.random.uniform(skip_key, (HEADS,), jnp.float32, 0.5, 1.5)
    return jnp.stack([exponents, biases, skips]).astype(jnp.float32)


def shard_levels(own_key, shape, cuts, smallest, high):
    level, own = 1.0, jax.random.fold_in(own_key, 6)
    for dim, shards_of in cuts:
        draws = jnp.exp(jax.random.uniform(jax.random.fold_in(own, dim), (shards_of,), jnp.float32, smallest / len(cuts), high / len(cuts)))
        level = level * jnp.repeat(draws, shape[dim] // shards_of).reshape([-1 if axis == dim else 1 for axis in range(len(shape))])
    return level


def gaussian(rng, extent, deviation, reach, shards=(), held_as=jnp.bfloat16):
    array = jax.random.normal(rng, extent, jnp.float32) * deviation
    if len(shards) > 0:
        array = shard_levels(rng, extent, shards, -0.22, 0.18) * array
    return jnp.clip(array, min=-reach, max=reach).astype(held_as)


def setup_inputs(seed: int = 0) -> dict:
    arg_keys = jax.random.split(jax.random.key(seed), 18)
    return {
        "tokens": gaussian(arg_keys[0], (TOKENS, D), 1.0, 6.0, ((0, 32),)),
        "cotangent": gaussian(arg_keys[1], (TOKENS, D), 1.0, 6.0, ((0, 32),)),
        "in_weight": gaussian(arg_keys[2], (D, PROJ), D ** -0.5, 0.15625, ((0, 32),), jnp.float32),
        "in_moment": gaussian(arg_keys[3], (D, PROJ), (0.033 * TOKENS ** 0.5), 24.0, ((0, 32),), jnp.float32),
        "in_square": jnp.clip(jnp.exp(math.log(5.89824) - 1.3862944 * jax.random.uniform(arg_keys[4], (D, PROJ), jnp.float32) ** shard_levels(arg_keys[4], (D, PROJ), ((0, 32),), -0.2, 0.2)), 1.47456, 5.89824),
        "out_weight": gaussian(arg_keys[5], (DI, D), DI ** -0.5, 0.109375, ((0, 32),), jnp.float32),
        "out_moment": gaussian(arg_keys[6], (DI, D), (0.11 * TOKENS ** 0.5), 80.0, ((0, 32),), jnp.float32),
        "out_square": jnp.clip(jnp.exp(math.log(65.536) - 1.3862944 * jax.random.uniform(arg_keys[7], (DI, D), jnp.float32) ** shard_levels(arg_keys[7], (DI, D), ((0, 32),), -0.2, 0.2)), 16.384, 65.536),
        "conv_table": gaussian(arg_keys[8], (CONV + 1, CH), CONV ** -0.5, 3.0, ((1, 32),), jnp.float32),
        "conv_moment": gaussian(arg_keys[9], (CONV + 1, CH), (0.033 * TOKENS ** 0.5), 24.0, ((1, 32),), jnp.float32),
        "conv_square": jnp.clip(jnp.exp(math.log(5.89824) - 1.3862944 * jax.random.uniform(arg_keys[10], (CONV + 1, CH), jnp.float32) ** shard_levels(arg_keys[10], (CONV + 1, CH), ((1, 32),), -0.2, 0.2)), 1.47456, 5.89824),
        "norm_gains": jnp.clip(1.0 + 0.1 * jax.random.normal(arg_keys[11], (D + DI,), jnp.float32), 0.5, 1.5),
        "gain_moment": gaussian(arg_keys[12], (D + DI,), (0.066 * TOKENS ** 0.5), 48.0, ((0, 32),), jnp.float32),
        "gain_square": jnp.clip(jnp.exp(math.log(23.59296) - 1.3862944 * jax.random.uniform(arg_keys[13], (D + DI,), jnp.float32) ** shard_levels(arg_keys[13], (D + DI,), ((0, 32),), -0.2, 0.2)), 5.89824, 23.59296),
        "head_table": draw_head_table(jax.random.fold_in(arg_keys[17], 71), 0),
        "head_moment": gaussian(arg_keys[15], (3, HEADS), (0.11 * TOKENS ** 0.5), 80.0, (), jnp.float32),
        "head_square": jnp.clip(jnp.exp(jax.random.uniform(arg_keys[16], (3, HEADS), jnp.float32, math.log(16.384), math.log(65.536))), 16.384, 65.536),
    }


@jax.custom_vjp
def low(v):
    return lax.optimization_barrier(v.astype(jnp.bfloat16)).astype(jnp.float32)

@jax.custom_vjp
def low_back(v):
    return v

def low_keep(v):
    return (low(v), None)

def low_pass(kept, grad):
    return (grad,)

def back_keep(v):
    return (v, None)

def back_low(kept, grad):
    return (low(grad),)
low.defvjp(low_keep, low_pass)
low_back.defvjp(back_keep, back_low)
norm_epsilon = 1e-05
adam_epsilon = 1e-08
beta_first = 0.9
beta_second = 0.999
rate_matrix = 0.05
rate_vector = 0.5
rate_heads = 2.0
weight_decay = 0.1
highest = lax.Precision.HIGHEST

def block_step(memory, pieces):
    payload, writer, reader, log_rates, step_sizes = pieces
    length = log_rates.shape[0]
    summed = jnp.cumsum(log_rates, axis=0).T
    positions = jnp.arange(length)
    causal = positions[:, None] >= positions[None, :]
    spread = summed[:, :, None] - summed[:, None, :]
    weights = jnp.exp(jnp.where(causal[None], spread, -jnp.inf))
    affinity = jnp.dot(reader, writer.T, precision=highest)
    weights = weights * affinity[None] * step_sizes.T[:, None, :]
    within = jnp.einsum('hts,shp->thp', weights, payload, precision=highest)
    carried = jnp.einsum('tn,hpn->thp', reader, memory, precision=highest) * jnp.exp(summed.T)[:, :, None]
    remain = jnp.exp(summed[:, -1:] - summed).T * step_sizes
    memory_new = jnp.exp(summed[:, -1])[:, None, None] * memory + jnp.einsum('shp,sn->hpn', payload * remain[:, :, None], writer, precision=highest)
    return (memory_new, within + carried)

def layer_forward(tokens_seq, in_weight, out_weight, conv_table, norm_gains, head_table):
    in_cast = low(in_weight)
    out_cast = low(out_weight)
    conv_cast = low(conv_table)
    gains_cast = low(norm_gains)
    first_gain = gains_cast[:D]
    second_gain = gains_cast[D:]
    inv_one = lax.rsqrt(lax.optimization_barrier(jnp.mean(tokens_seq * tokens_seq, axis=-1, keepdims=True)) + norm_epsilon)
    normed = low(tokens_seq * inv_one * first_gain)
    projected = low_back(jnp.dot(normed, in_cast, precision=highest))
    gate_part = projected[:, :DI]
    conv_in = projected[:, DI:DI + CH]
    step_raw = projected[:, DI + CH:]
    padded = jnp.concatenate([jnp.zeros((CONV - 1, CH), jnp.float32), conv_in], axis=0)
    filtered = conv_cast[CONV] + sum((conv_cast[offset] * padded[offset:offset + SEQ_LEN] for offset in range(CONV)))
    active = jax.nn.silu(filtered)
    payload = active[:, :DI].reshape(SEQ_LEN, HEADS, HEAD_DIM)
    writer = active[:, DI:DI + STATE]
    reader = active[:, DI + STATE:]
    step_sizes = jax.nn.softplus(step_raw + head_table[1])
    log_rates = -jnp.exp(head_table[0]) * step_sizes
    block_count = SEQ_LEN // BLOCK
    blocks = (payload.reshape(block_count, BLOCK, HEADS, HEAD_DIM), writer.reshape(block_count, BLOCK, STATE), reader.reshape(block_count, BLOCK, STATE), log_rates.reshape(block_count, BLOCK, HEADS), step_sizes.reshape(block_count, BLOCK, HEADS))
    final_memory, outputs = lax.scan(jax.checkpoint(block_step), jnp.zeros((HEADS, HEAD_DIM, STATE), jnp.float32), blocks)
    scanned = outputs.reshape(SEQ_LEN, HEADS, HEAD_DIM) + payload * head_table[2][:, None]
    gated_out = scanned.reshape(SEQ_LEN, DI) * jax.nn.silu(gate_part)
    inv_two = lax.rsqrt(lax.optimization_barrier(jnp.mean(gated_out * gated_out, axis=-1, keepdims=True)) + norm_epsilon)
    shaped = low(gated_out * inv_two * second_gain)
    return tokens_seq + jnp.dot(shaped, out_cast, precision=highest)

def adamw_step(weight, moment, square, gradient, step_rate, decay_rate):
    moment_new = beta_first * moment + (1.0 - beta_first) * gradient
    square_new = beta_second * square + (1.0 - beta_second) * gradient * gradient
    first_fix = moment_new / (1.0 - beta_first ** STEP)
    second_fix = square_new / (1.0 - beta_second ** STEP)
    weight_new = weight - step_rate * (first_fix / (jnp.sqrt(second_fix) + adam_epsilon) + decay_rate * weight)
    return (weight_new, moment_new, square_new)

def reference(tokens, cotangent, in_weight, in_moment, in_square, out_weight, out_moment, out_square, conv_table, conv_moment, conv_square, norm_gains, gain_moment, gain_square, head_table, head_moment, head_square):
    sequences = tokens.reshape(N_DP, SEQ_LEN, D)
    directions = cotangent.reshape(N_DP, SEQ_LEN, D)
    params = (in_weight, out_weight, conv_table, norm_gains, head_table)

    def per_sequence(totals, pair_in):
        tokens_seq, cot_seq = pair_in
        result, pullback = jax.vjp(layer_forward, tokens_seq.astype(jnp.float32), in_weight, out_weight, conv_table, norm_gains, head_table)
        gradients = pullback(cot_seq.astype(jnp.float32))
        totals = tuple((accumulated + fresh for accumulated, fresh in zip(totals, gradients[1:])))
        return (totals, (result, gradients[0]))
    starting = tuple((jnp.zeros_like(parameter) for parameter in params))
    totals, (results, input_grads) = lax.scan(per_sequence, starting, (sequences, directions))
    in_grad, out_grad, conv_grad, gains_grad, head_grad = totals
    in_new = adamw_step(in_weight, in_moment, in_square, in_grad, rate_matrix, weight_decay)
    out_new = adamw_step(out_weight, out_moment, out_square, out_grad, rate_matrix, weight_decay)
    conv_new = adamw_step(conv_table, conv_moment, conv_square, conv_grad, rate_vector, 0.0)
    gains_new = adamw_step(norm_gains, gain_moment, gain_square, gains_grad, rate_vector, 0.0)
    head_new = adamw_step(head_table, head_moment, head_square, head_grad, rate_heads, 0.0)
    return (results.reshape(TOKENS, D), input_grads.reshape(TOKENS, D), in_new[0], in_new[1], in_new[2], out_new[0], out_new[1], out_new[2], conv_new[0], conv_new[1], conv_new[2], gains_new[0], gains_new[1], gains_new[2], head_new[0], head_new[1], head_new[2])
```

```python
import functools

import jax
import jax.numpy as jnp
from jax import lax
from jax.experimental import pallas as pl
from jax.experimental.pallas import tpu as pltpu
from jax.sharding import PartitionSpec as P

D = 1536
HEADS = 48
HEAD_DIM = 64
STATE = 128
CONV = 4
STEP = 10
DI = 3072
CH = 3328

QUARTERS = 4
QH = HEADS // QUARTERS
QW = DI // QUARTERS
QC = QW + 2 * STATE
WIDE = QC + 128
LEN = 256
ROWS = 1024
HALF = ROWS // 2
BLOCKS = ROWS // LEN
SMALL = 768

norm_epsilon = 1e-05
adam_epsilon = 1e-08
beta_first = 0.9
beta_second = 0.999
rate_matrix = 0.05
rate_vector = 0.5
rate_heads = 2.0
weight_decay = 0.1
LOG2E = 1.4426950408889634

f32 = jnp.float32
bf16 = jnp.bfloat16
NN = (((1,), (0,)), ((), ()))
NT = (((1,), (1,)), ((), ()))
TN = (((0,), (0,)), ((), ()))
MIB = 1024 * 1024


def mm(a, b, dims=NN):
    return lax.dot_general(a, b, dims, preferred_element_type=f32)


def mm_exact(a, b, dims=NN):
    return lax.dot_general(
        a, b, dims, precision=lax.Precision.HIGHEST, preferred_element_type=f32
    )


def spread_heads(columns):
    rows = columns.shape[0]
    low = lax.broadcasted_iota(jnp.int32, (rows, 128), 1) < HEAD_DIM
    parts = []
    for pair in range(QH // 2):
        first = jnp.broadcast_to(columns[:, 2 * pair : 2 * pair + 1], (rows, 128))
        second = jnp.broadcast_to(columns[:, 2 * pair + 1 : 2 * pair + 2], (rows, 128))
        parts.append(jnp.where(low, first, second))
    return jnp.concatenate(parts, axis=1)


def softplus(v):
    return jnp.maximum(v, 0.0) + jnp.log1p(jnp.exp(-jnp.abs(v)))


def triangle(lower):
    rows = lax.broadcasted_iota(jnp.int32, (LEN, LEN), 0)
    cols = lax.broadcasted_iota(jnp.int32, (LEN, LEN), 1)
    return rows >= cols if lower else rows <= cols


def halves(pair):
    low = lax.broadcasted_iota(jnp.int32, pair.shape, 1) < HEAD_DIM
    zero = jnp.zeros_like(pair)
    return jnp.where(low, pair, zero), jnp.where(low, zero, pair)


def filter_rows(ext, conv_ref):
    total = conv_ref[CONV : CONV + 1, :]
    for k in range(CONV):
        total = total + conv_ref[k : k + 1, :] * ext[5 + k : 5 + k + LEN, :]
    return total


def forward_kernel(
    place, tok, gain, w, conv, head, skip, normed_out, proj_out, scanned_out, mem_out, ext, mem
):
    j = pl.program_id(0)

    @pl.when(j == 0)
    def _():
        ext[0:8, :] = jnp.zeros((8, QC), f32)
        mem[...] = jnp.zeros_like(mem)

    wide = tok[...].astype(f32)
    inv_one = lax.rsqrt(jnp.mean(wide * wide, axis=1, keepdims=True) + norm_epsilon)
    normed = (wide * inv_one * gain[...]).astype(bf16)
    normed_out[...] = normed
    proj = mm(normed, w[...])
    proj_out[...] = proj
    ext[8 : 8 + LEN, :] = proj[:, :QC]
    filtered = filter_rows(ext, conv)
    ext[0:8, :] = ext[LEN : LEN + 8, :]
    active = filtered * jax.nn.sigmoid(filtered)
    payload = active[:, :QW]
    writer = active[:, QW : QW + STATE].astype(bf16)
    reader = active[:, QW + STATE :].astype(bf16)

    steps = softplus(proj[:, QC:] + head[1:2, :])
    rates = head[0:1, :] * steps
    causal = triangle(True)
    summed = mm_exact(causal.astype(f32), rates) * LOG2E
    across = summed.T
    affinity = jnp.where(causal, mm(reader, writer, NT), 0.0)

    dosed = payload * spread_heads(steps)
    dosed_low = dosed.astype(bf16)
    state = mem[...]
    mem_out[0] = state
    grown = jnp.exp2(spread_heads(summed))
    carried = mm(reader, state.astype(bf16)) * grown
    within = []
    for pair in range(QH // 2):
        weights = []
        for h in (2 * pair, 2 * pair + 1):
            gap = jnp.minimum(summed[:, h : h + 1] - across[h : h + 1, :], 0.0)
            weights.append((jnp.exp2(gap) * affinity).astype(bf16))
        first, second = halves(dosed_low[:, 128 * pair : 128 * pair + 128])
        within.append(
            mm(jnp.concatenate(weights, axis=1), jnp.concatenate([first, second], axis=0))
        )
    scanned_out[...] = jnp.concatenate(within, axis=1) + carried + payload * skip[...]

    last = summed[LEN - 1 : LEN, :]
    remain = jnp.exp2(spread_heads(last - summed))
    added = mm(writer, (dosed * remain).astype(bf16), TN)
    mem[...] = state * jnp.exp2(spread_heads(last)) + added


def gate_kernel(place, normed, w_gate, cot, w_out, gain, scanned, gate_out, shaped_grad_out, stats_out):
    gate = mm(normed[...], w_gate[...])
    grad_shaped = mm(cot[...], w_out[...], NT)
    gate_out[...] = gate
    shaped_grad_out[...] = grad_shaped
    gated = scanned[...] * (gate * jax.nn.sigmoid(gate))
    squares = jnp.sum(gated * gated, axis=1, keepdims=True)
    inner = jnp.sum(grad_shaped * gain[...] * gated, axis=1, keepdims=True)
    lane = lax.broadcasted_iota(jnp.int32, (LEN, 128), 1)
    both = jnp.where(lane == 0, squares, jnp.where(lane == 1, inner, 0.0))
    stats_out[...] = both.T[0:8, :]


def finish_kernel(
    place, stats, gate_in, grad_shaped_in, scanned_in, w_out, gain,
    shaped_out, layer_out, scan_grad_out, gate_grad_out, gain_grad,
):
    j = pl.program_id(0)
    table = jnp.concatenate([stats[...], jnp.zeros((120, LEN), f32)], axis=0).T
    inv_two = lax.rsqrt(table[:, 0:1] / DI + norm_epsilon)
    mean = inv_two * table[:, 1:2] / DI
    gate = gate_in[...]
    scanned = scanned_in[...]
    grad_shaped = grad_shaped_in[...]
    sig = jax.nn.sigmoid(gate)
    lift = gate * sig
    unit = scanned * lift * inv_two
    shaped = (unit * gain[...]).astype(bf16)
    shaped_out[...] = shaped
    layer_out[...] = mm(shaped, w_out[...]).astype(bf16)
    grad_gated = inv_two * (grad_shaped * gain[...] - unit * mean)
    scan_grad_out[...] = grad_gated * lift
    gate_grad_out[...] = (grad_gated * scanned * sig * (1.0 + gate * (1.0 - sig))).astype(bf16)

    @pl.when(j == 0)
    def _():
        gain_grad[...] = jnp.zeros_like(gain_grad)

    gain_grad[0:1, :] += jnp.sum(grad_shaped * unit, axis=0, keepdims=True)


def backward_kernel(
    proj_in, before, scanned_in, grad_in, mem_in, conv, head, skip,
    wide_out, conv_grad, head_grad, skip_grad, ext, later, grad_mem,
):
    i = pl.program_id(0)
    j = BLOCKS - 1 - i

    @pl.when(i == 0)
    def _():
        later[LEN : LEN + 8, :] = jnp.zeros((8, QC), f32)
        grad_mem[...] = jnp.zeros_like(grad_mem)
        conv_grad[...] = jnp.zeros_like(conv_grad)
        head_grad[...] = jnp.zeros_like(head_grad)
        skip_grad[...] = jnp.zeros_like(skip_grad)

    @pl.when(i > 0)
    def _():
        later[LEN : LEN + 8, :] = later[0:8, :]

    conv_in = proj_in[:, :QC]
    ext[0:8, :] = jnp.where(j > 0, before[:, :QC], 0.0)
    ext[8 : 8 + LEN, :] = conv_in
    filtered = filter_rows(ext, conv)
    sig = jax.nn.sigmoid(filtered)
    active = filtered * sig
    slope = sig * (1.0 + filtered * (1.0 - sig))
    payload = active[:, :QW]
    writer = active[:, QW : QW + STATE].astype(bf16)
    reader = active[:, QW + STATE :].astype(bf16)

    raw = proj_in[:, QC:] + head[1:2, :]
    steps = softplus(raw)
    rates = head[0:1, :] * steps
    summed = mm_exact(triangle(True).astype(f32), rates) * LOG2E
    across = summed.T
    upper = triangle(False)
    affinity = jnp.where(upper, mm(writer, reader, NT), 0.0)

    grad = grad_in[...]
    grad_low = grad.astype(bf16)
    dose = spread_heads(steps)
    dosed = payload * dose
    dosed_low = dosed.astype(bf16)
    state = mem_in[0]
    state_grad = grad_mem[...]
    state_grad_low = state_grad.astype(bf16)
    last = summed[LEN - 1 : LEN, :]
    remain = jnp.exp2(spread_heads(last - summed))
    from_state = mm(writer, state_grad_low) * remain

    mixed = jnp.zeros((LEN, LEN), f32)
    within = []
    for pair in range(QH // 2):
        lanes = slice(128 * pair, 128 * pair + 128)
        grads = halves(grad_low[:, lanes])
        doses = halves(dosed_low[:, lanes])
        weights = []
        for h, dosed_half in zip((2 * pair, 2 * pair + 1), doses):
            gap = jnp.minimum(across[h : h + 1, :] - summed[:, h : h + 1], 0.0)
            decay = jnp.exp2(gap)
            weights.append((decay * affinity).astype(bf16))
            mixed = mixed + decay * mm(dosed_half, grad_low[:, lanes], NT)
        within.append(mm(jnp.concatenate(weights, axis=1), jnp.concatenate(grads, axis=0)))
    unit = jnp.concatenate(within, axis=1) + from_state

    payload_grad = dose * unit + skip[...] * grad
    core = scanned_in[...] - payload * skip[...]
    dosed_wide = dosed_low.astype(f32)
    balance = grad_low.astype(f32) * core - dosed_wide * unit
    high_part = balance.astype(bf16)
    low_part = (balance - high_part.astype(f32)).astype(bf16)
    heads_of = (
        lax.broadcasted_iota(jnp.int32, (QW, 128), 0) // HEAD_DIM
        == lax.broadcasted_iota(jnp.int32, (QW, 128), 1)
    ).astype(f32)
    heads_low = heads_of.astype(bf16)
    balance_sum = mm(high_part, heads_low) + mm(low_part, heads_low)
    direct = mm((payload * unit).astype(bf16), heads_low)
    decay_last = jnp.exp2(spread_heads(last))
    at_end = jnp.sum(dosed_wide * from_state, axis=0, keepdims=True) + decay_last * jnp.sum(
        state_grad * state, axis=0, keepdims=True
    )
    end_sum = mm_exact(jnp.broadcast_to(at_end, (8, QW)), heads_of)[0:1, :]
    rate_grad = mm_exact(upper.astype(f32), balance_sum) + end_sum
    step_grad = direct + head[0:1, :] * rate_grad
    raw_grad = step_grad * jax.nn.sigmoid(raw)
    head_grad[0:1, :] += jnp.sum(rate_grad * rates, axis=0, keepdims=True)
    head_grad[1:2, :] += jnp.sum(raw_grad, axis=0, keepdims=True)
    skip_grad[0:1, :] += jnp.sum(grad * payload, axis=0, keepdims=True)

    grown_grad = (jnp.exp2(spread_heads(summed)) * grad).astype(bf16)
    kept = (remain * dosed).astype(bf16)
    mixed_low = jnp.where(upper, mixed, 0.0).astype(bf16)
    writer_grad = mm(mixed_low, reader) + mm(kept, state_grad_low, NT)
    reader_grad = mm(mixed_low, writer, TN) + mm(grown_grad, state.astype(bf16), NT)
    grad_mem[...] = decay_last * state_grad + mm(reader, grown_grad, TN)

    filtered_grad = jnp.concatenate([payload_grad, writer_grad, reader_grad], axis=1) * slope
    later[0:LEN, :] = filtered_grad
    back = None
    for k in range(CONV):
        ahead = later[CONV - 1 - k : CONV - 1 - k + LEN, :]
        conv_grad[k : k + 1, :] += jnp.sum(ahead * conv_in, axis=0, keepdims=True)
        term = conv[k : k + 1, :] * ahead
        back = term if back is None else back + term
    conv_grad[CONV : CONV + 1, :] += jnp.sum(filtered_grad, axis=0, keepdims=True)
    wide_out[:, :QC] = back.astype(bf16)
    wide_out[:, QC:] = raw_grad.astype(bf16)


def outer_kernel(left_a, left_b, right_a, right_b, out):
    out[...] = (mm(left_a[...], right_a[...], TN) + mm(left_b[...], right_b[...], TN)).astype(bf16)


def input_grad_kernel(place, gate_grad, wide_grad, w_gate, w_wide, tok, out, gain_grad):
    grad = mm(gate_grad[...], w_gate[...], NT) + mm(wide_grad[...], w_wide[...], NT)
    out[...] = grad.astype(bf16)
    wide = tok[...].astype(f32)
    inv_one = lax.rsqrt(jnp.mean(wide * wide, axis=1, keepdims=True) + norm_epsilon)

    @pl.when(pl.program_id(0) == 0)
    def _():
        gain_grad[...] = jnp.zeros_like(gain_grad)

    gain_grad[0:1, :] += jnp.sum(grad * (wide * inv_one), axis=0, keepdims=True)


def own_first(j, place):
    per = BLOCKS // 2
    half = j // per
    side = place[0]
    return (half + side - 2 * half * side) * per + j % per


def rows_of(width, moved=False):
    if moved:
        return pl.BlockSpec((LEN, width), lambda j, place: (own_first(j, place), 0))
    return pl.BlockSpec((LEN, width), lambda j, *_: (j, 0))


def whole(*shape):
    return pl.BlockSpec(shape, lambda j, *_: (0,) * len(shape))


def params(mib):
    return pltpu.CompilerParams(
        vmem_limit_bytes=mib * MIB, dimension_semantics=("arbitrary",)
    )


def shape(dims, dtype):
    return jax.ShapeDtypeStruct(dims, dtype)


def cost(flops, read):
    return pl.CostEstimate(flops=int(flops), bytes_accessed=int(read), transcendentals=0)


def run_forward(place, tok, gain, w, conv, head, skip):
    return pl.pallas_call(
        forward_kernel,
        grid_spec=pltpu.PrefetchScalarGridSpec(
            num_scalar_prefetch=1,
            grid=(BLOCKS,),
            in_specs=[
                rows_of(D, True), whole(1, D), whole(D, WIDE), whole(8, QC), whole(8, 128),
                whole(1, QW),
            ],
            out_specs=[
                rows_of(D), rows_of(WIDE), rows_of(QW),
                pl.BlockSpec((1, STATE, QW), lambda j, *_: (j, 0, 0)),
            ],
            scratch_shapes=[pltpu.VMEM((LEN + 8, QC), f32), pltpu.VMEM((STATE, QW), f32)],
        ),
        out_shape=[
            shape((ROWS, D), bf16), shape((ROWS, WIDE), f32), shape((ROWS, QW), f32),
            shape((BLOCKS, STATE, QW), f32),
        ],
        compiler_params=params(40),
        cost_estimate=cost(2 * ROWS * D * WIDE * 2, 20e6),
        name="forward_scan",
    )(place, tok, gain, w, conv, head, skip)


def run_gate(place, normed, w_gate, cot, w_out, gain, scanned):
    return pl.pallas_call(
        gate_kernel,
        grid_spec=pltpu.PrefetchScalarGridSpec(
            num_scalar_prefetch=1,
            grid=(BLOCKS,),
            in_specs=[
                rows_of(D), whole(D, QW), rows_of(D, True), whole(QW, D), whole(1, QW),
                rows_of(QW),
            ],
            out_specs=[
                rows_of(QW), rows_of(QW), pl.BlockSpec((8, LEN), lambda j, *_: (0, j)),
            ],
        ),
        out_shape=[shape((ROWS, QW), f32), shape((ROWS, QW), f32), shape((8, ROWS), f32)],
        compiler_params=params(32),
        cost_estimate=cost(4 * ROWS * D * QW, 20e6),
        name="gate_and_stats",
    )(place, normed, w_gate, cot, w_out, gain, scanned)


def run_finish(place, stats, gate, grad_shaped, scanned, w_out, gain):
    return pl.pallas_call(
        finish_kernel,
        grid_spec=pltpu.PrefetchScalarGridSpec(
            num_scalar_prefetch=1,
            grid=(BLOCKS,),
            in_specs=[
                pl.BlockSpec((8, LEN), lambda j, *_: (0, j)), rows_of(QW), rows_of(QW),
                rows_of(QW), whole(QW, D), whole(1, QW),
            ],
            out_specs=[
                rows_of(QW, True), rows_of(D, True), rows_of(QW), rows_of(QW), whole(8, QW),
            ],
        ),
        out_shape=[
            shape((ROWS, QW), bf16), shape((ROWS, D), bf16), shape((ROWS, QW), f32),
            shape((ROWS, QW), bf16), shape((8, QW), f32),
        ],
        compiler_params=params(32),
        cost_estimate=cost(4 * ROWS * D * QW, 20e6),
        name="finish",
    )(place, stats, gate, grad_shaped, scanned, w_out, gain)


def run_backward(proj, scanned, grad, mem, conv, head, skip):
    def back(width):
        return pl.BlockSpec((LEN, width), lambda i: (BLOCKS - 1 - i, 0))

    tiles = LEN // 8
    return pl.pallas_call(
        backward_kernel,
        grid=(BLOCKS,),
        in_specs=[
            back(WIDE),
            pl.BlockSpec((8, WIDE), lambda i: (jnp.maximum((BLOCKS - 1 - i) * tiles - 1, 0), 0)),
            back(QW), back(QW),
            pl.BlockSpec((1, STATE, QW), lambda i: (BLOCKS - 1 - i, 0, 0)),
            whole(8, QC), whole(8, 128), whole(1, QW),
        ],
        out_specs=[back(WIDE), whole(8, QC), whole(8, 128), whole(8, QW)],
        out_shape=[
            shape((ROWS, WIDE), bf16), shape((8, QC), f32), shape((8, 128), f32),
            shape((8, QW), f32),
        ],
        scratch_shapes=[
            pltpu.VMEM((LEN + 8, QC), f32), pltpu.VMEM((LEN + 8, QC), f32),
            pltpu.VMEM((STATE, QW), f32),
        ],
        compiler_params=params(40),
        cost_estimate=cost(2 * ROWS * D * WIDE * 4, 20e6),
        name="backward_scan",
    )(proj, proj, scanned, grad, mem, conv, head, skip)


def run_outer(left_a, left_b, right_a, right_b):
    tall, width = left_a.shape[1], right_a.shape[1]
    tile = 256
    return pl.pallas_call(
        outer_kernel,
        grid=(tall // tile,),
        in_specs=[
            pl.BlockSpec((ROWS, tile), lambda i: (0, i)),
            pl.BlockSpec((ROWS, tile), lambda i: (0, i)),
            whole(ROWS, width), whole(ROWS, width),
        ],
        out_specs=pl.BlockSpec((tile, width), lambda i: (i, 0)),
        out_shape=shape((tall, width), bf16),
        compiler_params=params(40),
        cost_estimate=cost(4 * ROWS * tall * width, 15e6),
        name="weight_grad",
    )(left_a, left_b, right_a, right_b)


def run_input_grad(place, gate_grad, wide_grad, w_gate, w_wide, tok):
    return pl.pallas_call(
        input_grad_kernel,
        grid_spec=pltpu.PrefetchScalarGridSpec(
            num_scalar_prefetch=1,
            grid=(BLOCKS,),
            in_specs=[
                rows_of(QW), rows_of(WIDE), whole(D, QW), whole(D, WIDE), rows_of(D, True),
            ],
            out_specs=[rows_of(D, True), whole(8, D)],
        ),
        out_shape=[shape((ROWS, D), bf16), shape((8, D), f32)],
        compiler_params=params(40),
        cost_estimate=cost(2 * ROWS * D * (QW + WIDE), 15e6),
        name="input_grad",
    )(place, gate_grad, wide_grad, w_gate, w_wide, tok)


def other_side(block):
    return lax.ppermute(block, "seq", [(0, 1), (1, 0)])


def flip(block, bit):
    count = lax.axis_size("dp")
    return lax.ppermute(block, "dp", [(d, d ^ bit) for d in range(count)])


def other_core(block):
    return flip(block, 1)


def beside(block):
    return flip(block, 2)


def along(block):
    count = lax.axis_size("dp")
    return lax.ppermute(block, "dp", [(d, (d + 4) % count) for d in range(count)])


def in_order(place, own, received, axis=0):
    return jnp.where(
        place == 0,
        jnp.concatenate([own, received], axis=axis),
        jnp.concatenate([received, own], axis=axis),
    )


def pick(block, place, axis):
    return lax.dynamic_index_in_dim(block, place, axis, False)


def spread(piece, groups, put, base):
    dp = lax.axis_index("dp")
    ring, beside_place = dp // 4, (dp // 2) % 2
    current = piece
    for hop in range(groups):
        if hop:
            current = along(current)
        neighbour = beside(current)
        origin = (ring + groups - hop) % groups
        base = put(base, current, 2 * origin + beside_place)
        base = put(base, neighbour, 2 * origin + 1 - beside_place)
    return base


def collect(block_of, groups):
    dp = lax.axis_index("dp")
    ring, beside_place = dp // 4, (dp // 2) % 2
    total = None
    for hop in range(groups):
        target = (ring + 2 * groups - 1 - hop) % groups
        received = beside(block_of(2 * target + 1 - beside_place))
        part = block_of(2 * target + beside_place).astype(f32) + received.astype(f32)
        if hop:
            part = part + total.astype(f32)
        total = part.astype(bf16)
        if hop < groups - 1:
            total = along(total)
    return total


def gather_small(row):
    dp = lax.axis_index("dp")
    bit = 1
    while bit < lax.axis_size("dp"):
        row = in_order((dp // bit) % 2, row, flip(row, bit))
        bit *= 2
    return in_order(lax.axis_index("seq"), row, other_side(row))


def sum_small(block):
    block = block + other_side(block)
    bit = 1
    while bit < lax.axis_size("dp"):
        block = block + flip(block, bit)
        bit *= 2
    return block


def adamw_step(weight, moment, square, gradient, step_rate, decay_rate):
    moment_new = beta_first * moment + (1.0 - beta_first) * gradient
    square_new = beta_second * square + (1.0 - beta_second) * gradient * gradient
    first_fix = moment_new / (1.0 - beta_first**STEP)
    second_fix = square_new / (1.0 - beta_second**STEP)
    weight_new = weight - step_rate * (
        first_fix / (jnp.sqrt(second_fix) + adam_epsilon) + decay_rate * weight
    )
    return (weight_new, moment_new, square_new)


def by_quarter(block):
    rows, width = block.shape
    return block.reshape(rows, QUARTERS, width // QUARTERS).transpose(1, 0, 2)


def to_group(quarters, side, core):
    _, rows, width = quarters.shape
    sides = quarters.reshape(2, 2, rows, width)
    pair = in_order(
        side, pick(sides, side, 0)[None], other_side(pick(sides, 1 - side, 0))[None]
    )
    return in_order(
        core, pick(pair, core, 1)[:, None], other_core(pick(pair, 1 - core, 1))[:, None], 1
    )


def from_group(piece, side, core):
    cores = in_order(core, pick(piece, core, 1)[None], other_core(pick(piece, 1 - core, 1))[None])
    sides = in_order(
        side, pick(cores, side, 1)[None], other_side(pick(cores, 1 - side, 1))[None]
    )
    return sides.reshape(QUARTERS, piece.shape[2], piece.shape[3])


def on_device(
    tokens,
    cotangent,
    in_weight,
    in_moment,
    in_square,
    out_weight,
    out_moment,
    out_square,
    conv_table,
    conv_moment,
    conv_square,
    norm_gains,
    gain_moment,
    gain_square,
    head_table,
    head_moment,
    head_square,
):
    side = lax.axis_index("seq")
    dp = lax.axis_index("dp")
    core = dp % 2
    groups = lax.axis_size("dp") // 4
    chips = 2 * groups
    quarter = 2 * side + core
    number = side * lax.axis_size("dp") + dp
    place = jnp.reshape(side, (1,)).astype(jnp.int32)
    in_rows, out_rows = in_weight.shape[0], out_weight.shape[0]
    chip_rows = 2 * in_rows

    conv_width, gain_width = conv_table.shape[1], norm_gains.shape[0]
    small_size = 5 * conv_width + gain_width
    small_pad = -(-small_size // 128) * 128
    small_row = jnp.concatenate(
        [conv_table.astype(bf16).reshape(-1), norm_gains.astype(bf16)]
    )
    small_all = gather_small(jnp.pad(small_row, (0, small_pad - small_size))[None])
    devices = small_all.shape[0]
    conv_full = small_all[:, : 5 * conv_width].reshape(devices, 5, conv_width)
    conv_full = conv_full.transpose(1, 0, 2).reshape(5, CH).astype(f32)
    gains_full = small_all[:, 5 * conv_width : small_size].reshape(1, D + DI).astype(f32)
    first_gain = gains_full[:, :D]
    second_gain = lax.dynamic_slice(gains_full, (0, D + quarter * QW), (1, QW))
    conv_own = jnp.concatenate(
        [lax.dynamic_slice(conv_full, (0, quarter * QW), (5, QW)), conv_full[:, DI:]], axis=1
    )
    conv_own = jnp.pad(conv_own, ((0, 3), (0, 0)))
    head_own = lax.dynamic_slice(head_table, (0, quarter * QH), (3, QH))
    head_rows = jnp.concatenate([-jnp.exp(head_own[0:1]), head_own[1:2]], axis=0)
    head_rows = jnp.pad(head_rows, ((0, 6), (0, 128 - QH)))
    skip = jnp.repeat(head_own[2:3], HEAD_DIM, axis=1)

    low = in_weight.astype(bf16)
    wide_own = jnp.concatenate(
        [
            by_quarter(low[:, DI : 2 * DI]),
            jnp.broadcast_to(low[None, :, 2 * DI : DI + CH], (QUARTERS, in_rows, 2 * STATE)),
            by_quarter(low[:, DI + CH :]),
            jnp.zeros((QUARTERS, in_rows, WIDE - QC - QH), bf16),
        ],
        axis=2,
    )
    gate_own = by_quarter(low[:, :DI])
    out_own = out_weight.astype(bf16).reshape(out_rows, 2, QW)

    wide_piece = to_group(wide_own, side, core).reshape(2, chip_rows, WIDE)

    def put_in(base, piece, chip):
        return lax.dynamic_update_slice(base, piece[:, None], (0, chip, 0, 0))

    w_wide = spread(
        wide_piece, groups, put_in, jnp.zeros((2, chips, chip_rows, WIDE), bf16)
    ).reshape(D, WIDE)

    tok_a = jnp.concatenate([tokens, other_side(tokens)], axis=0)
    tok_b = other_core(tok_a)

    gate_piece = to_group(gate_own, side, core).reshape(4 * in_rows, QW)
    out_piece = in_order(core, pick(out_own, core, 1), other_core(pick(out_own, 1 - core, 1)))
    both_piece = jnp.stack([gate_piece, out_piece])

    def put_both(base, piece, chip):
        gate_base, out_base = base
        gate_part = piece[0].reshape(2, 1, chip_rows, QW)
        return (
            lax.dynamic_update_slice(gate_base, gate_part, (0, chip, 0, 0)),
            lax.dynamic_update_slice(out_base, piece[1][None], (chip, 0, 0)),
        )

    w_gate, out_half = spread(
        both_piece,
        groups,
        put_both,
        (
            jnp.zeros((2, chips, chip_rows, QW), bf16),
            jnp.zeros((chips, 2 * out_rows, QW), bf16),
        ),
    )
    w_gate = w_gate.reshape(D, QW)
    out_half = out_half.reshape(2, QW, QW)
    w_out = in_order(
        core, pick(out_half, core, 0), other_core(pick(out_half, 1 - core, 0)), axis=1
    )
    cot_a = jnp.concatenate([cotangent, other_side(cotangent)], axis=0)
    cot_b = other_core(cot_a)

    forward = [
        run_forward(place, tok, first_gain, w_wide, conv_own, head_rows, skip)
        for tok in (tok_a, tok_b)
    ]
    gated = [
        run_gate(place, fwd[0], w_gate, cot, w_out, second_gain, fwd[2])
        for fwd, cot in zip(forward, (cot_a, cot_b))
    ]
    stats = jnp.stack([gated[0][2], gated[1][2]])
    stats = stats + other_side(stats)
    swapped = other_core(stats)
    finished = [
        run_finish(
            place, stats[n] + swapped[1 - n], gated[n][0], gated[n][1], forward[n][2], w_out,
            second_gain,
        )
        for n in range(2)
    ]

    (shaped_a, layer_a, scan_grad_a, gate_grad_a, gain_a) = finished[0]
    (shaped_b, layer_b, scan_grad_b, gate_grad_b, gain_b) = finished[1]
    out_grad = run_outer(shaped_a, shaped_b, cot_a, cot_b)
    gate_grad = run_outer(forward[0][0], forward[1][0], gate_grad_a, gate_grad_b)
    out_cols = out_grad.reshape(QW, 2, QW)
    out_grad = in_order(core, pick(out_cols, core, 1), other_core(pick(out_cols, 1 - core, 1)))
    out_grad = out_grad.reshape(chips, 2 * out_rows, QW)
    gate_grad = gate_grad.reshape(2, chips, chip_rows, QW)

    def both_block(chip):
        return jnp.stack(
            [pick(gate_grad, chip, 1).reshape(4 * in_rows, QW), pick(out_grad, chip, 0)]
        )

    both_sum = collect(both_block, groups)

    layer = layer_a.astype(f32) + other_core(layer_b).astype(f32)
    layer_out = (
        tokens.astype(f32) + layer[:HALF] + other_side(layer[HALF:].astype(bf16)).astype(f32)
    )

    backward = [
        run_backward(fwd[1], fwd[2], grad, fwd[3], conv_own, head_rows, skip)
        for fwd, grad in zip(forward, (scan_grad_a, scan_grad_b))
    ]
    wide_a, wide_b = backward[0][0], backward[1][0]
    wide_grad = run_outer(forward[0][0], forward[1][0], wide_a, wide_b)
    wide_grad = wide_grad.reshape(2, chips, chip_rows, WIDE)
    wide_sum = collect(lambda chip: pick(wide_grad, chip, 1), groups)
    input_a, first_a = run_input_grad(place, gate_grad_a, wide_a, w_gate, w_wide, tok_a)
    input_b, first_b = run_input_grad(place, gate_grad_b, wide_b, w_gate, w_wide, tok_b)

    grad_normed = input_a.astype(f32) + other_core(input_b).astype(f32)
    grad_normed = grad_normed[:HALF] + other_side(grad_normed[HALF:].astype(bf16)).astype(f32)
    wide = tokens.astype(f32)
    inv_one = lax.rsqrt(jnp.mean(wide * wide, axis=1, keepdims=True) + norm_epsilon)
    unit_one = wide * inv_one
    lifted = grad_normed * first_gain
    tokens_grad = cotangent.astype(f32) + inv_one * (
        lifted - unit_one * jnp.mean(lifted * unit_one, axis=1, keepdims=True)
    )

    conv_grad = backward[0][1] + backward[1][1]
    head_grad = backward[0][2] + backward[1][2]
    skip_grad = (backward[0][3] + backward[1][3])[0].reshape(QH, HEAD_DIM).sum(axis=1)
    gain_grad = (gain_a + gain_b)[0:1]
    conv_all = jnp.concatenate(
        [
            lax.dynamic_update_slice(
                jnp.zeros((5, DI), f32), conv_grad[:5, :QW], (0, quarter * QW)
            ),
            conv_grad[:5, QW:],
        ],
        axis=1,
    )
    gains_all = jnp.concatenate(
        [
            (first_a + first_b)[0:1],
            lax.dynamic_update_slice(jnp.zeros((1, DI), f32), gain_grad, (0, quarter * QW)),
        ],
        axis=1,
    )
    heads_all = lax.dynamic_update_slice(
        jnp.zeros((3, HEADS), f32),
        jnp.concatenate([head_grad[0:2, :QH], skip_grad[None]], axis=0),
        (0, quarter * QH),
    )
    packed = jnp.concatenate(
        [
            conv_all.reshape(-1, 128),
            gains_all.reshape(-1, 128),
            jnp.pad(heads_all.reshape(-1), (0, 256 - 3 * HEADS)).reshape(2, 128),
        ],
        axis=0,
    )
    packed = sum_small(packed)
    conv_rows, gain_rows = 5 * CH // 128, (D + DI) // 128
    conv_sum = lax.dynamic_slice(
        packed[:conv_rows].reshape(5, CH), (0, number * conv_width), (5, conv_width)
    )
    gains_sum = lax.dynamic_slice(
        packed[conv_rows : conv_rows + gain_rows].reshape(-1), (number * gain_width,), (gain_width,)
    )
    head_sum = packed[conv_rows + gain_rows :].reshape(-1)[: 3 * HEADS].reshape(3, HEADS)

    gate_sum = from_group(both_sum[0].reshape(2, 2, in_rows, QW), side, core)
    wide_sum = from_group(wide_sum.reshape(2, 2, in_rows, WIDE), side, core).astype(f32)

    def joined(quarters):
        return quarters.transpose(1, 0, 2).reshape(in_rows, -1)

    in_grad = jnp.concatenate(
        [
            joined(gate_sum).astype(f32),
            joined(wide_sum[:, :, :QW]),
            jnp.sum(wide_sum[:, :, QW:QC], axis=0),
            joined(wide_sum[:, :, QC : QC + QH]),
        ],
        axis=1,
    )
    out_rows_sum = both_sum[1].reshape(2, out_rows, QW)
    out_grad = in_order(
        core, pick(out_rows_sum, core, 0), other_core(pick(out_rows_sum, 1 - core, 0)), axis=1
    ).astype(f32)

    in_new = adamw_step(in_weight, in_moment, in_square, in_grad, rate_matrix, weight_decay)
    out_new = adamw_step(out_weight, out_moment, out_square, out_grad, rate_matrix, weight_decay)
    conv_new = adamw_step(conv_table, conv_moment, conv_square, conv_sum, rate_vector, 0.0)
    gains_new = adamw_step(norm_gains, gain_moment, gain_square, gains_sum, rate_vector, 0.0)
    head_new = adamw_step(head_table, head_moment, head_square, head_sum, rate_heads, 0.0)
    return (layer_out, tokens_grad, *in_new, *out_new, *conv_new, *gains_new, *head_new)


def solution(mesh):
    tokens = P(("dp", "seq"), None)
    rows = P(("seq", "dp"), None)
    columns = P(None, ("seq", "dp"))
    line = P(("seq", "dp"))
    return jax.shard_map(
        on_device,
        mesh=mesh,
        in_specs=(tokens,) * 2 + (rows,) * 6 + (columns,) * 3 + (line,) * 3 + (P(),) * 3,
        out_specs=(tokens,) * 2 + (rows,) * 6 + (columns,) * 3 + (line,) * 3 + (P(),) * 3,
        check_vma=False,
    )
```

```python
import functools

import jax
import jax.numpy as jnp
from jax import lax
from jax.experimental import pallas as pl
from jax.experimental.pallas import tpu as pltpu
from jax.sharding import PartitionSpec as P

D = 1536
HEADS = 48
HEAD_DIM = 64
STATE = 128
CONV = 4
STEP = 10
DI = 3072
CH = 3328

QUARTERS = 4
QH = HEADS // QUARTERS
QW = DI // QUARTERS
QC = QW + 2 * STATE
WIDE = QC + 128
GH = QH // 2
GC = GH * HEAD_DIM
LEN = 256
ROWS = 1024
HALF = ROWS // 2
BLOCKS = ROWS // LEN

norm_epsilon = 1e-05
adam_epsilon = 1e-08
beta_first = 0.9
beta_second = 0.999
rate_matrix = 0.05
rate_vector = 0.5
rate_heads = 2.0
weight_decay = 0.1
LOG2E = 1.4426950408889634

f32 = jnp.float32
bf16 = jnp.bfloat16
NN = (((1,), (0,)), ((), ()))
NT = (((1,), (1,)), ((), ()))
TN = (((0,), (0,)), ((), ()))
MIB = 1024 * 1024


def mm(a, b, dims=NN):
    return lax.dot_general(a, b, dims, preferred_element_type=f32)


def mm_exact(a, b, dims=NN):
    return lax.dot_general(
        a, b, dims, precision=lax.Precision.HIGHEST, preferred_element_type=f32
    )


def spread_heads(columns, first_head, count):
    rows = columns.shape[0]
    low = lax.broadcasted_iota(jnp.int32, (rows, 128), 1) < HEAD_DIM
    parts = []
    for h in range(first_head, first_head + count, 2):
        first = jnp.broadcast_to(columns[:, h : h + 1], (rows, 128))
        second = jnp.broadcast_to(columns[:, h + 1 : h + 2], (rows, 128))
        parts.append(jnp.where(low, first, second))
    return jnp.concatenate(parts, axis=1)


def softplus(v):
    return jnp.maximum(v, 0.0) + jnp.log1p(jnp.exp(-jnp.abs(v)))


def triangle(lower):
    rows = lax.broadcasted_iota(jnp.int32, (LEN, LEN), 0)
    cols = lax.broadcasted_iota(jnp.int32, (LEN, LEN), 1)
    return rows >= cols if lower else rows <= cols


def halves(pair):
    low = lax.broadcasted_iota(jnp.int32, pair.shape, 1) < HEAD_DIM
    zero = jnp.zeros_like(pair)
    return jnp.where(low, pair, zero), jnp.where(low, zero, pair)


def parts_of(v):
    high = v.astype(bf16)
    return high, (v - high.astype(f32)).astype(bf16)


def affinity_of(first, second):
    both = jnp.concatenate(first, axis=1)
    high = jnp.concatenate([second[0], second[0]], axis=1)
    return mm(both, high, NT) + mm(first[0], second[1], NT)


def twice(pair):
    low = lax.broadcasted_iota(jnp.int32, pair.shape, 1) < HEAD_DIM
    turned = pltpu.roll(pair, HEAD_DIM, 1)
    return jnp.where(low, pair, turned).astype(bf16), jnp.where(low, turned, pair).astype(bf16)


def beside_rest(pair, rest):
    low = lax.broadcasted_iota(jnp.int32, pair.shape, 1) < HEAD_DIM
    turned = pltpu.roll(rest, HEAD_DIM, 1).astype(bf16)
    return jnp.where(low, pair, turned), jnp.where(low, turned, pair)


def filter_rows(ext, conv_ref):
    width = ext.shape[1]
    total = conv_ref[CONV : CONV + 1, :width]
    for k in range(CONV):
        total = total + conv_ref[k : k + 1, :width] * ext[5 + k : 5 + k + LEN, :]
    return total


def forward_kernel(
    half, place, near, far, gain, w, conv, head, skip, tail_in, state_in, *rest
):
    normed_out, turned_out, proj_out, scanned_out, mem_out = rest[-9:-4]
    tail_out, state_out, ext, mem = rest[-4:]
    j = pl.program_id(0)

    @pl.when(j == 0)
    def _():
        ext[0:8, :] = tail_in[...]
        mem[...] = state_in[...]

    wide = jnp.where(place[0] == half, near[...], far[...]).astype(f32)
    inv_one = lax.rsqrt(jnp.mean(wide * wide, axis=1, keepdims=True) + norm_epsilon)
    normed = (wide * inv_one * gain[...]).astype(bf16)
    normed_out[...] = normed
    turned_out[...] = normed.T
    proj = mm(normed, w[...])
    proj_out[...] = proj
    ext[8 : 8 + LEN, :] = proj[:, :QC]
    filtered = filter_rows(ext, conv)
    ext[0:8, :] = ext[LEN : LEN + 8, :]
    active = filtered * jax.nn.sigmoid(filtered)
    payload = active[:, :QW]
    writers = parts_of(active[:, QW : QW + STATE])
    readers = parts_of(active[:, QW + STATE :])
    writer = writers[0]

    steps = softplus(pltpu.roll(proj[:, QC:], place[2], 1) + head[1:2, :])
    rates = head[0:1, :] * steps
    causal = triangle(True)
    summed = mm_exact(causal.astype(f32), rates) * LOG2E
    across = summed.T
    affinity = jnp.where(causal, affinity_of(readers, writers), 0.0)

    dosed = payload * spread_heads(steps, 0, QH)
    dosed_low = dosed.astype(bf16)
    state = mem[...]
    mem_out[0] = state
    grown = jnp.exp2(spread_heads(summed, 0, QH))
    state_low, state_rest = parts_of(state)
    carried = mm(jnp.concatenate(readers, axis=1), jnp.concatenate([state_low] * 2, axis=0))
    carried = (carried + mm(readers[0], state_rest)) * grown
    within = []
    for pair in range(QH // 2):
        weights = []
        for h in (2 * pair, 2 * pair + 1):
            gap = jnp.minimum(summed[:, h : h + 1] - across[h : h + 1, :], 0.0)
            weights.append((jnp.exp2(gap) * affinity).astype(bf16))
        first, second = halves(dosed_low[:, 128 * pair : 128 * pair + 128])
        within.append(
            mm(jnp.concatenate(weights, axis=1), jnp.concatenate([first, second], axis=0))
        )
    scanned_out[...] = jnp.concatenate(within, axis=1) + carried + payload * skip[...]

    last = summed[LEN - 1 : LEN, :]
    remain = jnp.exp2(spread_heads(last - summed, 0, QH))
    added = mm(writer, (dosed * remain).astype(bf16), TN)
    mem[...] = state * jnp.exp2(spread_heads(last, 0, QH)) + added
    tail_out[...] = ext[0:8, :]
    state_out[...] = mem[...]


def by_core(core, own, other):
    first = core == 0
    return jnp.where(first, own, other), jnp.where(first, other, own)


def at_hand(side, near_a, far_a, near_b, far_b):
    j = pl.program_id(0)
    near = (j % BLOCKS) // (BLOCKS // 2) == side
    first = jnp.where(near, near_a[...], far_a[...])
    return jnp.where(j < BLOCKS, first, jnp.where(near, near_b[...], far_b[...]))


def gate_kernel(
    place, normed, w_gate, cot_na, cot_fa, cot_nb, cot_fb, w_own, w_other, gain, scanned,
    gate_out, shaped_grad_out, stats_out,
):
    gate = mm(normed[...], w_gate[...])
    cot = at_hand(place[0], cot_na, cot_fa, cot_nb, cot_fb)
    left, right = by_core(place[1], w_own[...], w_other[...])
    grad_shaped = mm(cot[:, :QW], left, NT) + mm(cot[:, QW:], right, NT)
    gate_out[...] = gate
    shaped_grad_out[...] = grad_shaped
    gated = scanned[...] * (gate * jax.nn.sigmoid(gate))
    squares = jnp.sum(gated * gated, axis=1, keepdims=True)
    inner = jnp.sum(grad_shaped * gain[...] * gated, axis=1, keepdims=True)
    lane = lax.broadcasted_iota(jnp.int32, (LEN, 128), 1)
    both = jnp.where(lane == 0, squares, jnp.where(lane == 1, inner, 0.0))
    stats_out[...] = both.T[0:8, :]


def finish_kernel(
    place, stats, gate_in, grad_shaped_in, scanned_in, w_own, w_other, gain,
    turned_out, layer_a_out, layer_b_out, scan_grad_out, gate_grad_out, gain_grad,
):
    j = pl.program_id(0)
    table = jnp.concatenate([stats[...], jnp.zeros((120, LEN), f32)], axis=0).T
    inv_two = lax.rsqrt(table[:, 0:1] / DI + norm_epsilon)
    mean = inv_two * table[:, 1:2] / DI
    gate = gate_in[...]
    scanned = scanned_in[...]
    grad_shaped = grad_shaped_in[...]
    sig = jax.nn.sigmoid(gate)
    lift = gate * sig
    unit = scanned * lift * inv_two
    shaped = (unit * gain[...]).astype(bf16)
    turned_out[...] = shaped.T
    left, right = by_core(place[1], w_own[...], w_other[...])
    layer = jnp.concatenate([mm(shaped, left), mm(shaped, right)], axis=1).astype(bf16)

    @pl.when(j < BLOCKS)
    def _():
        layer_a_out[...] = layer

    @pl.when(j >= BLOCKS)
    def _():
        layer_b_out[...] = layer

    grad_gated = inv_two * (grad_shaped * gain[...] - unit * mean)
    scan_grad_out[...] = grad_gated * lift
    gate_grad_out[...] = (grad_gated * scanned * sig * (1.0 + gate * (1.0 - sig))).astype(bf16)

    @pl.when(j == 0)
    def _():
        gain_grad[...] = jnp.zeros_like(gain_grad)

    gain_grad[0:1, :] += jnp.sum(grad_shaped * unit, axis=0, keepdims=True)


def backward_kernel(group, *refs):
    last_group = group == 1
    place, pay_in, rest_in, pay_before, rest_before, scanned_in, grad_in, mem_in = refs[:8]
    conv_pay, conv_rest, head, skip = refs[8:12]
    ext, later, grad_mem = refs[-3:]
    if last_group:
        carry_in = refs[12]
        out, conv_grad, conv_grad_rest, head_grad, skip_grad = refs[-8:-3]
    else:
        out, carry_out, conv_grad, head_grad, skip_grad = refs[-8:-3]
    i = pl.program_id(0)
    j = BLOCKS - 1 - i
    width = GC + 2 * STATE if last_group else GC
    first_head = group * GH

    @pl.when(i == 0)
    def _():
        later[LEN : LEN + 8, :] = jnp.zeros((8, GC + 2 * STATE), f32)
        grad_mem[...] = jnp.zeros_like(grad_mem)
        conv_grad[...] = jnp.zeros_like(conv_grad)
        head_grad[...] = jnp.zeros_like(head_grad)
        skip_grad[...] = jnp.zeros_like(skip_grad)
        if last_group:
            conv_grad_rest[...] = jnp.zeros_like(conv_grad_rest)

    @pl.when(i > 0)
    def _():
        later[LEN : LEN + 8, :] = later[0:8, :]

    conv_in = jnp.concatenate([pay_in[...], rest_in[:, : 2 * STATE]], axis=1)
    conv = jnp.concatenate([conv_pay[...], conv_rest[:, : 2 * STATE]], axis=1)
    before = jnp.concatenate([pay_before[...], rest_before[:, : 2 * STATE]], axis=1)
    ext[0:8, :] = jnp.where(j > 0, before, 0.0)
    ext[8 : 8 + LEN, :] = conv_in
    filtered = filter_rows(ext, conv)
    sig = jax.nn.sigmoid(filtered)
    active = filtered * sig
    slope = (sig * (1.0 + filtered * (1.0 - sig)))[:, :width]
    payload = active[:, :GC]
    writers = parts_of(active[:, GC : GC + STATE])
    readers = parts_of(active[:, GC + STATE :])
    writer, reader = writers[0], readers[0]

    raw = pltpu.roll(rest_in[:, 2 * STATE :], place[2], 1) + head[1:2, :]
    steps = softplus(raw)
    rates = head[0:1, :] * steps
    summed = mm_exact(triangle(True).astype(f32), rates) * LOG2E
    across = summed.T
    upper = triangle(False)
    affinity = jnp.where(upper, affinity_of(writers, readers), 0.0)

    grad = grad_in[...]
    grad_low = grad.astype(bf16)
    grad_rest = grad - grad_low.astype(f32)
    dose = spread_heads(steps, first_head, GH)
    dosed = payload * dose
    dosed_low = dosed.astype(bf16)
    state = mem_in[0]
    state_grad = grad_mem[...]
    state_grad_low = state_grad.astype(bf16)
    last = summed[LEN - 1 : LEN, :]
    remain = jnp.exp2(spread_heads(last - summed, first_head, GH))
    from_state = mm(writer, state_grad_low) * remain

    mixed = jnp.zeros((LEN, LEN), f32)
    within = []
    for pair in range(GH // 2):
        lanes = slice(128 * pair, 128 * pair + 128)
        grads = halves(grad_low[:, lanes])
        doses = twice(dosed[:, lanes])
        parts = beside_rest(grad_low[:, lanes], grad_rest[:, lanes])
        weights = []
        for n in range(2):
            h = first_head + 2 * pair + n
            gap = jnp.minimum(across[h : h + 1, :] - summed[:, h : h + 1], 0.0)
            decay = jnp.exp2(gap)
            weights.append((decay * affinity).astype(bf16))
            mixed = mixed + decay * mm(doses[n], parts[n], NT)
        within.append(mm(jnp.concatenate(weights, axis=1), jnp.concatenate(grads, axis=0)))
    unit = jnp.concatenate(within, axis=1) + from_state

    payload_grad = dose * unit + skip[...] * grad
    core = scanned_in[...] - payload * skip[...]
    dosed_wide = dosed_low.astype(f32)
    balance = grad_low.astype(f32) * core - dosed_wide * unit
    high_part = balance.astype(bf16)
    low_part = (balance - high_part.astype(f32)).astype(bf16)
    heads_of = (
        lax.broadcasted_iota(jnp.int32, (GC, 128), 0) // HEAD_DIM + first_head
        == lax.broadcasted_iota(jnp.int32, (GC, 128), 1)
    ).astype(f32)
    heads_low = heads_of.astype(bf16)
    balance_sum = mm(high_part, heads_low) + mm(low_part, heads_low)
    direct = mm((payload * unit).astype(bf16), heads_low)
    decay_last = jnp.exp2(spread_heads(last, first_head, GH))
    at_end = jnp.sum(dosed_wide * from_state, axis=0, keepdims=True) + decay_last * jnp.sum(
        state_grad * state, axis=0, keepdims=True
    )
    end_sum = mm_exact(jnp.broadcast_to(at_end, (8, GC)), heads_of)[0:1, :]
    rate_grad = mm_exact(upper.astype(f32), balance_sum) + end_sum
    step_grad = direct + head[0:1, :] * rate_grad
    raw_grad = step_grad * jax.nn.sigmoid(raw)
    head_grad[0:1, :] += jnp.sum(rate_grad * rates, axis=0, keepdims=True)
    head_grad[1:2, :] += jnp.sum(raw_grad, axis=0, keepdims=True)
    skip_grad[0:1, :] += jnp.sum(grad * payload, axis=0, keepdims=True)

    grown_wide = jnp.exp2(spread_heads(summed, first_head, GH)) * grad
    grown_grad = grown_wide.astype(bf16)
    grown_rest = (grown_wide - grown_grad.astype(f32)).astype(bf16)
    kept = (remain * dosed).astype(bf16)
    mixed_low = jnp.where(upper, mixed, 0.0).astype(bf16)
    writer_grad = mm(mixed_low, reader) + mm(kept, state_grad_low, NT)
    state_low = state.astype(bf16)
    reader_grad = (
        mm(mixed_low, writer, TN) + mm(grown_grad, state_low, NT) + mm(grown_rest, state_low, NT)
    )
    grad_mem[...] = decay_last * state_grad + mm(reader, grown_grad, TN)

    if last_group:
        writer_grad = writer_grad + carry_in[:, :STATE]
        reader_grad = reader_grad + carry_in[:, STATE : 2 * STATE]
        raw_grad = raw_grad + carry_in[:, 2 * STATE :]
        filtered_grad = jnp.concatenate([payload_grad, writer_grad, reader_grad], axis=1) * slope
    else:
        carry_out[...] = jnp.concatenate([writer_grad, reader_grad, raw_grad], axis=1)
        filtered_grad = payload_grad * slope
    later[0:LEN, :width] = filtered_grad
    back = None
    sums = []
    for k in range(CONV):
        ahead = later[CONV - 1 - k : CONV - 1 - k + LEN, :width]
        sums.append(jnp.sum(ahead * conv_in[:, :width], axis=0, keepdims=True))
        term = conv[k : k + 1, :width] * ahead
        back = term if back is None else back + term
    sums.append(jnp.sum(filtered_grad, axis=0, keepdims=True))
    sums = jnp.concatenate(sums + [jnp.zeros((7 - CONV, width), f32)], axis=0)
    conv_grad[...] += sums[:, :GC]
    out[:, :GC] = back[:, :GC].astype(bf16)
    if last_group:
        conv_grad_rest[...] += sums[:, GC:]
        out[:, GC : GC + 2 * STATE] = back[:, GC:].astype(bf16)
        out[:, GC + 2 * STATE :] = pltpu.roll(raw_grad, place[3], 1).astype(bf16)


def outer_kernel(left, *rest):
    out = rest[-1]
    total = None
    for n, right in enumerate(rest[:-1]):
        part = mm(left[:, n * HALF : (n + 1) * HALF], right[...])
        total = part if total is None else total + part
    out[...] = total.astype(bf16)


def pieces_kernel(chip_rows, blocks, place, left, right, *rest):
    out, dots = rest[-2:]
    weights, others = rest[:blocks], rest[blocks:-2]
    tile = left.shape[0]
    i = pl.program_id(0)
    per = tile // chip_rows
    steps = out.shape[0] // per
    result = mm(left[...], right[...])
    sums = jnp.zeros((tile, 128), f32)
    for n, weight in enumerate(weights):
        product = result[:, n * GC : (n + 1) * GC] * weight[...].astype(f32)
        sums = sums + (product[:, :128] + product[:, 128:256] + product[:, 256:])
    dots[...] = jnp.broadcast_to(jnp.sum(sums.T, axis=0, keepdims=True), (8, tile))
    for n in range(per):
        part = result[n * chip_rows : (n + 1) * chip_rows].astype(bf16)
        if others:
            out[(i % steps) * per + n, 0, i // steps] = part
        else:
            out[(i % steps) * per + n, i // steps] = part
    if others:
        half = out.shape[0] // 2

        @pl.when(i == 0)
        def _():
            own, other = others
            core = place[1]
            out[pl.ds(core * half, half), 1] = own[...]
            out[pl.ds((1 - core) * half, half), 1] = other[...]


def input_grad_kernel(place, gate_grad, pay_grad, rest_grad, w_gate, w_wide, out):
    grad = (
        mm(gate_grad[...], w_gate[...], NT)
        + mm(pay_grad[...], w_wide[:, :GC], NT)
        + mm(rest_grad[...], w_wide[:, GC:], NT)
    )
    out[...] = grad.astype(bf16)


def own_first(j, place):
    per = BLOCKS // 2
    half = j // per
    side = place[0]
    return (half + side - 2 * half * side) * per + j % per


def rows_of(width, first=0):
    return pl.BlockSpec((LEN, width), lambda j, *_: (j + first, 0))


def moved_columns(height):
    return pl.BlockSpec(
        (height, LEN),
        lambda j, place: (0, own_first(j % BLOCKS, place) + (j // BLOCKS) * BLOCKS),
    )


def first_rows(width):
    return pl.BlockSpec(
        (LEN, width), lambda j, place: (own_first(jnp.minimum(j, BLOCKS - 1), place), 0)
    )


def second_rows(width):
    return pl.BlockSpec(
        (LEN, width), lambda j, place: (own_first(jnp.maximum(j - BLOCKS, 0), place), 0)
    )


def whole(*shape):
    return pl.BlockSpec(shape, lambda j, *_: (0,) * len(shape))


def params():
    return pltpu.CompilerParams(
        vmem_limit_bytes=60 * MIB, dimension_semantics=("arbitrary",)
    )


def shape(dims, dtype):
    return jax.ShapeDtypeStruct(dims, dtype)


def cost(microseconds):
    return pl.CostEstimate(
        flops=int(microseconds * 1e9),
        bytes_accessed=int(microseconds * 3.5e6),
        transcendentals=0,
    )


def run_forward(place, near, far, gain, w, conv, head, skip, carried, buffers, part):
    per = BLOCKS // 2
    first = part * per
    if buffers is None:
        buffers = ()
    anywhere = pl.BlockSpec(memory_space=pl.ANY)
    return pl.pallas_call(
        functools.partial(forward_kernel, part % 2),
        grid_spec=pltpu.PrefetchScalarGridSpec(
            num_scalar_prefetch=1,
            grid=(per,),
            in_specs=[
                rows_of(D), rows_of(D), whole(1, D), whole(D, WIDE), whole(8, WIDE), whole(8, 128), whole(1, QW),
                whole(8, QC), whole(STATE, QW),
            ] + [anywhere] * len(buffers),
            out_specs=[
                rows_of(D, first), pl.BlockSpec((D, LEN), lambda j, *_: (0, j + first)),
                rows_of(WIDE, first), rows_of(QW, first),
                pl.BlockSpec((1, STATE, QW), lambda j, *_: (j + first, 0, 0)),
                whole(8, QC), whole(STATE, QW),
            ],
            scratch_shapes=[pltpu.VMEM((LEN + 8, QC), f32), pltpu.VMEM((STATE, QW), f32)],
        ),
        out_shape=[
            shape((2 * ROWS, D), bf16), shape((D, 2 * ROWS), bf16),
            shape((2 * ROWS, WIDE), f32), shape((2 * ROWS, QW), f32),
            shape((2 * BLOCKS, STATE, QW), f32), shape((8, QC), f32), shape((STATE, QW), f32),
        ],
        input_output_aliases={10 + n: n for n in range(len(buffers))},
        compiler_params=params(),
        cost_estimate=cost(13),
        name="forward_scan",
    )(place, near, far, gain, w, conv, head, skip, *carried, *buffers)


def assemble_kernel(count, place, *refs):
    pieces, (gate, own, send) = refs[:count], refs[count:]
    half = count // 2
    for n, piece in enumerate(pieces):
        chip = place[4 + n]
        gate[0, chip] = piece[0, 0]
        gate[1, chip] = piece[0, 1]
        mine = chip // half == place[1]

        @pl.when(mine)
        def _():
            own[chip % half] = piece[1]

        @pl.when(jnp.logical_not(mine))
        def _():
            send[chip % half] = piece[1]


def run_assemble(place, pieces):
    count = len(pieces)
    _, _, rows, width = pieces[0].shape
    outs = [(2, count, rows, width)] + [(count // 2, 2, rows, width)] * 2
    return pl.pallas_call(
        functools.partial(assemble_kernel, count),
        grid_spec=pltpu.PrefetchScalarGridSpec(
            num_scalar_prefetch=1,
            grid=(1,),
            in_specs=[whole(2, 2, rows, width)] * count,
            out_specs=[whole(*dims) for dims in outs],
        ),
        out_shape=[shape(dims, bf16) for dims in outs],
        compiler_params=params(),
        cost_estimate=cost(3),
        name="assemble",
    )(place, *pieces)


def run_gate(place, normed, w_gate, cots, w_out, gain, scanned):
    per = BLOCKS // 2

    def half(sequence, far):
        def index(j, place):
            first = sequence * BLOCKS + (1 - place[0] if far else place[0]) * per
            return (jnp.clip(j - first, 0, per - 1), 0)

        return pl.BlockSpec((LEN, D), index)

    return pl.pallas_call(
        gate_kernel,
        grid_spec=pltpu.PrefetchScalarGridSpec(
            num_scalar_prefetch=1,
            grid=(2 * BLOCKS,),
            in_specs=[
                rows_of(D), whole(D, QW), half(0, False), half(0, True), half(1, False),
                half(1, True), whole(QW, QW), whole(QW, QW), whole(1, QW), rows_of(QW),
            ],
            out_specs=[
                rows_of(QW), rows_of(QW), pl.BlockSpec((8, LEN), lambda j, *_: (0, j)),
            ],
        ),
        out_shape=[
            shape((2 * ROWS, QW), f32), shape((2 * ROWS, QW), f32), shape((8, 2 * ROWS), f32),
        ],
        compiler_params=params(),
        cost_estimate=cost(2),
        name="gate_and_stats",
    )(place, normed, w_gate, *cots, *w_out, gain, scanned)


def run_finish(place, stats, gate, grad_shaped, scanned, w_out, gain):
    return pl.pallas_call(
        finish_kernel,
        grid_spec=pltpu.PrefetchScalarGridSpec(
            num_scalar_prefetch=1,
            grid=(2 * BLOCKS,),
            in_specs=[
                pl.BlockSpec((8, LEN), lambda j, *_: (0, j)), rows_of(QW), rows_of(QW),
                rows_of(QW), whole(QW, QW), whole(QW, QW), whole(1, QW),
            ],
            out_specs=[
                moved_columns(QW), first_rows(D), second_rows(D), rows_of(QW), rows_of(QW),
                whole(8, QW),
            ],
        ),
        out_shape=[
            shape((QW, 2 * ROWS), bf16), shape((ROWS, D), bf16), shape((ROWS, D), bf16),
            shape((2 * ROWS, QW), f32), shape((2 * ROWS, QW), bf16), shape((8, QW), f32),
        ],
        compiler_params=params(),
        cost_estimate=cost(2),
        name="finish",
    )(place, stats, gate, grad_shaped, scanned, *w_out, gain)


def run_backward(place, group, sequence, proj, scanned, grad, mem, conv, head, skip, carry, buffers):
    top = (sequence + 1) * BLOCKS - 1
    tiles = LEN // 8

    def back(width, column):
        return pl.BlockSpec((LEN, width), lambda i, *_: (top - i, column))

    def before(column):
        return pl.BlockSpec((8, GC), lambda i, *_: (jnp.maximum((top - i) * tiles - 1, 0), column))

    def column_of(rows, column):
        return pl.BlockSpec((rows, GC), lambda i, *_: (0, column))

    anywhere = pl.BlockSpec(memory_space=pl.ANY)
    in_specs = [
        back(GC, group), back(GC, 2), before(group), before(2), back(GC, group), back(GC, group),
        pl.BlockSpec((1, STATE, GC), lambda i, *_: (top - i, 0, group)),
        column_of(8, group), column_of(8, 2), whole(8, 128), column_of(1, group),
    ]
    args = [place, proj, proj, proj, proj, scanned, grad, mem, conv, conv, head, skip]
    sums_spec = [whole(8, GC)]
    sums_shape = [shape((8, GC), f32)]
    if group:
        in_specs.append(back(GC, 0))
        args.append(carry)
        out_specs = [back(2 * GC, 0)]
        out_shape = [shape((2 * ROWS, 2 * GC), bf16)]
        sums_spec = sums_spec + [whole(8, 2 * STATE)]
        sums_shape = sums_shape + [shape((8, 2 * STATE), f32)]
    else:
        out_specs = [back(GC, 0), back(GC, 0)]
        out_shape = [shape((2 * ROWS, GC), bf16), shape((2 * ROWS, GC), f32)]
    aliases = {len(args) + n: n for n in range(len(buffers))}
    return pl.pallas_call(
        functools.partial(backward_kernel, group),
        grid_spec=pltpu.PrefetchScalarGridSpec(
            num_scalar_prefetch=1,
            grid=(BLOCKS,),
            in_specs=in_specs + [anywhere] * len(buffers),
            out_specs=out_specs + sums_spec + [whole(8, 128), whole(8, GC)],
            scratch_shapes=[
                pltpu.VMEM((LEN + 8, GC + 2 * STATE), f32),
                pltpu.VMEM((LEN + 8, GC + 2 * STATE), f32),
                pltpu.VMEM((STATE, GC), f32),
            ],
        ),
        out_shape=out_shape + sums_shape + [shape((8, 128), f32), shape((8, GC), f32)],
        input_output_aliases=aliases,
        compiler_params=params(),
        cost_estimate=cost(2),
        name="backward_scan",
    )(*args, *buffers)


def run_outer(left, rights):
    tall, width = left.shape[0], rights[0].shape[1]
    tile = 384
    return pl.pallas_call(
        outer_kernel,
        grid=(tall // tile,),
        in_specs=[pl.BlockSpec((tile, 2 * ROWS), lambda i: (i, 0))]
        + [whole(HALF, width) for _ in rights],
        out_specs=pl.BlockSpec((tile, width), lambda i: (i, 0)),
        out_shape=shape((tall, width), bf16),
        compiler_params=params(),
        cost_estimate=cost(1),
        name="weight_grad",
    )(left, *rights)


def run_pieces(place, left, right, chips, weights, columns, others=()):
    tall, width = left.shape[0], right.shape[1]
    tile = 384
    chip_rows = tall // (2 * chips)
    dims = (chips,) + (2,) * (2 if others else 1) + (chip_rows, width)

    def block(column):
        return pl.BlockSpec((tile, GC), lambda i, *_: (i, column))

    beside_specs = []
    if others:
        part = others[1].shape
        beside_specs = [
            pl.BlockSpec(part, lambda i, place: (0, 0, 0, place[1])),
            whole(*part),
        ]
    return pl.pallas_call(
        functools.partial(pieces_kernel, chip_rows, len(columns)),
        grid_spec=pltpu.PrefetchScalarGridSpec(
            num_scalar_prefetch=1,
            grid=(tall // tile,),
            in_specs=[
                pl.BlockSpec((tile, 2 * ROWS), lambda i, *_: (i, 0)), whole(*right.shape),
            ] + [block(column) for column in columns] + beside_specs,
            out_specs=[whole(*dims), pl.BlockSpec((8, tile), lambda i, *_: (0, i))],
        ),
        out_shape=[shape(dims, bf16), shape((8, tall), f32)],
        compiler_params=params(),
        cost_estimate=cost(1),
        name="weight_grad",
    )(place, left, right, *([weights] * len(columns)), *others)


def tokens_grad_kernel(tok, cot, gain, near, core, *rest):
    sides, out = rest[:-1], rest[-1]
    i = pl.program_id(0)
    rows = out.shape[0]
    parts = [ref[n : n + rows, :] for ref in sides for n in range(0, ref.shape[0], rows)]
    side = parts[0]
    for n in range(1, len(parts)):
        side = jnp.where(i == n, parts[n], side)
    grad = near[...].astype(f32) + core[...].astype(f32) + side.astype(f32)
    wide = tok[...].astype(f32)
    inv_one = lax.rsqrt(jnp.mean(wide * wide, axis=1, keepdims=True) + norm_epsilon)
    unit = wide * inv_one
    lifted = grad * gain[...]
    mean = jnp.mean(lifted * unit, axis=1, keepdims=True)
    out[...] = cot[...].astype(f32) + inv_one * (lifted - unit * mean)


def run_tokens_grad(tokens, cotangent, gain, near, core, sides):
    rows = min(part.shape[0] for part in sides)
    block = pl.BlockSpec((rows, D), lambda i: (i, 0))
    return pl.pallas_call(
        tokens_grad_kernel,
        grid=(HALF // rows,),
        in_specs=[block, block, whole(1, D), block, block]
        + [whole(*part.shape) for part in sides],
        out_specs=block,
        out_shape=shape((HALF, D), f32),
        compiler_params=params(),
        cost_estimate=cost(4),
        name="tokens_grad",
    )(tokens, cotangent, gain, near, core, *sides)


def run_input_grad(place, sequence, far, gate_grad, pay_grad, rest_grad, w_gate, w_wide):
    per = BLOCKS // 2

    def rows(width):
        def index(j, place):
            half = 1 - place[0] if far else place[0]
            return (sequence * BLOCKS + half * per + j, 0)

        return pl.BlockSpec((LEN, width), index)

    return pl.pallas_call(
        input_grad_kernel,
        grid_spec=pltpu.PrefetchScalarGridSpec(
            num_scalar_prefetch=1,
            grid=(per,),
            in_specs=[rows(QW), rows(GC), rows(2 * GC), whole(D, QW), whole(D, WIDE)],
            out_specs=rows_of(D),
        ),
        out_shape=shape((HALF, D), bf16),
        compiler_params=params(),
        cost_estimate=cost(1),
        name="input_grad",
    )(place, gate_grad, pay_grad, rest_grad, w_gate, w_wide)


def other_side(block):
    return lax.ppermute(block, "seq", [(0, 1), (1, 0)])


def after(block, *others):
    return lax.optimization_barrier((block, *others))[0]


def tie(*blocks):
    return lax.optimization_barrier(blocks)


def flip(block, bit):
    count = lax.axis_size("dp")
    return lax.ppermute(block, "dp", [(d, d ^ bit) for d in range(count)])


def other_core(block):
    return flip(block, 1)


def beside(block):
    return flip(block, 2)


def along(block):
    count = lax.axis_size("dp")
    return lax.ppermute(block, "dp", [(d, (d + 4) % count) for d in range(count)])


def in_order(place, own, received, axis=0):
    return jnp.where(
        place == 0,
        jnp.concatenate([own, received], axis=axis),
        jnp.concatenate([received, own], axis=axis),
    )


def pick(block, place, axis):
    return lax.dynamic_index_in_dim(block, place, axis, False)


class Spread:
    def __init__(self, piece, groups, put, base, hold=()):
        dp = lax.axis_index("dp")
        self.ring, self.beside_place = dp // 4, (dp // 2) % 2
        self.groups, self.put, self.base = groups, put, base
        self.hop, self.current = 0, piece
        self.neighbour = beside(after(piece, *hold) if hold else piece)

    def place(self, hold=()):
        origin = (self.ring + self.groups - self.hop) % self.groups
        current, neighbour = self.current, self.neighbour
        if hold:
            current, neighbour, *_ = tie(current, neighbour, *hold)
        self.base = self.put(self.base, current, 2 * origin + self.beside_place)
        self.base = self.put(self.base, neighbour, 2 * origin + 1 - self.beside_place)

    def step(self, hold=(), place_hold=()):
        moved = along(self.current)
        if hold:
            moved = after(moved, *hold)
        self.place(place_hold)
        self.hop, self.current, self.neighbour = self.hop + 1, moved, beside(moved)
        return moved


class Collect:
    def __init__(self, block_of, groups):
        dp = lax.axis_index("dp")
        self.ring, self.beside_place = dp // 4, (dp // 2) % 2
        self.block_of, self.groups = block_of, groups
        self.hop, self.total = 0, None
        self.received = beside(self.block(1 - self.beside_place))

    def block(self, place):
        target = (self.ring + 2 * self.groups - 1 - self.hop) % self.groups
        return self.block_of(2 * target + place)

    def step(self, *hold):
        received = after(self.received, *hold) if hold else self.received
        part = self.block(self.beside_place).astype(f32) + received.astype(f32)
        if self.hop:
            part = part + self.total.astype(f32)
        part = part.astype(bf16)
        self.hop += 1
        if self.hop < self.groups:
            part, following = tie(part, self.block(1 - self.beside_place))
            self.total = along(part)
            self.received = beside(following)
        return part

    def rest(self):
        while self.hop < self.groups:
            part = self.step()
        return part


def gather_small(row, hold):
    dp = lax.axis_index("dp")
    block = row.reshape((1, 1) + row.shape)
    block = hold(in_order(lax.axis_index("seq"), block, other_side(block), axis=0))
    bit = 1
    while bit < lax.axis_size("dp"):
        block = in_order((dp // bit) % 2, block, flip(block, bit), axis=1)
        bit *= 2
    return block.reshape((-1,) + row.shape)


def sum_small(block, bit):
    while bit < lax.axis_size("dp"):
        block = block + flip(block, bit)
        bit *= 2
    return block


def columns_of(block, half):
    return lax.dynamic_slice(block, (0, half * QW), (block.shape[0], QW))


def adamw_step(weight, moment, square, gradient, step_rate, decay_rate):
    moment_new = beta_first * moment + (1.0 - beta_first) * gradient
    square_new = beta_second * square + (1.0 - beta_second) * gradient * gradient
    first_fix = moment_new / (1.0 - beta_first**STEP)
    second_fix = square_new / (1.0 - beta_second**STEP)
    weight_new = weight - step_rate * (
        first_fix / (jnp.sqrt(second_fix) + adam_epsilon) + decay_rate * weight
    )
    return (weight_new, moment_new, square_new)


def to_side(halves_of, side):
    return in_order(side, halves_of(side)[None], other_side(halves_of(1 - side))[None])


def to_core(pair, quarter_of, core):
    return in_order(
        core, quarter_of(pair, core)[:, None], other_core(quarter_of(pair, 1 - core))[:, None], 1
    )


def from_cores(piece, core):
    return in_order(core, pick(piece, core, 1), other_core(pick(piece, 1 - core, 1)), 2)


def from_sides(cores, side):
    return in_order(side, pick(cores, side, 0), other_side(pick(cores, 1 - side, 0)), 1)


def from_group(piece, side, core):
    return from_sides(from_cores(piece, core), side)


def from_group_shared(piece, side, core):
    mine, got = pick(piece, core, 1), other_core(pick(piece, 1 - core, 1))
    cores = in_order(core, mine[:, :, :GC], got[:, :, :GC], 2)
    shared = (mine[:, :, GC:].astype(f32) + got[:, :, GC:].astype(f32)).astype(bf16)
    both = jnp.concatenate([cores, shared], axis=2)
    mine, got = pick(both, side, 0), other_side(pick(both, 1 - side, 0))
    sides = in_order(side, mine[:, : 2 * GC], got[:, : 2 * GC], 1)
    return sides, mine[:, 2 * GC :].astype(f32) + got[:, 2 * GC :].astype(f32)


def on_device(
    tokens,
    cotangent,
    in_weight,
    in_moment,
    in_square,
    out_weight,
    out_moment,
    out_square,
    conv_table,
    conv_moment,
    conv_square,
    norm_gains,
    gain_moment,
    gain_square,
    head_table,
    head_moment,
    head_square,
):
    side = lax.axis_index("seq")
    dp = lax.axis_index("dp")
    core = dp % 2
    groups = lax.axis_size("dp") // 4
    chips = 2 * groups
    quarter = 2 * side + core
    number = side * lax.axis_size("dp") + dp
    turn = quarter * QH
    place = jnp.stack([side, core, 128 - turn, turn]).astype(jnp.int32)
    in_rows, out_rows = in_weight.shape[0], out_weight.shape[0]
    chip_rows = 2 * in_rows

    low = in_weight.astype(bf16)
    shared_own = jnp.pad(low[:, 2 * DI :], ((0, 0), (0, GC - 2 * STATE - HEADS)))

    def wide_half(side):
        own = lax.dynamic_slice(low, (0, DI + side * 2 * QW), (in_rows, 2 * QW))
        return jnp.concatenate([own, shared_own], axis=1)

    def wide_quarter(pair, core):
        own = lax.dynamic_slice(pair, (0, 0, core * QW), (2, in_rows, QW))
        return jnp.concatenate([own, pair[:, :, 2 * QW :]], axis=2)

    def gate_half(side):
        return lax.dynamic_slice(low, (0, side * 2 * QW), (in_rows, 2 * QW))

    def gate_quarter(pair, core):
        return lax.dynamic_slice(pair, (0, 0, core * QW), (2, in_rows, QW))

    wide_pair = to_side(wide_half, side)
    low, wide_pair = tie(low, wide_pair)
    gate_pair = to_side(gate_half, side)
    wide_piece = to_core(wide_pair, wide_quarter, core).reshape(2, chip_rows, WIDE)
    gate_piece = to_core(gate_pair, gate_quarter, core).reshape(4 * in_rows, QW)

    def put_in(base, piece, chip):
        return lax.dynamic_update_slice(base, piece[:, None], (0, chip, 0, 0))

    wide_spread = Spread(
        wide_piece, groups, put_in, jnp.zeros((2, chips, chip_rows, WIDE), bf16)
    )

    conv_width, gain_width = conv_table.shape[1], norm_gains.shape[0]
    small_size = 5 * conv_width + gain_width
    small_pad = -(-small_size // 128) * 128
    small_row = jnp.concatenate(
        [conv_table.astype(bf16).reshape(-1), norm_gains.astype(bf16)]
    )
    wide_hops = [wide_spread.step()]
    small_all = gather_small(
        jnp.pad(small_row, (0, small_pad - small_size)),
        lambda block: after(block, wide_hops[0]),
    )
    devices = small_all.shape[0]
    conv_full = small_all[:, : 5 * conv_width].reshape(devices, 5, conv_width)
    conv_full = conv_full.transpose(1, 0, 2).reshape(5, CH).astype(f32)
    gains_full = small_all[:, 5 * conv_width : small_size].reshape(1, D + DI).astype(f32)
    first_gain = gains_full[:, :D]
    second_gain = lax.dynamic_slice(gains_full, (0, D + quarter * QW), (1, QW))
    conv_own = jnp.concatenate(
        [lax.dynamic_slice(conv_full, (0, quarter * QW), (5, QW)), conv_full[:, DI:]], axis=1
    )
    conv_own = jnp.pad(conv_own, ((0, 3), (0, WIDE - QC)))
    head_own = lax.dynamic_slice(head_table, (0, quarter * QH), (3, QH))
    head_rows = jnp.concatenate([-jnp.exp(head_own[0:1]), head_own[1:2]], axis=0)
    head_rows = jnp.pad(head_rows, ((0, 6), (0, 128 - QH)))
    skip = jnp.repeat(head_own[2:3], HEAD_DIM, axis=1)

    small = (first_gain, second_gain, conv_own, head_rows, skip)
    wide_hops += [wide_spread.step() for _ in range(groups - 2)]
    wide_spread.place()
    w_wide = wide_spread.base.reshape(D, WIDE)

    tokens_sent, gate_piece = tie(tokens, gate_piece)
    tok_far = other_side(tokens_sent)
    cotangent_sent, tok_far = tie(cotangent, tok_far)
    tok_near_b, tok_far_b = other_core(tokens), other_core(tok_far)

    out_low = out_weight.astype(bf16)
    out_piece = in_order(
        core, columns_of(out_low, core), other_core(columns_of(out_low, 1 - core))
    )
    both_piece = jnp.stack([gate_piece, out_piece]).reshape(2, 2, chip_rows, QW)
    both_piece = after(both_piece, wide_hops[-1])

    def keep(base, piece, chip):
        return base + [(piece, chip)]

    both_spread = Spread(both_piece, groups, keep, [], (w_wide,))
    cot_far = other_side(cotangent_sent)
    cots = (cotangent, cot_far, other_core(cotangent), other_core(cot_far))

    start = (jnp.zeros((8, QC), f32), jnp.zeros((STATE, QW), f32))
    buffers, carried = None, start
    gain = first_gain
    for part in range(4):
        near, far = (tok_near_b, tok_far_b) if part >= 2 else (tokens, tok_far)
        *buffers, tail, state = run_forward(
            place, near, far, gain, w_wide, conv_own, head_rows, skip,
            carried if part % 2 else start, buffers, part,
        )
        carried = (tail, state)
        if both_spread.hop < groups - 1:
            moved = both_spread.step((buffers[0],), (buffers[0],))
            waits = [piece for piece, _ in both_spread.base[-2:]]
            gain = after(first_gain, moved, *waits)
    while both_spread.hop < groups - 1:
        both_spread.step()
    both_spread.place((buffers[0],))
    pieces, origins = zip(*both_spread.base)
    w_gate, w_own, w_send = run_assemble(
        jnp.concatenate([place, jnp.stack(origins).astype(jnp.int32)]), pieces
    )
    w_gate = w_gate.reshape(D, QW)
    w_out = (w_own.reshape(QW, QW), other_core(w_send).reshape(QW, QW))
    normed, normed_turned, proj, scanned, mem = buffers
    gate, grad_shaped, stats = run_gate(
        place, normed, w_gate, cots, w_out, second_gain, scanned
    )
    stats = stats + other_side(stats)
    swapped = other_core(stats)
    stats = stats + jnp.concatenate([swapped[:, ROWS:], swapped[:, :ROWS]], axis=1)
    shaped_turned, layer_a, layer_b, scan_grad, gate_grad, gain_grad = run_finish(
        place, stats, gate, grad_shaped, scanned, w_out, second_gain
    )

    layer_far = other_core(layer_b)
    out_grad = run_outer(shaped_turned, cots)
    layer_far, out_grad = tie(layer_far, out_grad)
    layer_send = (layer_a[HALF:].astype(f32) + layer_far[HALF:].astype(f32)).astype(bf16)
    layer_side = other_side(layer_send)

    split = (chips // 2, 2, chip_rows)
    out_far = other_core(columns_of(out_grad, 1 - core)).reshape(*split, QW)
    out_pieces = (out_grad.reshape(*split, D), out_far)
    both_pieces, gate_dots = run_pieces(
        place, normed_turned, after(gate_grad, layer_send), chips, w_gate, (0, 1), out_pieces
    )

    def blocks_of(pieces):
        return lambda chip: pick(pieces, chip, 0)

    both_sums = Collect(blocks_of(both_pieces), groups)

    def backward(group, sequence, carry, buffers, *waits):
        return run_backward(
            place, group, sequence, proj, scanned, after(scan_grad, *waits), mem, conv_own,
            head_rows, skip, carry, buffers,
        )

    first_b = backward(0, 1, None, (), both_pieces)
    both_sum = both_sums.step(first_b[-1])
    first_a = backward(0, 0, None, first_b[:2], both_sum)
    pay_grad, carry = first_a[:2]
    pay_pieces, pay_dots = run_pieces(place, normed_turned, pay_grad, chips, w_wide, (0,))
    pay_sums = Collect(blocks_of(pay_pieces), groups)
    both_sum = both_sums.step(pay_pieces)
    second_b = backward(1, 1, carry, (), both_sum, layer_side, pay_pieces)
    pay_sum = pay_sums.step(second_b[-1])
    both_sum = both_sums.step(second_b[-1])
    second_a = backward(1, 0, carry, second_b[:1], both_sum, pay_sum)
    rest_grad = second_a[0]
    pay_sum = pay_sums.step(second_a[-1])
    both_sum = both_sums.step(second_a[-1]) if groups == 4 else both_sums.rest()
    rest_pieces, rest_dots = run_pieces(
        place, normed_turned, after(rest_grad, pay_sum, both_sum), chips, w_wide, (1, 2)
    )
    rest_sums = Collect(blocks_of(rest_pieces), groups)
    pay_sum = pay_sums.step(rest_pieces)
    both_sum, pay_sum = tie(both_sum, pay_sum)
    gate_cores = from_cores(both_sum[0].reshape(2, 2, in_rows, QW), core)
    out_rows_sum = both_sum[1].reshape(2, out_rows, QW)
    out_rows_far = other_core(pick(out_rows_sum, 1 - core, 0))

    conv_grad = jnp.concatenate(
        [first_a[2] + first_b[2], second_a[1] + second_b[1], second_a[2] + second_b[2]], axis=1
    )
    head_grad = first_a[3] + first_b[3] + second_a[3] + second_b[3]
    skip_grad = jnp.concatenate([first_a[4] + first_b[4], second_a[4] + second_b[4]], axis=1)
    skip_grad = skip_grad[0].reshape(QH, HEAD_DIM).sum(axis=1)
    conv_all = jnp.concatenate(
        [
            lax.dynamic_update_slice(
                jnp.zeros((5, DI), f32), conv_grad[:5, :QW], (0, quarter * QW)
            ),
            conv_grad[:5, QW:],
        ],
        axis=1,
    )
    gains_all = jnp.concatenate(
        [
            (gate_dots + pay_dots + rest_dots)[0:1] / first_gain,
            lax.dynamic_update_slice(jnp.zeros((1, DI), f32), gain_grad[0:1], (0, quarter * QW)),
        ],
        axis=1,
    )
    heads_all = lax.dynamic_update_slice(
        jnp.zeros((3, HEADS), f32),
        jnp.concatenate([head_grad[0:2, :QH], skip_grad[None]], axis=0),
        (0, quarter * QH),
    )
    packed = jnp.concatenate(
        [
            conv_all.reshape(-1, 128),
            gains_all.reshape(-1, 128),
            jnp.pad(heads_all.reshape(-1), (0, 256 - 3 * HEADS)).reshape(2, 128),
        ],
        axis=0,
    )

    def input_grad(sequence, far, *waits):
        return run_input_grad(
            place, sequence, far, gate_grad, pay_grad, after(rest_grad, *waits), w_gate, w_wide
        )

    far_b = input_grad(1, True, rest_pieces, pay_sum, packed, gate_cores, out_rows_far)
    far_core = other_core(far_b)
    gate_sum = from_sides(gate_cores, side)
    rest_sum = rest_sums.step(far_b)
    pay_sum = pay_sums.step(far_b) if groups == 4 else pay_sums.rest()
    packed = packed + after(other_side(packed), far_b)
    far_a = input_grad(0, True, rest_sum, pay_sum, packed, gate_sum)
    grad_send = (far_a.astype(f32) + far_core.astype(f32)).astype(bf16)
    pay_cores = from_cores(pay_sum.reshape(2, 2, in_rows, GC), core)
    rest_sum = rest_sums.step(far_a)
    packed = packed + after(other_core(packed), far_a)
    near_b = input_grad(1, False, rest_sum, grad_send, packed, pay_cores)
    part = HALF // 4
    sides = [other_side(grad_send[:part])]
    near_core = other_core(near_b)
    rest_sum = rest_sums.step(near_b)
    sides[0], near_b = tie(sides[0], near_b)
    packed = packed + after(flip(packed, 2), near_b)
    near_a = input_grad(0, False, rest_sum, packed, sides[0])
    sides.append(other_side(grad_send[part : 3 * part]))
    if groups == 4:
        rest_sum = rest_sums.step(near_a)
    else:
        rest_sum = rest_sums.rest()
    packed = sum_small(after(packed, near_a), 4)
    pay_sum = from_sides(pay_cores, side)
    rest_sum, pay_sum, layer_side, sides[1] = tie(rest_sum, pay_sum, layer_side, sides[1])
    sides.append(other_side(grad_send[3 * part :]))
    layer_out = (
        tokens.astype(f32) + layer_a[:HALF].astype(f32) + layer_far[:HALF].astype(f32)
    ) + layer_side.astype(f32)
    out_rows_sum, near_a = tie(out_rows_sum, near_a)
    out_grad = in_order(core, pick(out_rows_sum, core, 0), out_rows_far, axis=1).astype(f32)
    tokens_grad = run_tokens_grad(tokens, cotangent, first_gain, near_a, near_core, sides)
    conv_rows, gain_rows = 5 * CH // 128, (D + DI) // 128
    conv_sum = lax.dynamic_slice(
        packed[:conv_rows].reshape(5, CH), (0, number * conv_width), (5, conv_width)
    )
    gains_sum = lax.dynamic_slice(
        packed[conv_rows : conv_rows + gain_rows].reshape(-1), (number * gain_width,), (gain_width,)
    )
    head_sum = packed[conv_rows + gain_rows :].reshape(-1)[: 3 * HEADS].reshape(3, HEADS)

    rest_sum, shared_sum = from_group_shared(
        rest_sum.reshape(2, 2, in_rows, 2 * GC), side, core
    )
    columns = [gate_sum]
    for n in range(QUARTERS):
        columns += [pay_sum[:, n * GC : (n + 1) * GC], rest_sum[:, n * GC : (n + 1) * GC]]
    rest_sum, packed = tie(rest_sum, packed)
    in_grad = jnp.concatenate(
        [column.astype(f32) for column in columns] + [shared_sum[:, : 2 * STATE + HEADS]], axis=1
    )
    in_new = adamw_step(in_weight, in_moment, in_square, in_grad, rate_matrix, weight_decay)
    out_new = adamw_step(out_weight, out_moment, out_square, out_grad, rate_matrix, weight_decay)
    conv_new = adamw_step(conv_table, conv_moment, conv_square, conv_sum, rate_vector, 0.0)
    gains_new = adamw_step(norm_gains, gain_moment, gain_square, gains_sum, rate_vector, 0.0)
    head_new = adamw_step(head_table, head_moment, head_square, head_sum, rate_heads, 0.0)
    return (layer_out, tokens_grad, *in_new, *out_new, *conv_new, *gains_new, *head_new)


def solution(mesh):
    tokens = P(("dp", "seq"), None)
    rows = P(("seq", "dp"), None)
    columns = P(None, ("seq", "dp"))
    line = P(("seq", "dp"))
    return jax.shard_map(
        on_device,
        mesh=mesh,
        in_specs=(tokens,) * 2 + (rows,) * 6 + (columns,) * 3 + (line,) * 3 + (P(),) * 3,
        out_specs=(tokens,) * 2 + (rows,) * 6 + (columns,) * 3 + (line,) * 3 + (P(),) * 3,
        check_vma=False,
    )
```

```python
import functools

import jax
import jax.numpy as jnp
from jax import lax
from jax.experimental import pallas as pl
from jax.experimental.pallas import tpu as pltpu
from jax.sharding import PartitionSpec as P

D = 1536
HEADS = 48
HEAD_DIM = 64
STATE = 128
CONV = 4
STEP = 10
DI = 3072
CH = 3328

QUARTERS = 4
QH = HEADS // QUARTERS
QW = DI // QUARTERS
QC = QW + 2 * STATE
WIDE = QC + 128
GC = QW // 2
LEN = 256
ROWS = 1024
HALF = ROWS // 2
BLOCKS = ROWS // LEN

norm_epsilon = 1e-05
adam_epsilon = 1e-08
beta_first = 0.9
beta_second = 0.999
rate_matrix = 0.05
rate_vector = 0.5
rate_heads = 2.0
weight_decay = 0.1
LOG2E = 1.4426950408889634

f32 = jnp.float32
bf16 = jnp.bfloat16
NN = (((1,), (0,)), ((), ()))
NT = (((1,), (1,)), ((), ()))
TN = (((0,), (0,)), ((), ()))
MIB = 1024 * 1024


def mm(a, b, dims=NN):
    return lax.dot_general(a, b, dims, preferred_element_type=f32)


def mm_exact(a, b, dims=NN):
    return lax.dot_general(
        a, b, dims, precision=lax.Precision.HIGHEST, preferred_element_type=f32
    )


def spread_heads(columns, first_head, count):
    rows = columns.shape[0]
    low = lax.broadcasted_iota(jnp.int32, (rows, 128), 1) < HEAD_DIM
    parts = []
    for h in range(first_head, first_head + count, 2):
        first = jnp.broadcast_to(columns[:, h : h + 1], (rows, 128))
        second = jnp.broadcast_to(columns[:, h + 1 : h + 2], (rows, 128))
        parts.append(jnp.where(low, first, second))
    return jnp.concatenate(parts, axis=1)


def softplus(v):
    return jnp.maximum(v, 0.0) + jnp.log1p(jnp.exp(-jnp.abs(v)))


def triangle(lower):
    rows = lax.broadcasted_iota(jnp.int32, (LEN, LEN), 0)
    cols = lax.broadcasted_iota(jnp.int32, (LEN, LEN), 1)
    return rows >= cols if lower else rows <= cols


def halves(pair):
    low = lax.broadcasted_iota(jnp.int32, pair.shape, 1) < HEAD_DIM
    zero = jnp.zeros_like(pair)
    return jnp.where(low, pair, zero), jnp.where(low, zero, pair)


def parts_of(v):
    high = v.astype(bf16)
    return high, (v - high.astype(f32)).astype(bf16)


def affinity_of(first, second):
    both = jnp.concatenate(first, axis=1)
    high = jnp.concatenate([second[0], second[0]], axis=1)
    return mm(both, high, NT) + mm(first[0], second[1], NT)


def running(mask, v):
    high = v.astype(bf16).astype(f32)
    left = v - high
    middle = left.astype(bf16).astype(f32)
    packed = high + pltpu.roll(middle, 16, 1) + pltpu.roll(left - middle, 32, 1)
    product = mm(mask.astype(f32).astype(bf16), packed.astype(bf16))
    return product + pltpu.roll(product, 112, 1) + pltpu.roll(product, 96, 1)


def twice(pair):
    low = lax.broadcasted_iota(jnp.int32, pair.shape, 1) < HEAD_DIM
    turned = pltpu.roll(pair, HEAD_DIM, 1)
    return jnp.where(low, pair, turned).astype(bf16), jnp.where(low, turned, pair).astype(bf16)


def beside_rest(pair, rest):
    low = lax.broadcasted_iota(jnp.int32, pair.shape, 1) < HEAD_DIM
    turned = pltpu.roll(rest, HEAD_DIM, 1).astype(bf16)
    return jnp.where(low, pair, turned), jnp.where(low, turned, pair)


def filter_rows(ext, conv_ref):
    width = ext.shape[1]
    total = conv_ref[CONV : CONV + 1, :width]
    for k in range(CONV):
        total = total + conv_ref[k : k + 1, :width] * ext[5 + k : 5 + k + LEN, :]
    return total


def forward_kernel(
    half, place, near, far, gain, w, conv, head, skip, tail_in, state_in, *rest
):
    normed_out, turned_out, proj_out, filtered_out, scanned_out, mem_out = rest[-10:-4]
    tail_out, state_out, ext, mem = rest[-4:]
    j = pl.program_id(0)

    @pl.when(j == 0)
    def _():
        ext[0:8, :] = tail_in[...]
        mem[...] = state_in[...]

    wide = jnp.where(place[0] == half, near[...], far[...]).astype(f32)
    inv_one = lax.rsqrt(jnp.mean(wide * wide, axis=1, keepdims=True) + norm_epsilon)
    normed = (wide * inv_one * gain[...]).astype(bf16)
    normed_out[...] = normed
    turned_out[...] = normed.T
    proj = mm(normed, w[...])
    proj_out[...] = proj
    ext[8 : 8 + LEN, :] = proj[:, :QC]
    filtered = filter_rows(ext, conv)
    filtered_out[:, :QC] = filtered
    ext[0:8, :] = ext[LEN : LEN + 8, :]
    active = filtered * jax.nn.sigmoid(filtered)
    payload = active[:, :QW]
    writers = parts_of(active[:, QW : QW + STATE])
    readers = parts_of(active[:, QW + STATE :])
    writer = writers[0]

    steps = softplus(pltpu.roll(proj[:, QC:], place[2], 1) + head[1:2, :])
    rates = head[0:1, :] * steps
    causal = triangle(True)
    summed = running(causal, rates) * LOG2E
    across = summed.T
    affinity = jnp.where(causal, affinity_of(readers, writers), 0.0)

    dosed = payload * spread_heads(steps, 0, QH)
    dosed_low = dosed.astype(bf16)
    state = mem[...]
    mem_out[0] = state
    grown = jnp.exp2(spread_heads(summed, 0, QH))
    state_low, state_rest = parts_of(state)
    carried = mm(jnp.concatenate(readers, axis=1), jnp.concatenate([state_low] * 2, axis=0))
    carried = (carried + mm(readers[0], state_rest)) * grown
    within = []
    for pair in range(QH // 2):
        weights = []
        for h in (2 * pair, 2 * pair + 1):
            gap = jnp.minimum(summed[:, h : h + 1] - across[h : h + 1, :], 0.0)
            weights.append((jnp.exp2(gap) * affinity).astype(bf16))
        first, second = halves(dosed_low[:, 128 * pair : 128 * pair + 128])
        within.append(
            mm(jnp.concatenate(weights, axis=1), jnp.concatenate([first, second], axis=0))
        )
    scanned_out[...] = jnp.concatenate(within, axis=1) + carried + payload * skip[...]

    last = summed[LEN - 1 : LEN, :]
    remain = jnp.exp2(spread_heads(last - summed, 0, QH))
    added = mm(writer, (dosed * remain).astype(bf16), TN)
    mem[...] = state * jnp.exp2(spread_heads(last, 0, QH)) + added
    tail_out[...] = ext[0:8, :]
    state_out[...] = mem[...]


def by_core(core, own, other):
    first = core == 0
    return jnp.where(first, own, other), jnp.where(first, other, own)


def at_hand(side, near_a, far_a, near_b, far_b):
    j = pl.program_id(0)
    near = (j % BLOCKS) // (BLOCKS // 2) == side
    first = jnp.where(near, near_a[...], far_a[...])
    return jnp.where(j < BLOCKS, first, jnp.where(near, near_b[...], far_b[...]))


def gate_kernel(
    place, normed, w_gate, cot_na, cot_fa, cot_nb, cot_fb, w_own, w_other, gain, scanned,
    gate_out, shaped_grad_out, stats_out,
):
    gate = mm(normed[...], w_gate[...])
    cot = at_hand(place[0], cot_na, cot_fa, cot_nb, cot_fb)
    left, right = by_core(place[1], w_own[...], w_other[...])
    grad_shaped = mm(cot[:, :QW], left, NT) + mm(cot[:, QW:], right, NT)
    gate_out[...] = gate
    shaped_grad_out[...] = grad_shaped
    gated = scanned[...] * (gate * jax.nn.sigmoid(gate))
    squares = jnp.sum(gated * gated, axis=1, keepdims=True)
    inner = jnp.sum(grad_shaped * gain[...] * gated, axis=1, keepdims=True)
    lane = lax.broadcasted_iota(jnp.int32, (LEN, 128), 1)
    both = jnp.where(lane == 0, squares, jnp.where(lane == 1, inner, 0.0))
    stats_out[...] = both.T[0:8, :]


def finish_kernel(
    place, stats, gate_in, grad_shaped_in, scanned_in, w_own, w_other, gain,
    turned_out, layer_a_out, layer_b_out, scan_grad_out, gate_grad_out, gain_grad,
):
    j = pl.program_id(0)
    table = jnp.concatenate([stats[...], jnp.zeros((120, LEN), f32)], axis=0).T
    inv_two = lax.rsqrt(table[:, 0:1] / DI + norm_epsilon)
    mean = inv_two * table[:, 1:2] / DI
    gate = gate_in[...]
    scanned = scanned_in[...]
    grad_shaped = grad_shaped_in[...]
    sig = jax.nn.sigmoid(gate)
    lift = gate * sig
    unit = scanned * lift * inv_two
    shaped = (unit * gain[...]).astype(bf16)
    turned_out[...] = shaped.T
    left, right = by_core(place[1], w_own[...], w_other[...])
    layer = jnp.concatenate([mm(shaped, left), mm(shaped, right)], axis=1).astype(bf16)

    @pl.when(j < BLOCKS)
    def _():
        layer_a_out[...] = layer

    @pl.when(j >= BLOCKS)
    def _():
        layer_b_out[...] = layer

    grad_gated = inv_two * (grad_shaped * gain[...] - unit * mean)
    scan_grad_out[...] = grad_gated * lift
    gate_grad_out[...] = (grad_gated * scanned * sig * (1.0 + gate * (1.0 - sig))).astype(bf16)

    @pl.when(j == 0)
    def _():
        gain_grad[...] = jnp.zeros_like(gain_grad)

    gain_grad[0:1, :] += jnp.sum(grad_shaped * unit, axis=0, keepdims=True)


def backward_kernel(
    place, proj_in, filtered_in, scanned_in, grad_in, mem_in, conv, head, skip, later_in, state_in,
    *rest
):
    out, conv_grad, head_grad, skip_grad, later_out, state_out, later, grad_mem = rest[-8:]
    i = pl.program_id(0)

    @pl.when(i == 0)
    def _():
        later[LEN : LEN + 8, :] = later_in[...]
        grad_mem[...] = state_in[...]
        conv_grad[...] = jnp.zeros_like(conv_grad)
        head_grad[...] = jnp.zeros_like(head_grad)
        skip_grad[...] = jnp.zeros_like(skip_grad)

    @pl.when(i > 0)
    def _():
        later[LEN : LEN + 8, :] = later[0:8, :]

    conv_in = proj_in[:, :QC]
    filtered = filtered_in[:, :QC]
    sig = jax.nn.sigmoid(filtered)
    active = filtered * sig
    slope = sig * (1.0 + filtered * (1.0 - sig))
    payload = active[:, :QW]
    writers = parts_of(active[:, QW : QW + STATE])
    readers = parts_of(active[:, QW + STATE :])
    writer, reader = writers[0], readers[0]

    raw = pltpu.roll(proj_in[:, QC:], place[2], 1) + head[1:2, :]
    steps = softplus(raw)
    rates = head[0:1, :] * steps
    summed = running(triangle(True), rates) * LOG2E
    across = summed.T
    upper = triangle(False)
    affinity = jnp.where(upper, affinity_of(writers, readers), 0.0)

    grad = grad_in[...]
    grad_low = grad.astype(bf16)
    grad_rest = grad - grad_low.astype(f32)
    dose = spread_heads(steps, 0, QH)
    dosed = payload * dose
    dosed_low = dosed.astype(bf16)
    state = mem_in[0]
    state_grad = grad_mem[...]
    state_grad_low = state_grad.astype(bf16)
    last = summed[LEN - 1 : LEN, :]
    remain = jnp.exp2(spread_heads(last - summed, 0, QH))
    from_state = mm(writer, state_grad_low) * remain

    mixed = jnp.zeros((LEN, LEN), f32)
    within = []
    for pair in range(QH // 2):
        lanes = slice(128 * pair, 128 * pair + 128)
        grads = halves(grad_low[:, lanes])
        doses = twice(dosed[:, lanes])
        parts = beside_rest(grad_low[:, lanes], grad_rest[:, lanes])
        weights = []
        for n in range(2):
            h = 2 * pair + n
            gap = jnp.minimum(across[h : h + 1, :] - summed[:, h : h + 1], 0.0)
            decay = jnp.exp2(gap)
            weights.append((decay * affinity).astype(bf16))
            mixed = mixed + decay * mm(doses[n], parts[n], NT)
        within.append(mm(jnp.concatenate(weights, axis=1), jnp.concatenate(grads, axis=0)))
    unit = jnp.concatenate(within, axis=1) + from_state

    payload_grad = dose * unit + skip[...] * grad
    core = scanned_in[...] - payload * skip[...]
    dosed_wide = dosed_low.astype(f32)
    balance = grad_low.astype(f32) * core - dosed_wide * unit
    high_part = balance.astype(bf16)
    low_part = (balance - high_part.astype(f32)).astype(bf16)
    decay_last = jnp.exp2(spread_heads(last, 0, QH))
    at_end = jnp.sum(dosed_wide * from_state, axis=0, keepdims=True) + decay_last * jnp.sum(
        state_grad * state, axis=0, keepdims=True
    )
    end_high = at_end.astype(bf16).astype(f32)
    end_middle = (at_end - end_high).astype(bf16).astype(f32)
    row = lax.broadcasted_iota(jnp.int32, (16, QW), 0)
    end_parts = jnp.where(
        row == 0,
        end_high,
        jnp.where(row == 1, end_middle, jnp.where(row == 2, at_end - end_high - end_middle, 0.0)),
    ).astype(bf16)
    heads_of = (
        lax.broadcasted_iota(jnp.int32, (QW, 128), 0) // HEAD_DIM
        == lax.broadcasted_iota(jnp.int32, (QW, 128), 1)
    ).astype(f32)
    by_head = mm(
        jnp.concatenate([high_part, low_part, (payload * unit).astype(bf16), end_parts], axis=0),
        heads_of.astype(bf16),
    )
    balance_sum = by_head[:LEN] + by_head[LEN : 2 * LEN]
    direct = by_head[2 * LEN : 3 * LEN]
    end_sum = jnp.sum(by_head[3 * LEN :], axis=0, keepdims=True)
    rate_grad = running(upper, balance_sum) + end_sum
    step_grad = direct + head[0:1, :] * rate_grad
    raw_grad = step_grad * jax.nn.sigmoid(raw)
    head_grad[0:1, :] += jnp.sum(rate_grad * rates, axis=0, keepdims=True)
    head_grad[1:2, :] += jnp.sum(raw_grad, axis=0, keepdims=True)
    skip_grad[0:1, :] += jnp.sum(grad * payload, axis=0, keepdims=True)

    grown_wide = jnp.exp2(spread_heads(summed, 0, QH)) * grad
    grown_grad = grown_wide.astype(bf16)
    grown_rest = (grown_wide - grown_grad.astype(f32)).astype(bf16)
    kept = (remain * dosed).astype(bf16)
    mixed_low = jnp.where(upper, mixed, 0.0).astype(bf16)
    writer_grad = mm(mixed_low, reader) + mm(kept, state_grad_low, NT)
    state_low = state.astype(bf16)
    reader_grad = (
        mm(mixed_low, writer, TN) + mm(grown_grad, state_low, NT) + mm(grown_rest, state_low, NT)
    )
    grad_mem[...] = decay_last * state_grad + mm(reader, grown_grad, TN)

    filtered_grad = jnp.concatenate([payload_grad, writer_grad, reader_grad], axis=1) * slope
    later[0:LEN, :] = filtered_grad
    back = None
    sums = []
    for k in range(CONV):
        ahead = later[CONV - 1 - k : CONV - 1 - k + LEN, :]
        sums.append(jnp.sum(ahead * conv_in, axis=0, keepdims=True))
        term = conv[k : k + 1, :QC] * ahead
        back = term if back is None else back + term
    sums.append(jnp.sum(filtered_grad, axis=0, keepdims=True))
    conv_grad[...] += jnp.concatenate(sums + [jnp.zeros((7 - CONV, QC), f32)], axis=0)
    out[:, :QC] = back.astype(bf16)
    out[:, QC:] = pltpu.roll(raw_grad, place[3], 1).astype(bf16)
    later_out[...] = later[0:8, :]
    state_out[...] = grad_mem[...]


def outer_kernel(left, *rest):
    out = rest[-1]
    total = None
    for n, right in enumerate(rest[:-1]):
        part = mm(left[:, n * HALF : (n + 1) * HALF], right[...])
        total = part if total is None else total + part
    out[...] = total.astype(bf16)


def pieces_kernel(chip_rows, blocks, place, left, right, *rest):
    out, dots = rest[-2:]
    weights, others = rest[:blocks], rest[blocks:-2]
    tile = left.shape[0]
    i = pl.program_id(0)
    per = tile // chip_rows
    steps = out.shape[0] // per
    result = mm(left[...], right[...])
    sums = jnp.zeros((tile, 128), f32)
    for n, weight in enumerate(weights):
        product = result[:, n * GC : (n + 1) * GC] * weight[...].astype(f32)
        sums = sums + (product[:, :128] + product[:, 128:256] + product[:, 256:])
    dots[...] = jnp.broadcast_to(jnp.sum(sums.T, axis=0, keepdims=True), (8, tile))
    for n in range(per):
        part = result[n * chip_rows : (n + 1) * chip_rows].astype(bf16)
        if others:
            out[(i % steps) * per + n, 0, i // steps] = part
        else:
            out[(i % steps) * per + n, i // steps] = part
    if others:
        half = out.shape[0] // 2

        @pl.when(i == 0)
        def _():
            own, other = others
            core = place[1]
            out[pl.ds(core * half, half), 1] = own[...]
            out[pl.ds((1 - core) * half, half), 1] = other[...]


def input_grad(gate_grad, wide_grad, w_gate, w_wide):
    grad = mm(gate_grad[...], w_gate[...], NT) + mm(wide_grad[...], w_wide[...], NT)
    return grad.astype(bf16)


def input_grad_kernel(place, *refs):
    refs[-1][...] = input_grad(*refs[:-1])


def own_first(j, place):
    per = BLOCKS // 2
    half = j // per
    side = place[0]
    return (half + side - 2 * half * side) * per + j % per


def rows_of(width, first=0):
    return pl.BlockSpec((LEN, width), lambda j, *_: (j + first, 0))


def moved_columns(height):
    return pl.BlockSpec(
        (height, LEN),
        lambda j, place: (0, own_first(j % BLOCKS, place) + (j // BLOCKS) * BLOCKS),
    )


def first_rows(width):
    return pl.BlockSpec(
        (LEN, width), lambda j, place: (own_first(jnp.minimum(j, BLOCKS - 1), place), 0)
    )


def second_rows(width):
    return pl.BlockSpec(
        (LEN, width), lambda j, place: (own_first(jnp.maximum(j - BLOCKS, 0), place), 0)
    )


def whole(*shape):
    return pl.BlockSpec(shape, lambda j, *_: (0,) * len(shape))


def params():
    return pltpu.CompilerParams(
        vmem_limit_bytes=60 * MIB, dimension_semantics=("arbitrary",)
    )


def shape(dims, dtype):
    return jax.ShapeDtypeStruct(dims, dtype)


def cost(microseconds):
    return pl.CostEstimate(
        flops=int(microseconds * 1e9),
        bytes_accessed=int(microseconds * 3.5e6),
        transcendentals=0,
    )


def run_forward(place, near, far, gain, w, conv, head, skip, carried, buffers, part):
    per = BLOCKS // 2
    first = part * per
    if buffers is None:
        buffers = ()
    anywhere = pl.BlockSpec(memory_space=pl.ANY)
    return pl.pallas_call(
        functools.partial(forward_kernel, part % 2),
        grid_spec=pltpu.PrefetchScalarGridSpec(
            num_scalar_prefetch=1,
            grid=(per,),
            in_specs=[
                rows_of(D), rows_of(D), whole(1, D), whole(D, WIDE), whole(8, WIDE), whole(8, 128), whole(1, QW),
                whole(8, QC), whole(STATE, QW),
            ] + [anywhere] * len(buffers),
            out_specs=[
                rows_of(D, first), pl.BlockSpec((D, LEN), lambda j, *_: (0, j + first)),
                rows_of(WIDE, first), rows_of(WIDE, first), rows_of(QW, first),
                pl.BlockSpec((1, STATE, QW), lambda j, *_: (j + first, 0, 0)),
                whole(8, QC), whole(STATE, QW),
            ],
            scratch_shapes=[pltpu.VMEM((LEN + 8, QC), f32), pltpu.VMEM((STATE, QW), f32)],
        ),
        out_shape=[
            shape((2 * ROWS, D), bf16), shape((D, 2 * ROWS), bf16),
            shape((2 * ROWS, WIDE), f32), shape((2 * ROWS, WIDE), f32),
            shape((2 * ROWS, QW), f32), shape((2 * BLOCKS, STATE, QW), f32), shape((8, QC), f32), shape((STATE, QW), f32),
        ],
        input_output_aliases={10 + n: n for n in range(len(buffers))},
        compiler_params=params(),
        cost_estimate=cost(13),
        name="forward_scan",
    )(place, near, far, gain, w, conv, head, skip, *carried, *buffers)


def assemble_kernel(count, place, *refs):
    pieces, (gate, own, send) = refs[:count], refs[count:]
    half = count // 2
    for n, piece in enumerate(pieces):
        chip = place[4 + n]
        gate[0, chip] = piece[0, 0]
        gate[1, chip] = piece[0, 1]
        mine = chip // half == place[1]

        @pl.when(mine)
        def _():
            own[chip % half] = piece[1]

        @pl.when(jnp.logical_not(mine))
        def _():
            send[chip % half] = piece[1]


def run_assemble(place, pieces):
    count = len(pieces)
    _, _, rows, width = pieces[0].shape
    outs = [(2, count, rows, width)] + [(count // 2, 2, rows, width)] * 2
    return pl.pallas_call(
        functools.partial(assemble_kernel, count),
        grid_spec=pltpu.PrefetchScalarGridSpec(
            num_scalar_prefetch=1,
            grid=(1,),
            in_specs=[whole(2, 2, rows, width)] * count,
            out_specs=[whole(*dims) for dims in outs],
        ),
        out_shape=[shape(dims, bf16) for dims in outs],
        compiler_params=params(),
        cost_estimate=cost(3),
        name="assemble",
    )(place, *pieces)


def run_gate(place, normed, w_gate, cots, w_out, gain, scanned):
    per = BLOCKS // 2

    def half(sequence, far):
        def index(j, place):
            first = sequence * BLOCKS + (1 - place[0] if far else place[0]) * per
            return (jnp.clip(j - first, 0, per - 1), 0)

        return pl.BlockSpec((LEN, D), index)

    return pl.pallas_call(
        gate_kernel,
        grid_spec=pltpu.PrefetchScalarGridSpec(
            num_scalar_prefetch=1,
            grid=(2 * BLOCKS,),
            in_specs=[
                rows_of(D), whole(D, QW), half(0, False), half(0, True), half(1, False),
                half(1, True), whole(QW, QW), whole(QW, QW), whole(1, QW), rows_of(QW),
            ],
            out_specs=[
                rows_of(QW), rows_of(QW), pl.BlockSpec((8, LEN), lambda j, *_: (0, j)),
            ],
        ),
        out_shape=[
            shape((2 * ROWS, QW), f32), shape((2 * ROWS, QW), f32), shape((8, 2 * ROWS), f32),
        ],
        compiler_params=params(),
        cost_estimate=cost(2),
        name="gate_and_stats",
    )(place, normed, w_gate, *cots, *w_out, gain, scanned)


def run_finish(place, stats, gate, grad_shaped, scanned, w_out, gain):
    return pl.pallas_call(
        finish_kernel,
        grid_spec=pltpu.PrefetchScalarGridSpec(
            num_scalar_prefetch=1,
            grid=(2 * BLOCKS,),
            in_specs=[
                pl.BlockSpec((8, LEN), lambda j, *_: (0, j)), rows_of(QW), rows_of(QW),
                rows_of(QW), whole(QW, QW), whole(QW, QW), whole(1, QW),
            ],
            out_specs=[
                moved_columns(QW), first_rows(D), second_rows(D), rows_of(QW), rows_of(QW),
                whole(8, QW),
            ],
        ),
        out_shape=[
            shape((QW, 2 * ROWS), bf16), shape((ROWS, D), bf16), shape((ROWS, D), bf16),
            shape((2 * ROWS, QW), f32), shape((2 * ROWS, QW), bf16), shape((8, QW), f32),
        ],
        compiler_params=params(),
        cost_estimate=cost(2),
        name="finish",
    )(place, stats, gate, grad_shaped, scanned, *w_out, gain)


def run_backward(
    place, sequence, half, proj, filtered, scanned, grad, mem, conv, head, skip, carried, buffers
):
    per = BLOCKS // 2
    top = sequence * BLOCKS + (half + 1) * per - 1

    def back(width):
        return pl.BlockSpec((LEN, width), lambda i, *_: (top - i, 0))

    args = [place, proj, filtered, scanned, grad, mem, conv, head, skip, *carried]
    return pl.pallas_call(
        backward_kernel,
        grid_spec=pltpu.PrefetchScalarGridSpec(
            num_scalar_prefetch=1,
            grid=(per,),
            in_specs=[
                back(WIDE), back(WIDE), back(QW), back(QW),
                pl.BlockSpec((1, STATE, QW), lambda i, *_: (top - i, 0, 0)),
                whole(8, WIDE), whole(8, 128), whole(1, QW), whole(8, QC), whole(STATE, QW),
            ] + [pl.BlockSpec(memory_space=pl.ANY)] * len(buffers),
            out_specs=[
                back(WIDE), whole(8, QC), whole(8, 128), whole(8, QW), whole(8, QC),
                whole(STATE, QW),
            ],
            scratch_shapes=[pltpu.VMEM((LEN + 8, QC), f32), pltpu.VMEM((STATE, QW), f32)],
        ),
        out_shape=[
            shape((2 * ROWS, WIDE), bf16), shape((8, QC), f32), shape((8, 128), f32),
            shape((8, QW), f32), shape((8, QC), f32), shape((STATE, QW), f32),
        ],
        input_output_aliases={len(args) + n: n for n in range(len(buffers))},
        compiler_params=params(),
        cost_estimate=cost(2),
        name="backward_scan",
    )(*args, *buffers)


def run_outer(left, rights):
    tall, width = left.shape[0], rights[0].shape[1]
    tile = 384
    return pl.pallas_call(
        outer_kernel,
        grid=(tall // tile,),
        in_specs=[pl.BlockSpec((tile, 2 * ROWS), lambda i: (i, 0))]
        + [whole(HALF, width) for _ in rights],
        out_specs=pl.BlockSpec((tile, width), lambda i: (i, 0)),
        out_shape=shape((tall, width), bf16),
        compiler_params=params(),
        cost_estimate=cost(1),
        name="weight_grad",
    )(left, *rights)


def run_pieces(place, left, right, chips, weights, columns, others=()):
    tall, width = left.shape[0], right.shape[1]
    tile = 384
    chip_rows = tall // (2 * chips)
    dims = (chips,) + (2,) * (2 if others else 1) + (chip_rows, width)

    def block(column):
        return pl.BlockSpec((tile, GC), lambda i, *_: (i, column))

    beside_specs = []
    if others:
        part = others[1].shape
        beside_specs = [
            pl.BlockSpec(part, lambda i, place: (0, 0, 0, place[1])),
            whole(*part),
        ]
    return pl.pallas_call(
        functools.partial(pieces_kernel, chip_rows, len(columns)),
        grid_spec=pltpu.PrefetchScalarGridSpec(
            num_scalar_prefetch=1,
            grid=(tall // tile,),
            in_specs=[
                pl.BlockSpec((tile, 2 * ROWS), lambda i, *_: (i, 0)), whole(*right.shape),
            ] + [block(column) for column in columns] + beside_specs,
            out_specs=[whole(*dims), pl.BlockSpec((8, tile), lambda i, *_: (0, i))],
        ),
        out_shape=[shape(dims, bf16), shape((8, tall), f32)],
        compiler_params=params(),
        cost_estimate=cost(1),
        name="weight_grad",
    )(place, left, right, *([weights] * len(columns)), *others)


def tokens_grad_kernel(tok, cot, gain, near, core, *rest):
    sides, out = rest[:-1], rest[-1]
    i = pl.program_id(0)
    rows = out.shape[0]
    parts = [ref[n : n + rows, :] for ref in sides for n in range(0, ref.shape[0], rows)]
    side = parts[0]
    for n in range(1, len(parts)):
        side = jnp.where(i == n, parts[n], side)
    grad = near[...].astype(f32) + core[...].astype(f32) + side.astype(f32)
    wide = tok[...].astype(f32)
    inv_one = lax.rsqrt(jnp.mean(wide * wide, axis=1, keepdims=True) + norm_epsilon)
    unit = wide * inv_one
    lifted = grad * gain[...]
    mean = jnp.mean(lifted * unit, axis=1, keepdims=True)
    out[...] = cot[...].astype(f32) + inv_one * (lifted - unit * mean)


def run_tokens_grad(tokens, cotangent, gain, near, core, sides):
    rows = min(part.shape[0] for part in sides)
    block = pl.BlockSpec((rows, D), lambda i: (i, 0))
    return pl.pallas_call(
        tokens_grad_kernel,
        grid=(HALF // rows,),
        in_specs=[block, block, whole(1, D), block, block]
        + [whole(*part.shape) for part in sides],
        out_specs=block,
        out_shape=shape((HALF, D), f32),
        compiler_params=params(),
        cost_estimate=cost(4),
        name="tokens_grad",
    )(tokens, cotangent, gain, near, core, *sides)


def run_input_grad(place, sequence, far, gate_grad, wide_grad, w_gate, w_wide):
    per = BLOCKS // 2

    def rows(width):
        def index(j, place):
            half = 1 - place[0] if far else place[0]
            return (sequence * BLOCKS + half * per + j, 0)

        return pl.BlockSpec((LEN, width), index)

    return pl.pallas_call(
        input_grad_kernel,
        grid_spec=pltpu.PrefetchScalarGridSpec(
            num_scalar_prefetch=1,
            grid=(per,),
            in_specs=[rows(QW), rows(WIDE), whole(D, QW), whole(D, WIDE)],
            out_specs=rows_of(D),
        ),
        out_shape=shape((HALF, D), bf16),
        compiler_params=params(),
        cost_estimate=cost(1),
        name="input_grad",
    )(place, gate_grad, wide_grad, w_gate, w_wide)


def other_side(block):
    return lax.ppermute(block, "seq", [(0, 1), (1, 0)])


def after(block, *others):
    return lax.optimization_barrier((block, *others))[0]


def tie(*blocks):
    return lax.optimization_barrier(blocks)


def flip(block, bit):
    count = lax.axis_size("dp")
    return lax.ppermute(block, "dp", [(d, d ^ bit) for d in range(count)])


def other_core(block):
    return flip(block, 1)


def beside(block):
    return flip(block, 2)


def along(block):
    count = lax.axis_size("dp")
    return lax.ppermute(block, "dp", [(d, (d + 4) % count) for d in range(count)])


def in_order(place, own, received, axis=0):
    return jnp.where(
        place == 0,
        jnp.concatenate([own, received], axis=axis),
        jnp.concatenate([received, own], axis=axis),
    )


def pick(block, place, axis):
    return lax.dynamic_index_in_dim(block, place, axis, False)


class Spread:
    def __init__(self, piece, groups, put, base, hold=()):
        dp = lax.axis_index("dp")
        self.ring, self.beside_place = dp // 4, (dp // 2) % 2
        self.groups, self.put, self.base = groups, put, base
        self.hop, self.current = 0, piece
        self.neighbour = beside(after(piece, *hold) if hold else piece)

    def place(self, hold=()):
        origin = (self.ring + self.groups - self.hop) % self.groups
        current, neighbour = self.current, self.neighbour
        if hold:
            current, neighbour, *_ = tie(current, neighbour, *hold)
        self.base = self.put(self.base, current, 2 * origin + self.beside_place)
        self.base = self.put(self.base, neighbour, 2 * origin + 1 - self.beside_place)

    def step(self, hold=(), place_hold=()):
        moved = along(self.current)
        if hold:
            moved = after(moved, *hold)
        self.place(place_hold)
        self.hop, self.current, self.neighbour = self.hop + 1, moved, beside(moved)
        return moved


class Collect:
    def __init__(self, block_of, groups):
        dp = lax.axis_index("dp")
        self.ring, self.beside_place = dp // 4, (dp // 2) % 2
        self.block_of, self.groups = block_of, groups
        self.hop, self.total = 0, None
        self.first = self.block(1 - self.beside_place)
        self.received = beside(self.first)

    def block(self, place):
        target = (self.ring + 2 * self.groups - 1 - self.hop) % self.groups
        return self.block_of(2 * target + place)

    def step(self, *hold):
        received = after(self.received, *hold) if hold else self.received
        part = self.block(self.beside_place).astype(f32) + received.astype(f32)
        if self.hop:
            part = part + self.total.astype(f32)
        part = part.astype(bf16)
        self.hop += 1
        if self.hop < self.groups:
            part, following = tie(part, self.block(1 - self.beside_place))
            self.total = along(part)
            self.received = beside(following)
        return part

    def rest(self):
        part = None
        while self.hop < self.groups:
            part = self.step()
        return part


def gather_small(row, hold, later):
    dp = lax.axis_index("dp")
    block = row.reshape((1, 1) + row.shape)
    block = hold(in_order(lax.axis_index("seq"), block, other_side(block), axis=0))
    bit = 1
    while bit < lax.axis_size("dp"):
        received = flip(block, bit)
        if bit in later:
            received = after(received, later[bit])
        block = in_order((dp // bit) % 2, block, received, axis=1)
        bit *= 2
    return block.reshape((-1,) + row.shape)


def sum_small(block, bit, hold):
    while bit < lax.axis_size("dp"):
        block = block + after(flip(block, bit), hold)
        bit *= 2
    return block


def columns_of(block, half):
    return lax.dynamic_slice(block, (0, half * QW), (block.shape[0], QW))


def adamw_step(weight, moment, square, gradient, step_rate, decay_rate):
    moment_new = beta_first * moment + (1.0 - beta_first) * gradient
    square_new = beta_second * square + (1.0 - beta_second) * gradient * gradient
    first_fix = moment_new / (1.0 - beta_first**STEP)
    second_fix = square_new / (1.0 - beta_second**STEP)
    weight_new = weight - step_rate * (
        first_fix / (jnp.sqrt(second_fix) + adam_epsilon) + decay_rate * weight
    )
    return (weight_new, moment_new, square_new)


def to_side(halves_of, side):
    return in_order(side, halves_of(side)[None], other_side(halves_of(1 - side))[None])


def to_core(pair, quarter_of, core):
    return in_order(
        core, quarter_of(pair, core)[:, None], other_core(quarter_of(pair, 1 - core))[:, None], 1
    )


def from_cores(piece, core):
    return in_order(core, pick(piece, core, 1), other_core(pick(piece, 1 - core, 1)), 2)


def from_sides(cores, side, *hold):
    received = after(other_side(pick(cores, 1 - side, 0)), *hold)
    return in_order(side, pick(cores, side, 0), received, 1)


def from_cores_shared(piece, core):
    mine, got = pick(piece, core, 1), other_core(pick(piece, 1 - core, 1))
    cores = in_order(core, mine[:, :, :QW], got[:, :, :QW], 2)
    shared = (mine[:, :, QW:].astype(f32) + got[:, :, QW:].astype(f32)).astype(bf16)
    return jnp.concatenate([cores, shared], axis=2)


def from_sides_shared(both, side):
    mine, got = pick(both, side, 0), other_side(pick(both, 1 - side, 0))
    sides = in_order(side, mine[:, : 2 * QW], got[:, : 2 * QW], 1)
    return sides, mine[:, 2 * QW :].astype(f32) + got[:, 2 * QW :].astype(f32)


def on_device(
    tokens,
    cotangent,
    in_weight,
    in_moment,
    in_square,
    out_weight,
    out_moment,
    out_square,
    conv_table,
    conv_moment,
    conv_square,
    norm_gains,
    gain_moment,
    gain_square,
    head_table,
    head_moment,
    head_square,
):
    side = lax.axis_index("seq")
    dp = lax.axis_index("dp")
    core = dp % 2
    groups = lax.axis_size("dp") // 4
    chips = 2 * groups
    quarter = 2 * side + core
    number = side * lax.axis_size("dp") + dp
    turn = quarter * QH
    place = jnp.stack([side, core, 128 - turn, turn]).astype(jnp.int32)
    in_rows, out_rows = in_weight.shape[0], out_weight.shape[0]
    chip_rows = 2 * in_rows

    low = in_weight.astype(bf16)
    shared_own = jnp.pad(low[:, 2 * DI :], ((0, 0), (0, GC - 2 * STATE - HEADS)))

    def wide_half(side):
        own = lax.dynamic_slice(low, (0, DI + side * 2 * QW), (in_rows, 2 * QW))
        return jnp.concatenate([own, shared_own], axis=1)

    def wide_quarter(pair, core):
        own = lax.dynamic_slice(pair, (0, 0, core * QW), (2, in_rows, QW))
        return jnp.concatenate([own, pair[:, :, 2 * QW :]], axis=2)

    def gate_half(side):
        return lax.dynamic_slice(low, (0, side * 2 * QW), (in_rows, 2 * QW))

    def gate_quarter(pair, core):
        return lax.dynamic_slice(pair, (0, 0, core * QW), (2, in_rows, QW))

    wide_pair = to_side(wide_half, side)
    low, wide_pair = tie(low, wide_pair)
    gate_pair = to_side(gate_half, side)
    wide_piece = to_core(wide_pair, wide_quarter, core).reshape(2, chip_rows, WIDE)
    gate_piece = to_core(gate_pair, gate_quarter, core).reshape(4 * in_rows, QW)

    def put_in(base, piece, chip):
        return lax.dynamic_update_slice(base, piece[:, None], (0, chip, 0, 0))

    wide_spread = Spread(
        wide_piece, groups, put_in, jnp.zeros((2, chips, chip_rows, WIDE), bf16)
    )

    conv_width, gain_width = conv_table.shape[1], norm_gains.shape[0]
    small_size = 5 * conv_width + gain_width
    small_pad = -(-small_size // 128) * 128
    small_row = jnp.concatenate(
        [conv_table.astype(bf16).reshape(-1), norm_gains.astype(bf16)]
    )
    wide_hops = [wide_spread.step() for _ in range(groups - 1)]
    small_all = gather_small(
        jnp.pad(small_row, (0, small_pad - small_size)),
        lambda block: after(block, wide_hops[0]),
        {4: wide_hops[1]},
    )
    small_all = after(small_all, wide_hops[-1])
    devices = small_all.shape[0]
    conv_full = small_all[:, : 5 * conv_width].reshape(devices, 5, conv_width)
    conv_full = conv_full.transpose(1, 0, 2).reshape(5, CH).astype(f32)
    gains_full = small_all[:, 5 * conv_width : small_size].reshape(1, D + DI).astype(f32)
    first_gain = gains_full[:, :D]
    second_gain = lax.dynamic_slice(gains_full, (0, D + quarter * QW), (1, QW))
    conv_own = jnp.concatenate(
        [lax.dynamic_slice(conv_full, (0, quarter * QW), (5, QW)), conv_full[:, DI:]], axis=1
    )
    conv_own = jnp.pad(conv_own, ((0, 3), (0, WIDE - QC)))
    head_own = lax.dynamic_slice(head_table, (0, quarter * QH), (3, QH))
    head_rows = jnp.concatenate([-jnp.exp(head_own[0:1]), head_own[1:2]], axis=0)
    head_rows = jnp.pad(head_rows, ((0, 6), (0, 128 - QH)))
    skip = jnp.repeat(head_own[2:3], HEAD_DIM, axis=1)

    small = (first_gain, second_gain, conv_own, head_rows, skip)
    wide_spread.place()
    w_wide = wide_spread.base.reshape(D, WIDE)

    tokens_sent, gate_piece = tie(tokens, gate_piece)
    tok_far = other_side(tokens_sent)
    cotangent_sent, tok_far = tie(cotangent, tok_far)
    tok_near_b, tok_far_b = other_core(tokens), other_core(tok_far)

    out_low = out_weight.astype(bf16)
    out_piece = in_order(
        core, columns_of(out_low, core), other_core(columns_of(out_low, 1 - core))
    )
    both_piece = jnp.stack([gate_piece, out_piece]).reshape(2, 2, chip_rows, QW)
    both_piece = after(both_piece, wide_hops[-1])

    def keep(base, piece, chip):
        return base + [(piece, chip)]

    both_spread = Spread(both_piece, groups, keep, [], (w_wide,))
    cot_far = other_side(cotangent_sent)
    cots = (cotangent, cot_far, other_core(cotangent), other_core(cot_far))

    start = (jnp.zeros((8, QC), f32), jnp.zeros((STATE, QW), f32))
    buffers, carried = None, start
    gain = first_gain
    for part in range(4):
        near, far = (tok_near_b, tok_far_b) if part >= 2 else (tokens, tok_far)
        *buffers, tail, state = run_forward(
            place, near, far, gain, w_wide, conv_own, head_rows, skip,
            carried if part % 2 else start, buffers, part,
        )
        carried = (tail, state)
        if both_spread.hop < groups - 1:
            moved = both_spread.step((buffers[0],), (buffers[0],))
            waits = [piece for piece, _ in both_spread.base[-2:]]
            gain = after(first_gain, moved, *waits)
    while both_spread.hop < groups - 1:
        both_spread.step()
    both_spread.place((buffers[0],))
    pieces, origins = zip(*both_spread.base)
    w_gate, w_own, w_send = run_assemble(
        jnp.concatenate([place, jnp.stack(origins).astype(jnp.int32)]), pieces
    )
    w_gate = w_gate.reshape(D, QW)
    w_out = (w_own.reshape(QW, QW), other_core(w_send).reshape(QW, QW))
    normed, normed_turned, proj, filtered, scanned, mem = buffers
    gate, grad_shaped, stats = run_gate(
        place, normed, w_gate, cots, w_out, second_gain, scanned
    )
    stats = stats + other_side(stats)
    swapped = other_core(stats)
    stats = stats + jnp.concatenate([swapped[:, ROWS:], swapped[:, :ROWS]], axis=1)
    shaped_turned, layer_a, layer_b, scan_grad, gate_grad, gain_grad = run_finish(
        place, stats, gate, grad_shaped, scanned, w_out, second_gain
    )

    layer_far = other_core(layer_b)
    out_grad = run_outer(shaped_turned, cots)
    layer_far, out_grad = tie(layer_far, out_grad)
    layer_send = (layer_a[HALF:].astype(f32) + layer_far[HALF:].astype(f32)).astype(bf16)
    layer_side = other_side(layer_send)

    split = (chips // 2, 2, chip_rows)
    out_far = other_core(columns_of(out_grad, 1 - core)).reshape(*split, QW)
    out_pieces = (out_grad.reshape(*split, D), out_far)
    both_pieces, gate_dots = run_pieces(
        place, normed_turned, after(gate_grad, layer_send), chips, w_gate, (0, 1), out_pieces
    )

    def blocks_of(pieces):
        return lambda chip: pick(pieces, chip, 0)

    both_sums = Collect(blocks_of(both_pieces), groups)

    waits = (both_pieces,)
    buffers, sums = (), []
    for sequence in (1, 0):
        carried = start
        for half in (1, 0):
            wide_grad, *part_sums, later, state = run_backward(
                place, sequence, half, proj, filtered, scanned, after(scan_grad, *waits), mem,
                conv_own, head_rows, skip, carried, buffers,
            )
            buffers, carried = (wide_grad,), (later, state)
            sums.append(part_sums)
            both_sum = both_sums.step(part_sums[0])
            waits = (both_sum,)
            if len(sums) == 2:
                waits = (both_sum, layer_side)
    both_sum = both_sums.rest() if groups > 4 else both_sum
    conv_grad, head_grad, skip_grad = (sum(parts[1:], parts[0]) for parts in zip(*sums))
    rest_pieces, rest_dots = run_pieces(
        place, normed_turned, after(wide_grad, both_sum), chips, w_wide, (0, 1, 2)
    )
    rest_sums = Collect(blocks_of(rest_pieces), groups)
    both_sum, wide_grad = tie(both_sum, wide_grad)
    gate_cores = from_cores(both_sum[0].reshape(2, 2, in_rows, QW), core)
    out_rows_sum = both_sum[1].reshape(2, out_rows, QW)
    out_rows_far = other_core(pick(out_rows_sum, 1 - core, 0))

    skip_grad = skip_grad[0].reshape(QH, HEAD_DIM).sum(axis=1)
    conv_all = jnp.concatenate(
        [
            lax.dynamic_update_slice(
                jnp.zeros((5, DI), f32), conv_grad[:5, :QW], (0, quarter * QW)
            ),
            conv_grad[:5, QW:],
        ],
        axis=1,
    )
    gains_all = jnp.concatenate(
        [
            (gate_dots + rest_dots)[0:1] / first_gain,
            lax.dynamic_update_slice(jnp.zeros((1, DI), f32), gain_grad[0:1], (0, quarter * QW)),
        ],
        axis=1,
    )
    heads_all = lax.dynamic_update_slice(
        jnp.zeros((3, HEADS), f32),
        jnp.concatenate([head_grad[0:2, :QH], skip_grad[None]], axis=0),
        (0, quarter * QH),
    )
    packed = jnp.concatenate(
        [
            conv_all.reshape(-1, 128),
            gains_all.reshape(-1, 128),
            jnp.pad(heads_all.reshape(-1), (0, 256 - 3 * HEADS)).reshape(2, 128),
        ],
        axis=0,
    )

    def input_rows(sequence, far, *waits):
        return run_input_grad(
            place, sequence, far, gate_grad, after(wide_grad, *waits), w_gate, w_wide
        )

    far_b = input_rows(1, True, rest_sums.first, packed, gate_cores, out_rows_far)
    far_core = other_core(far_b)
    packed = packed + after(other_side(packed), far_b)
    far_a = input_rows(0, True, packed)
    rest_sum = rest_sums.step(far_a)
    gate_sum = from_sides(gate_cores, side, rest_sum)
    packed = packed + after(other_core(packed), far_a)
    grad_send = (far_a.astype(f32) + far_core.astype(f32)).astype(bf16)
    near_b = input_rows(1, False, rest_sum, grad_send, packed, gate_sum)
    part = HALF // 4
    sides = [other_side(grad_send[:part])]
    near_core = other_core(near_b)
    sides[0], near_b = tie(sides[0], near_b)
    rest_sum = rest_sums.step(sides[0])
    near_a = input_rows(0, False, rest_sum)
    sides.append(other_side(grad_send[part : 2 * part]))
    sides.append(other_side(grad_send[2 * part : 3 * part]))
    sides[1], near_a = tie(sides[1], near_a)
    rest_sum = rest_sums.step(sides[1])
    out_rows_sum = after(out_rows_sum, rest_sum)
    layer_side = after(layer_side, rest_sum)
    layer_out = (
        tokens.astype(f32) + layer_a[:HALF].astype(f32) + layer_far[:HALF].astype(f32)
    ) + layer_side.astype(f32)
    sides[2], rest_sum, layer_out = tie(sides[2], rest_sum, layer_out)
    rest_sum = rest_sums.step(sides[2])
    if rest_sums.hop < groups:
        rest_sum = rest_sums.rest()
    sides.append(other_side(grad_send[3 * part :]))
    out_grad = in_order(core, pick(out_rows_sum, core, 0), out_rows_far, axis=1).astype(f32)

    both_group, rest_sum = tie(
        from_cores_shared(rest_sum.reshape(2, 2, in_rows, WIDE), core), rest_sum
    )
    packed = after(packed, rest_sum)
    packed = packed + after(flip(packed, 2), both_group)
    rest_sum, shared_sum = from_sides_shared(both_group, side)
    packed = packed + after(flip(packed, 4), rest_sum)
    tokens_grad = run_tokens_grad(
        tokens, cotangent, after(first_gain, rest_sum), near_a, near_core, sides
    )
    packed = sum_small(packed, 8, tokens_grad)
    conv_rows, gain_rows = 5 * CH // 128, (D + DI) // 128
    conv_sum = lax.dynamic_slice(
        packed[:conv_rows].reshape(5, CH), (0, number * conv_width), (5, conv_width)
    )
    gains_sum = lax.dynamic_slice(
        packed[conv_rows : conv_rows + gain_rows].reshape(-1), (number * gain_width,), (gain_width,)
    )
    head_sum = packed[conv_rows + gain_rows :].reshape(-1)[: 3 * HEADS].reshape(3, HEADS)

    in_grad = jnp.concatenate(
        [gate_sum.astype(f32), rest_sum.astype(f32), shared_sum[:, : 2 * STATE + HEADS]], axis=1
    )
    in_new = adamw_step(in_weight, in_moment, in_square, in_grad, rate_matrix, weight_decay)
    out_new = adamw_step(out_weight, out_moment, out_square, out_grad, rate_matrix, weight_decay)
    conv_new = adamw_step(conv_table, conv_moment, conv_square, conv_sum, rate_vector, 0.0)
    gains_new = adamw_step(norm_gains, gain_moment, gain_square, gains_sum, rate_vector, 0.0)
    head_new = adamw_step(head_table, head_moment, head_square, head_sum, rate_heads, 0.0)
    return (layer_out, tokens_grad, *in_new, *out_new, *conv_new, *gains_new, *head_new)


def solution(mesh):
    tokens = P(("dp", "seq"), None)
    rows = P(("seq", "dp"), None)
    columns = P(None, ("seq", "dp"))
    line = P(("seq", "dp"))
    return jax.shard_map(
        on_device,
        mesh=mesh,
        in_specs=(tokens,) * 2 + (rows,) * 6 + (columns,) * 3 + (line,) * 3 + (P(),) * 3,
        out_specs=(tokens,) * 2 + (rows,) * 6 + (columns,) * 3 + (line,) * 3 + (P(),) * 3,
        check_vma=False,
    )
```

```python
import functools

import jax
import jax.numpy as jnp
from jax import lax
from jax.experimental import pallas as pl
from jax.experimental.pallas import tpu as pltpu
from jax.sharding import PartitionSpec as P

D = 1536
HEADS = 48
HEAD_DIM = 64
STATE = 128
CONV = 4
STEP = 10
DI = 3072
CH = 3328

QUARTERS = 4
QH = HEADS // QUARTERS
QW = DI // QUARTERS
QC = QW + 2 * STATE
WIDE = QC + 128
GC = QW // 2
LEN = 256
ROWS = 1024
HALF = ROWS // 2
BLOCKS = ROWS // LEN

norm_epsilon = 1e-05
adam_epsilon = 1e-08
beta_first = 0.9
beta_second = 0.999
rate_matrix = 0.05
rate_vector = 0.5
rate_heads = 2.0
weight_decay = 0.1
LOG2E = 1.4426950408889634

f32 = jnp.float32
bf16 = jnp.bfloat16
NN = (((1,), (0,)), ((), ()))
NT = (((1,), (1,)), ((), ()))
TN = (((0,), (0,)), ((), ()))
MIB = 1024 * 1024


def mm(a, b, dims=NN):
    return lax.dot_general(a, b, dims, preferred_element_type=f32)


def mm_exact(a, b, dims=NN):
    return lax.dot_general(
        a, b, dims, precision=lax.Precision.HIGHEST, preferred_element_type=f32
    )


def spread_heads(columns, first_head, count):
    rows = columns.shape[0]
    low = lax.broadcasted_iota(jnp.int32, (rows, 128), 1) < HEAD_DIM
    parts = []
    for h in range(first_head, first_head + count, 2):
        first = jnp.broadcast_to(columns[:, h : h + 1], (rows, 128))
        second = jnp.broadcast_to(columns[:, h + 1 : h + 2], (rows, 128))
        parts.append(jnp.where(low, first, second))
    return jnp.concatenate(parts, axis=1)


def softplus(v):
    return jnp.maximum(v, 0.0) + jnp.log1p(jnp.exp(-jnp.abs(v)))


def triangle(lower):
    rows = lax.broadcasted_iota(jnp.int32, (LEN, LEN), 0)
    cols = lax.broadcasted_iota(jnp.int32, (LEN, LEN), 1)
    return rows >= cols if lower else rows <= cols


def halves(pair):
    low = lax.broadcasted_iota(jnp.int32, pair.shape, 1) < HEAD_DIM
    zero = jnp.zeros_like(pair)
    return jnp.where(low, pair, zero), jnp.where(low, zero, pair)


def parts_of(v):
    high = v.astype(bf16)
    return high, (v - high.astype(f32)).astype(bf16)


def affinity_of(first, second):
    both = jnp.concatenate(first, axis=1)
    high = jnp.concatenate([second[0], second[0]], axis=1)
    return mm(both, high, NT) + mm(first[0], second[1], NT)


def packed(v):
    high = v.astype(bf16).astype(f32)
    left = v - high
    middle = left.astype(bf16).astype(f32)
    parts = high + pltpu.roll(middle, 16, 1) + pltpu.roll(left - middle, 32, 1)
    return parts.astype(bf16)


def spread_product(v):
    lane = lax.broadcasted_iota(jnp.int32, v.shape, 1)
    row = lax.broadcasted_iota(jnp.int32, (128, QW), 0)
    column = lax.broadcasted_iota(jnp.int32, (128, QW), 1)
    ones = jnp.where((row % 16 == column // HEAD_DIM) & (row < 48), 1.0, 0.0)
    return mm(packed(jnp.where(lane < QH, v, 0.0)), ones.astype(bf16))


def running(mask, v):
    product = mm(mask.astype(f32).astype(bf16), packed(v))
    return product + pltpu.roll(product, 112, 1) + pltpu.roll(product, 96, 1)


def twice(pair):
    low = lax.broadcasted_iota(jnp.int32, pair.shape, 1) < HEAD_DIM
    turned = pltpu.roll(pair, HEAD_DIM, 1)
    return jnp.where(low, pair, turned).astype(bf16), jnp.where(low, turned, pair).astype(bf16)


def beside_rest(pair, rest):
    low = lax.broadcasted_iota(jnp.int32, pair.shape, 1) < HEAD_DIM
    turned = pltpu.roll(rest, HEAD_DIM, 1).astype(bf16)
    return jnp.where(low, pair, turned), jnp.where(low, turned, pair)


def filter_rows(ext, conv_ref):
    width = ext.shape[1]
    total = conv_ref[CONV : CONV + 1, :width]
    for k in range(CONV):
        total = total + conv_ref[k : k + 1, :width] * ext[5 + k : 5 + k + LEN, :]
    return total


def forward_kernel(
    half, place, near, far, gain, w, conv, head, skip, tail_in, state_in, *rest
):
    normed_out, turned_out, proj_out, filtered_out, scanned_out, mem_out = rest[-10:-4]
    tail_out, state_out, ext, mem = rest[-4:]
    j = pl.program_id(0)

    @pl.when(j == 0)
    def _():
        ext[0:8, :] = tail_in[...]
        mem[...] = state_in[...]

    wide = jnp.where(place[0] == half, near[...], far[...]).astype(f32)
    inv_one = lax.rsqrt(jnp.mean(wide * wide, axis=1, keepdims=True) + norm_epsilon)
    normed = (wide * inv_one * gain[...]).astype(bf16)
    normed_out[...] = normed
    turned_out[...] = normed.T
    proj = mm(normed, w[...])
    proj_out[...] = proj
    ext[8 : 8 + LEN, :] = proj[:, :QC]
    filtered = filter_rows(ext, conv)
    filtered_out[:, :QC] = filtered
    ext[0:8, :] = ext[LEN : LEN + 8, :]
    active = filtered * jax.nn.sigmoid(filtered)
    payload = active[:, :QW]
    writers = parts_of(active[:, QW : QW + STATE])
    readers = parts_of(active[:, QW + STATE :])
    writer = writers[0]

    steps = softplus(pltpu.roll(proj[:, QC:], place[2], 1) + head[1:2, :])
    rates = head[0:1, :] * steps
    causal = triangle(True)
    summed = running(causal, rates) * LOG2E
    across = summed.T
    affinity = jnp.where(causal, affinity_of(readers, writers), 0.0)

    dosed = payload * spread_product(steps)
    dosed_low = dosed.astype(bf16)
    state = mem[...]
    mem_out[0] = state
    summed_wide = spread_heads(summed, 0, QH)
    grown = jnp.exp2(summed_wide)
    state_low, state_rest = parts_of(state)
    carried = mm(jnp.concatenate(readers, axis=1), jnp.concatenate([state_low] * 2, axis=0))
    carried = (carried + mm(readers[0], state_rest)) * grown
    within = []
    for pair in range(QH // 2):
        weights = []
        for h in (2 * pair, 2 * pair + 1):
            gap = jnp.minimum(summed[:, h : h + 1] - across[h : h + 1, :], 0.0)
            weights.append((jnp.exp2(gap) * affinity).astype(bf16))
        first, second = halves(dosed_low[:, 128 * pair : 128 * pair + 128])
        within.append(
            mm(jnp.concatenate(weights, axis=1), jnp.concatenate([first, second], axis=0))
        )
    scanned_out[...] = jnp.concatenate(within, axis=1) + carried + payload * skip[...]

    last = summed[LEN - 1 : LEN, :]
    last_wide = spread_heads(last, 0, QH)
    remain = jnp.exp2(last_wide - summed_wide)
    added = mm(writer, (dosed * remain).astype(bf16), TN)
    mem[...] = state * jnp.exp2(last_wide) + added
    tail_out[...] = ext[0:8, :]
    state_out[...] = mem[...]


def by_core(core, own, other):
    first = core == 0
    return jnp.where(first, own, other), jnp.where(first, other, own)


def at_hand(side, near_a, far_a, near_b, far_b):
    j = pl.program_id(0)
    near = (j % BLOCKS) // (BLOCKS // 2) == side
    first = jnp.where(near, near_a[...], far_a[...])
    return jnp.where(j < BLOCKS, first, jnp.where(near, near_b[...], far_b[...]))


def gate_kernel(
    place, normed, w_gate, cot_na, cot_fa, cot_nb, cot_fb, w_own, w_other, gain, scanned,
    gate_out, shaped_grad_out, stats_out,
):
    gate = mm(normed[...], w_gate[...])
    cot = at_hand(place[0], cot_na, cot_fa, cot_nb, cot_fb)
    left, right = by_core(place[1], w_own[...], w_other[...])
    grad_shaped = mm(cot[:, :QW], left, NT) + mm(cot[:, QW:], right, NT)
    gate_out[...] = gate
    shaped_grad_out[...] = grad_shaped
    gated = scanned[...] * (gate * jax.nn.sigmoid(gate))
    squares = jnp.sum(gated * gated, axis=1, keepdims=True)
    inner = jnp.sum(grad_shaped * gain[...] * gated, axis=1, keepdims=True)
    lane = lax.broadcasted_iota(jnp.int32, (LEN, 128), 1)
    both = jnp.where(lane == 0, squares, jnp.where(lane == 1, inner, 0.0))
    stats_out[...] = both.T[0:8, :]


def finish_kernel(
    place, stats, gate_in, grad_shaped_in, scanned_in, w_own, w_other, gain,
    turned_out, layer_a_out, layer_b_out, scan_grad_out, gate_grad_out, gain_grad,
):
    j = pl.program_id(0)
    table = jnp.concatenate([stats[...], jnp.zeros((120, LEN), f32)], axis=0).T
    inv_two = lax.rsqrt(table[:, 0:1] / DI + norm_epsilon)
    mean = inv_two * table[:, 1:2] / DI
    gate = gate_in[...]
    scanned = scanned_in[...]
    grad_shaped = grad_shaped_in[...]
    sig = jax.nn.sigmoid(gate)
    lift = gate * sig
    unit = scanned * lift * inv_two
    shaped = (unit * gain[...]).astype(bf16)
    turned_out[...] = shaped.T
    left, right = by_core(place[1], w_own[...], w_other[...])
    layer = jnp.concatenate([mm(shaped, left), mm(shaped, right)], axis=1).astype(bf16)

    @pl.when(j < BLOCKS)
    def _():
        layer_a_out[...] = layer

    @pl.when(j >= BLOCKS)
    def _():
        layer_b_out[...] = layer

    grad_gated = inv_two * (grad_shaped * gain[...] - unit * mean)
    scan_grad_out[...] = grad_gated * lift
    gate_grad_out[...] = (grad_gated * scanned * sig * (1.0 + gate * (1.0 - sig))).astype(bf16)

    @pl.when(j == 0)
    def _():
        gain_grad[...] = jnp.zeros_like(gain_grad)

    gain_grad[0:1, :] += jnp.sum(grad_shaped * unit, axis=0, keepdims=True)


def backward_kernel(
    place, proj_in, filtered_in, scanned_in, grad_in, mem_in, conv, head, skip, later_in, state_in,
    *rest
):
    out, conv_grad, head_grad, skip_grad, later_out, state_out, later, grad_mem = rest[-8:]
    i = pl.program_id(0)

    @pl.when(i == 0)
    def _():
        later[LEN : LEN + 8, :] = later_in[...]
        grad_mem[...] = state_in[...]
        conv_grad[...] = jnp.zeros_like(conv_grad)
        head_grad[...] = jnp.zeros_like(head_grad)
        skip_grad[...] = jnp.zeros_like(skip_grad)

    @pl.when(i > 0)
    def _():
        later[LEN : LEN + 8, :] = later[0:8, :]

    conv_in = proj_in[:, :QC]
    filtered = filtered_in[:, :QC]
    sig = jax.nn.sigmoid(filtered)
    active = filtered * sig
    slope = sig * (1.0 + filtered * (1.0 - sig))
    payload = active[:, :QW]
    writers = parts_of(active[:, QW : QW + STATE])
    readers = parts_of(active[:, QW + STATE :])
    writer, reader = writers[0], readers[0]

    raw = pltpu.roll(proj_in[:, QC:], place[2], 1) + head[1:2, :]
    steps = softplus(raw)
    rates = head[0:1, :] * steps
    summed = running(triangle(True), rates) * LOG2E
    across = summed.T
    upper = triangle(False)
    affinity = jnp.where(upper, affinity_of(writers, readers), 0.0)

    grad = grad_in[...]
    grad_low = grad.astype(bf16)
    grad_rest = grad - grad_low.astype(f32)
    dose = spread_product(steps)
    dosed = payload * dose
    dosed_low = dosed.astype(bf16)
    state = mem_in[0]
    state_grad = grad_mem[...]
    state_grad_low = state_grad.astype(bf16)
    last = summed[LEN - 1 : LEN, :]
    last_wide = spread_heads(last, 0, QH)
    summed_wide = spread_heads(summed, 0, QH)
    remain = jnp.exp2(last_wide - summed_wide)
    from_state = mm(writer, state_grad_low) * remain

    mixed = jnp.zeros((LEN, LEN), f32)
    within = []
    for pair in range(QH // 2):
        lanes = slice(128 * pair, 128 * pair + 128)
        grads = halves(grad_low[:, lanes])
        doses = twice(dosed[:, lanes])
        parts = beside_rest(grad_low[:, lanes], grad_rest[:, lanes])
        weights = []
        for n in range(2):
            h = 2 * pair + n
            gap = jnp.minimum(across[h : h + 1, :] - summed[:, h : h + 1], 0.0)
            decay = jnp.exp2(gap)
            weights.append((decay * affinity).astype(bf16))
            mixed = mixed + decay * mm(doses[n], parts[n], NT)
        within.append(mm(jnp.concatenate(weights, axis=1), jnp.concatenate(grads, axis=0)))
    unit = jnp.concatenate(within, axis=1) + from_state

    payload_grad = dose * unit + skip[...] * grad
    core = scanned_in[...] - payload * skip[...]
    dosed_wide = dosed_low.astype(f32)
    balance = grad_low.astype(f32) * core - dosed_wide * unit
    high_part = balance.astype(bf16)
    low_part = (balance - high_part.astype(f32)).astype(bf16)
    decay_last = jnp.exp2(last_wide)
    at_end = jnp.sum(dosed_wide * from_state, axis=0, keepdims=True) + decay_last * jnp.sum(
        state_grad * state, axis=0, keepdims=True
    )
    end_high = at_end.astype(bf16).astype(f32)
    end_middle = (at_end - end_high).astype(bf16).astype(f32)
    row = lax.broadcasted_iota(jnp.int32, (16, QW), 0)
    end_parts = jnp.where(
        row == 0,
        end_high,
        jnp.where(row == 1, end_middle, jnp.where(row == 2, at_end - end_high - end_middle, 0.0)),
    ).astype(bf16)
    heads_of = (
        lax.broadcasted_iota(jnp.int32, (QW, 128), 0) // HEAD_DIM
        == lax.broadcasted_iota(jnp.int32, (QW, 128), 1)
    ).astype(f32)
    by_head = mm(
        jnp.concatenate([high_part, low_part, (payload * unit).astype(bf16), end_parts], axis=0),
        heads_of.astype(bf16),
    )
    balance_sum = by_head[:LEN] + by_head[LEN : 2 * LEN]
    direct = by_head[2 * LEN : 3 * LEN]
    end_sum = jnp.sum(by_head[3 * LEN :], axis=0, keepdims=True)
    rate_grad = running(upper, balance_sum) + end_sum
    step_grad = direct + head[0:1, :] * rate_grad
    raw_grad = step_grad * jax.nn.sigmoid(raw)
    head_grad[0:1, :] += jnp.sum(rate_grad * rates, axis=0, keepdims=True)
    head_grad[1:2, :] += jnp.sum(raw_grad, axis=0, keepdims=True)
    skip_grad[0:1, :] += jnp.sum(grad * payload, axis=0, keepdims=True)

    grown_wide = jnp.exp2(summed_wide) * grad
    grown_grad = grown_wide.astype(bf16)
    grown_rest = (grown_wide - grown_grad.astype(f32)).astype(bf16)
    kept = (remain * dosed).astype(bf16)
    mixed_low = jnp.where(upper, mixed, 0.0).astype(bf16)
    writer_grad = mm(mixed_low, reader) + mm(kept, state_grad_low, NT)
    state_low = state.astype(bf16)
    reader_grad = (
        mm(mixed_low, writer, TN) + mm(grown_grad, state_low, NT) + mm(grown_rest, state_low, NT)
    )
    grad_mem[...] = decay_last * state_grad + mm(reader, grown_grad, TN)

    filtered_grad = jnp.concatenate([payload_grad, writer_grad, reader_grad], axis=1) * slope
    later[0:LEN, :] = filtered_grad
    back = None
    sums = []
    for k in range(CONV):
        ahead = later[CONV - 1 - k : CONV - 1 - k + LEN, :]
        sums.append(jnp.sum(ahead * conv_in, axis=0, keepdims=True))
        term = conv[k : k + 1, :QC] * ahead
        back = term if back is None else back + term
    sums.append(jnp.sum(filtered_grad, axis=0, keepdims=True))
    conv_grad[...] += jnp.concatenate(sums + [jnp.zeros((7 - CONV, QC), f32)], axis=0)
    out[:, :QC] = back.astype(bf16)
    out[:, QC:] = pltpu.roll(raw_grad, place[3], 1).astype(bf16)
    later_out[...] = later[0:8, :]
    state_out[...] = grad_mem[...]


def outer_kernel(left, *rest):
    out = rest[-1]
    total = None
    for n, right in enumerate(rest[:-1]):
        part = mm(left[:, n * HALF : (n + 1) * HALF], right[...])
        total = part if total is None else total + part
    out[...] = total.astype(bf16)


def pieces_kernel(chip_rows, blocks, place, left, right, *rest):
    out, dots = rest[-2:]
    weights, others = rest[:blocks], rest[blocks:-2]
    tile = left.shape[0]
    i = pl.program_id(0)
    per = tile // chip_rows
    steps = out.shape[0] // per
    result = mm(left[...], right[...])
    sums = jnp.zeros((tile, 128), f32)
    for n, weight in enumerate(weights):
        product = result[:, n * GC : (n + 1) * GC] * weight[...].astype(f32)
        sums = sums + (product[:, :128] + product[:, 128:256] + product[:, 256:])
    dots[...] = jnp.broadcast_to(jnp.sum(sums.T, axis=0, keepdims=True), (8, tile))
    for n in range(per):
        part = result[n * chip_rows : (n + 1) * chip_rows].astype(bf16)
        if others:
            out[(i % steps) * per + n, 0, i // steps] = part
        else:
            out[(i % steps) * per + n, i // steps] = part
    if others:
        half = out.shape[0] // 2

        @pl.when(i == 0)
        def _():
            own, other = others
            core = place[1]
            out[pl.ds(core * half, half), 1] = own[...]
            out[pl.ds((1 - core) * half, half), 1] = other[...]


def input_grad(gate_grad, wide_grad, w_gate, w_wide):
    grad = mm(gate_grad[...], w_gate[...], NT) + mm(wide_grad[...], w_wide[...], NT)
    return grad.astype(bf16)


def input_grad_kernel(place, *refs):
    refs[-1][...] = input_grad(*refs[:-1])


def own_first(j, place):
    per = BLOCKS // 2
    half = j // per
    side = place[0]
    return (half + side - 2 * half * side) * per + j % per


def rows_of(width, first=0):
    return pl.BlockSpec((LEN, width), lambda j, *_: (j + first, 0))


def moved_columns(height):
    return pl.BlockSpec(
        (height, LEN),
        lambda j, place: (0, own_first(j % BLOCKS, place) + (j // BLOCKS) * BLOCKS),
    )


def first_rows(width):
    return pl.BlockSpec(
        (LEN, width), lambda j, place: (own_first(jnp.minimum(j, BLOCKS - 1), place), 0)
    )


def second_rows(width):
    return pl.BlockSpec(
        (LEN, width), lambda j, place: (own_first(jnp.maximum(j - BLOCKS, 0), place), 0)
    )


def whole(*shape):
    return pl.BlockSpec(shape, lambda j, *_: (0,) * len(shape))


def params():
    return pltpu.CompilerParams(
        vmem_limit_bytes=60 * MIB, dimension_semantics=("arbitrary",)
    )


def shape(dims, dtype):
    return jax.ShapeDtypeStruct(dims, dtype)


def cost(microseconds):
    return pl.CostEstimate(
        flops=int(microseconds * 1e9),
        bytes_accessed=int(microseconds * 3.5e6),
        transcendentals=0,
    )


def run_forward(place, near, far, gain, w, conv, head, skip, carried, buffers, part):
    per = BLOCKS // 2
    first = part * per
    if buffers is None:
        buffers = ()
    anywhere = pl.BlockSpec(memory_space=pl.ANY)
    return pl.pallas_call(
        functools.partial(forward_kernel, part % 2),
        grid_spec=pltpu.PrefetchScalarGridSpec(
            num_scalar_prefetch=1,
            grid=(per,),
            in_specs=[
                rows_of(D), rows_of(D), whole(1, D), whole(D, WIDE), whole(8, WIDE), whole(8, 128), whole(1, QW),
                whole(8, QC), whole(STATE, QW),
            ] + [anywhere] * len(buffers),
            out_specs=[
                rows_of(D, first), pl.BlockSpec((D, LEN), lambda j, *_: (0, j + first)),
                rows_of(WIDE, first), rows_of(WIDE, first), rows_of(QW, first),
                pl.BlockSpec((1, STATE, QW), lambda j, *_: (j + first, 0, 0)),
                whole(8, QC), whole(STATE, QW),
            ],
            scratch_shapes=[pltpu.VMEM((LEN + 8, QC), f32), pltpu.VMEM((STATE, QW), f32)],
        ),
        out_shape=[
            shape((2 * ROWS, D), bf16), shape((D, 2 * ROWS), bf16),
            shape((2 * ROWS, WIDE), f32), shape((2 * ROWS, WIDE), f32),
            shape((2 * ROWS, QW), f32), shape((2 * BLOCKS, STATE, QW), f32), shape((8, QC), f32), shape((STATE, QW), f32),
        ],
        input_output_aliases={10 + n: n for n in range(len(buffers))},
        compiler_params=params(),
        cost_estimate=cost(13),
        name="forward_scan",
    )(place, near, far, gain, w, conv, head, skip, *carried, *buffers)


def assemble_kernel(count, place, *refs):
    pieces, (gate, own, send) = refs[:count], refs[count:]
    half = count // 2
    for n, piece in enumerate(pieces):
        chip = place[4 + n]
        gate[0, chip] = piece[0, 0]
        gate[1, chip] = piece[0, 1]
        mine = chip // half == place[1]

        @pl.when(mine)
        def _():
            own[chip % half] = piece[1]

        @pl.when(jnp.logical_not(mine))
        def _():
            send[chip % half] = piece[1]


def run_assemble(place, pieces):
    count = len(pieces)
    _, _, rows, width = pieces[0].shape
    outs = [(2, count, rows, width)] + [(count // 2, 2, rows, width)] * 2
    return pl.pallas_call(
        functools.partial(assemble_kernel, count),
        grid_spec=pltpu.PrefetchScalarGridSpec(
            num_scalar_prefetch=1,
            grid=(1,),
            in_specs=[whole(2, 2, rows, width)] * count,
            out_specs=[whole(*dims) for dims in outs],
        ),
        out_shape=[shape(dims, bf16) for dims in outs],
        compiler_params=params(),
        cost_estimate=cost(3),
        name="assemble",
    )(place, *pieces)


def run_gate(place, normed, w_gate, cots, w_out, gain, scanned):
    per = BLOCKS // 2

    def half(sequence, far):
        def index(j, place):
            first = sequence * BLOCKS + (1 - place[0] if far else place[0]) * per
            return (jnp.clip(j - first, 0, per - 1), 0)

        return pl.BlockSpec((LEN, D), index)

    return pl.pallas_call(
        gate_kernel,
        grid_spec=pltpu.PrefetchScalarGridSpec(
            num_scalar_prefetch=1,
            grid=(2 * BLOCKS,),
            in_specs=[
                rows_of(D), whole(D, QW), half(0, False), half(0, True), half(1, False),
                half(1, True), whole(QW, QW), whole(QW, QW), whole(1, QW), rows_of(QW),
            ],
            out_specs=[
                rows_of(QW), rows_of(QW), pl.BlockSpec((8, LEN), lambda j, *_: (0, j)),
            ],
        ),
        out_shape=[
            shape((2 * ROWS, QW), f32), shape((2 * ROWS, QW), f32), shape((8, 2 * ROWS), f32),
        ],
        compiler_params=params(),
        cost_estimate=cost(2),
        name="gate_and_stats",
    )(place, normed, w_gate, *cots, *w_out, gain, scanned)


def run_finish(place, stats, gate, grad_shaped, scanned, w_out, gain):
    return pl.pallas_call(
        finish_kernel,
        grid_spec=pltpu.PrefetchScalarGridSpec(
            num_scalar_prefetch=1,
            grid=(2 * BLOCKS,),
            in_specs=[
                pl.BlockSpec((8, LEN), lambda j, *_: (0, j)), rows_of(QW), rows_of(QW),
                rows_of(QW), whole(QW, QW), whole(QW, QW), whole(1, QW),
            ],
            out_specs=[
                moved_columns(QW), first_rows(D), second_rows(D), rows_of(QW), rows_of(QW),
                whole(8, QW),
            ],
        ),
        out_shape=[
            shape((QW, 2 * ROWS), bf16), shape((ROWS, D), bf16), shape((ROWS, D), bf16),
            shape((2 * ROWS, QW), f32), shape((2 * ROWS, QW), bf16), shape((8, QW), f32),
        ],
        compiler_params=params(),
        cost_estimate=cost(2),
        name="finish",
    )(place, stats, gate, grad_shaped, scanned, *w_out, gain)


def run_backward(
    place, sequence, half, proj, filtered, scanned, grad, mem, conv, head, skip, carried, buffers
):
    per = BLOCKS // 2
    top = sequence * BLOCKS + (half + 1) * per - 1

    def back(width):
        return pl.BlockSpec((LEN, width), lambda i, *_: (top - i, 0))

    args = [place, proj, filtered, scanned, grad, mem, conv, head, skip, *carried]
    return pl.pallas_call(
        backward_kernel,
        grid_spec=pltpu.PrefetchScalarGridSpec(
            num_scalar_prefetch=1,
            grid=(per,),
            in_specs=[
                back(WIDE), back(WIDE), back(QW), back(QW),
                pl.BlockSpec((1, STATE, QW), lambda i, *_: (top - i, 0, 0)),
                whole(8, WIDE), whole(8, 128), whole(1, QW), whole(8, QC), whole(STATE, QW),
            ] + [pl.BlockSpec(memory_space=pl.ANY)] * len(buffers),
            out_specs=[
                back(WIDE), whole(8, QC), whole(8, 128), whole(8, QW), whole(8, QC),
                whole(STATE, QW),
            ],
            scratch_shapes=[pltpu.VMEM((LEN + 8, QC), f32), pltpu.VMEM((STATE, QW), f32)],
        ),
        out_shape=[
            shape((2 * ROWS, WIDE), bf16), shape((8, QC), f32), shape((8, 128), f32),
            shape((8, QW), f32), shape((8, QC), f32), shape((STATE, QW), f32),
        ],
        input_output_aliases={len(args) + n: n for n in range(len(buffers))},
        compiler_params=params(),
        cost_estimate=cost(2),
        name="backward_scan",
    )(*args, *buffers)


def run_outer(left, rights):
    tall, width = left.shape[0], rights[0].shape[1]
    tile = 384
    return pl.pallas_call(
        outer_kernel,
        grid=(tall // tile,),
        in_specs=[pl.BlockSpec((tile, 2 * ROWS), lambda i: (i, 0))]
        + [whole(HALF, width) for _ in rights],
        out_specs=pl.BlockSpec((tile, width), lambda i: (i, 0)),
        out_shape=shape((tall, width), bf16),
        compiler_params=params(),
        cost_estimate=cost(1),
        name="weight_grad",
    )(left, *rights)


def run_pieces(place, left, right, chips, weights, columns, others=()):
    tall, width = left.shape[0], right.shape[1]
    tile = 384
    chip_rows = tall // (2 * chips)
    dims = (chips,) + (2,) * (2 if others else 1) + (chip_rows, width)

    def block(column):
        return pl.BlockSpec((tile, GC), lambda i, *_: (i, column))

    beside_specs = []
    if others:
        part = others[1].shape
        beside_specs = [
            pl.BlockSpec(part, lambda i, place: (0, 0, 0, place[1])),
            whole(*part),
        ]
    return pl.pallas_call(
        functools.partial(pieces_kernel, chip_rows, len(columns)),
        grid_spec=pltpu.PrefetchScalarGridSpec(
            num_scalar_prefetch=1,
            grid=(tall // tile,),
            in_specs=[
                pl.BlockSpec((tile, 2 * ROWS), lambda i, *_: (i, 0)), whole(*right.shape),
            ] + [block(column) for column in columns] + beside_specs,
            out_specs=[whole(*dims), pl.BlockSpec((8, tile), lambda i, *_: (0, i))],
        ),
        out_shape=[shape(dims, bf16), shape((8, tall), f32)],
        compiler_params=params(),
        cost_estimate=cost(1),
        name="weight_grad",
    )(place, left, right, *([weights] * len(columns)), *others)


def tokens_grad_kernel(tok, cot, gain, near, core, *rest):
    sides, out = rest[:-1], rest[-1]
    i = pl.program_id(0)
    rows = out.shape[0]
    parts = [ref[n : n + rows, :] for ref in sides for n in range(0, ref.shape[0], rows)]
    side = parts[0]
    for n in range(1, len(parts)):
        side = jnp.where(i == n, parts[n], side)
    grad = near[...].astype(f32) + core[...].astype(f32) + side.astype(f32)
    wide = tok[...].astype(f32)
    inv_one = lax.rsqrt(jnp.mean(wide * wide, axis=1, keepdims=True) + norm_epsilon)
    unit = wide * inv_one
    lifted = grad * gain[...]
    mean = jnp.mean(lifted * unit, axis=1, keepdims=True)
    out[...] = cot[...].astype(f32) + inv_one * (lifted - unit * mean)


def run_tokens_grad(tokens, cotangent, gain, near, core, sides):
    rows = min(part.shape[0] for part in sides)
    block = pl.BlockSpec((rows, D), lambda i: (i, 0))
    return pl.pallas_call(
        tokens_grad_kernel,
        grid=(HALF // rows,),
        in_specs=[block, block, whole(1, D), block, block]
        + [whole(*part.shape) for part in sides],
        out_specs=block,
        out_shape=shape((HALF, D), f32),
        compiler_params=params(),
        cost_estimate=cost(4),
        name="tokens_grad",
    )(tokens, cotangent, gain, near, core, *sides)


def run_input_grad(place, sequence, far, gate_grad, wide_grad, w_gate, w_wide):
    per = BLOCKS // 2

    def rows(width):
        def index(j, place):
            half = 1 - place[0] if far else place[0]
            return (sequence * BLOCKS + half * per + j, 0)

        return pl.BlockSpec((LEN, width), index)

    return pl.pallas_call(
        input_grad_kernel,
        grid_spec=pltpu.PrefetchScalarGridSpec(
            num_scalar_prefetch=1,
            grid=(per,),
            in_specs=[rows(QW), rows(WIDE), whole(D, QW), whole(D, WIDE)],
            out_specs=rows_of(D),
        ),
        out_shape=shape((HALF, D), bf16),
        compiler_params=params(),
        cost_estimate=cost(1),
        name="input_grad",
    )(place, gate_grad, wide_grad, w_gate, w_wide)


def other_side(block):
    return lax.ppermute(block, "seq", [(0, 1), (1, 0)])


def after(block, *others):
    return lax.optimization_barrier((block, *others))[0]


def tie(*blocks):
    return lax.optimization_barrier(blocks)


def flip(block, bit):
    count = lax.axis_size("dp")
    return lax.ppermute(block, "dp", [(d, d ^ bit) for d in range(count)])


def other_core(block):
    return flip(block, 1)


def beside(block):
    return flip(block, 2)


def along(block):
    count = lax.axis_size("dp")
    return lax.ppermute(block, "dp", [(d, (d + 4) % count) for d in range(count)])


def in_order(place, own, received, axis=0):
    return jnp.where(
        place == 0,
        jnp.concatenate([own, received], axis=axis),
        jnp.concatenate([received, own], axis=axis),
    )


def pick(block, place, axis):
    return lax.dynamic_index_in_dim(block, place, axis, False)


class Spread:
    def __init__(self, piece, groups, put, base, hold=()):
        dp = lax.axis_index("dp")
        self.ring, self.beside_place = dp // 4, (dp // 2) % 2
        self.groups, self.put, self.base = groups, put, base
        self.hop, self.current = 0, piece
        self.neighbour = beside(after(piece, *hold) if hold else piece)

    def place(self, hold=()):
        origin = (self.ring + self.groups - self.hop) % self.groups
        current, neighbour = self.current, self.neighbour
        if hold:
            current, neighbour, *_ = tie(current, neighbour, *hold)
        self.base = self.put(self.base, current, 2 * origin + self.beside_place)
        self.base = self.put(self.base, neighbour, 2 * origin + 1 - self.beside_place)

    def step(self, hold=(), place_hold=()):
        moved = along(self.current)
        if hold:
            moved = after(moved, *hold)
        self.place(place_hold)
        self.hop, self.current, self.neighbour = self.hop + 1, moved, beside(moved)
        return moved


class Collect:
    def __init__(self, block_of, groups):
        dp = lax.axis_index("dp")
        self.ring, self.beside_place = dp // 4, (dp // 2) % 2
        self.block_of, self.groups = block_of, groups
        self.hop, self.total = 0, None
        self.first = self.block(1 - self.beside_place)
        self.received = beside(self.first)

    def block(self, place):
        target = (self.ring + 2 * self.groups - 1 - self.hop) % self.groups
        return self.block_of(2 * target + place)

    def step(self, *hold):
        received = after(self.received, *hold) if hold else self.received
        part = self.block(self.beside_place).astype(f32) + received.astype(f32)
        if self.hop:
            part = part + self.total.astype(f32)
        part = part.astype(bf16)
        self.hop += 1
        if self.hop < self.groups:
            part, following = tie(part, self.block(1 - self.beside_place))
            self.total = along(part)
            self.received = beside(following)
        return part

    def rest(self):
        part = None
        while self.hop < self.groups:
            part = self.step()
        return part


def gather_small(row, hold, later):
    dp = lax.axis_index("dp")
    block = row.reshape((1, 1) + row.shape)
    block = hold(in_order(lax.axis_index("seq"), block, other_side(block), axis=0))
    bit = 1
    while bit < lax.axis_size("dp"):
        received = flip(block, bit)
        if bit in later:
            received = after(received, later[bit])
        block = in_order((dp // bit) % 2, block, received, axis=1)
        bit *= 2
    return block.reshape((-1,) + row.shape)


def sum_small(block, bit, hold):
    while bit < lax.axis_size("dp"):
        block = block + after(flip(block, bit), hold)
        bit *= 2
    return block


def columns_of(block, half):
    return lax.dynamic_slice(block, (0, half * QW), (block.shape[0], QW))


def adamw_step(weight, moment, square, gradient, step_rate, decay_rate):
    moment_new = beta_first * moment + (1.0 - beta_first) * gradient
    square_new = beta_second * square + (1.0 - beta_second) * gradient * gradient
    first_fix = moment_new / (1.0 - beta_first**STEP)
    second_fix = square_new / (1.0 - beta_second**STEP)
    weight_new = weight - step_rate * (
        first_fix / (jnp.sqrt(second_fix) + adam_epsilon) + decay_rate * weight
    )
    return (weight_new, moment_new, square_new)


def to_side(halves_of, side):
    return in_order(side, halves_of(side)[None], other_side(halves_of(1 - side))[None])


def to_core(pair, quarter_of, core):
    return in_order(
        core, quarter_of(pair, core)[:, None], other_core(quarter_of(pair, 1 - core))[:, None], 1
    )


def from_cores(piece, core):
    return in_order(core, pick(piece, core, 1), other_core(pick(piece, 1 - core, 1)), 2)


def from_sides(cores, side, *hold):
    received = after(other_side(pick(cores, 1 - side, 0)), *hold)
    return in_order(side, pick(cores, side, 0), received, 1)


def from_cores_shared(piece, core):
    mine, got = pick(piece, core, 1), other_core(pick(piece, 1 - core, 1))
    cores = in_order(core, mine[:, :, :QW], got[:, :, :QW], 2)
    shared = (mine[:, :, QW:].astype(f32) + got[:, :, QW:].astype(f32)).astype(bf16)
    return jnp.concatenate([cores, shared], axis=2)


def from_sides_shared(both, side):
    mine, got = pick(both, side, 0), other_side(pick(both, 1 - side, 0))
    sides = in_order(side, mine[:, : 2 * QW], got[:, : 2 * QW], 1)
    return sides, mine[:, 2 * QW :].astype(f32) + got[:, 2 * QW :].astype(f32)


def on_device(
    tokens,
    cotangent,
    in_weight,
    in_moment,
    in_square,
    out_weight,
    out_moment,
    out_square,
    conv_table,
    conv_moment,
    conv_square,
    norm_gains,
    gain_moment,
    gain_square,
    head_table,
    head_moment,
    head_square,
):
    side = lax.axis_index("seq")
    dp = lax.axis_index("dp")
    core = dp % 2
    groups = lax.axis_size("dp") // 4
    chips = 2 * groups
    quarter = 2 * side + core
    number = side * lax.axis_size("dp") + dp
    turn = quarter * QH
    place = jnp.stack([side, core, 128 - turn, turn]).astype(jnp.int32)
    in_rows, out_rows = in_weight.shape[0], out_weight.shape[0]
    chip_rows = 2 * in_rows

    low = in_weight.astype(bf16)
    shared_own = jnp.pad(low[:, 2 * DI :], ((0, 0), (0, GC - 2 * STATE - HEADS)))

    def wide_half(side):
        own = lax.dynamic_slice(low, (0, DI + side * 2 * QW), (in_rows, 2 * QW))
        return jnp.concatenate([own, shared_own], axis=1)

    def wide_quarter(pair, core):
        own = lax.dynamic_slice(pair, (0, 0, core * QW), (2, in_rows, QW))
        return jnp.concatenate([own, pair[:, :, 2 * QW :]], axis=2)

    def gate_half(side):
        return lax.dynamic_slice(low, (0, side * 2 * QW), (in_rows, 2 * QW))

    def gate_quarter(pair, core):
        return lax.dynamic_slice(pair, (0, 0, core * QW), (2, in_rows, QW))

    wide_pair = to_side(wide_half, side)
    low, wide_pair = tie(low, wide_pair)
    gate_pair = to_side(gate_half, side)
    wide_piece = to_core(wide_pair, wide_quarter, core).reshape(2, chip_rows, WIDE)
    gate_piece = to_core(gate_pair, gate_quarter, core).reshape(4 * in_rows, QW)

    def put_in(base, piece, chip):
        return lax.dynamic_update_slice(base, piece[:, None], (0, chip, 0, 0))

    wide_spread = Spread(
        wide_piece, groups, put_in, jnp.zeros((2, chips, chip_rows, WIDE), bf16)
    )

    conv_width, gain_width = conv_table.shape[1], norm_gains.shape[0]
    small_size = 5 * conv_width + gain_width
    small_pad = -(-small_size // 128) * 128
    small_row = jnp.concatenate(
        [conv_table.astype(bf16).reshape(-1), norm_gains.astype(bf16)]
    )
    wide_hops = [wide_spread.step() for _ in range(groups - 1)]
    small_all = gather_small(
        jnp.pad(small_row, (0, small_pad - small_size)),
        lambda block: after(block, wide_hops[0]),
        {4: wide_hops[1]},
    )
    small_all = after(small_all, wide_hops[-1])
    devices = small_all.shape[0]
    conv_full = small_all[:, : 5 * conv_width].reshape(devices, 5, conv_width)
    conv_full = conv_full.transpose(1, 0, 2).reshape(5, CH).astype(f32)
    gains_full = small_all[:, 5 * conv_width : small_size].reshape(1, D + DI).astype(f32)
    first_gain = gains_full[:, :D]
    second_gain = lax.dynamic_slice(gains_full, (0, D + quarter * QW), (1, QW))
    conv_own = jnp.concatenate(
        [lax.dynamic_slice(conv_full, (0, quarter * QW), (5, QW)), conv_full[:, DI:]], axis=1
    )
    conv_own = jnp.pad(conv_own, ((0, 3), (0, WIDE - QC)))
    head_own = lax.dynamic_slice(head_table, (0, quarter * QH), (3, QH))
    head_rows = jnp.concatenate([-jnp.exp(head_own[0:1]), head_own[1:2]], axis=0)
    head_rows = jnp.pad(head_rows, ((0, 6), (0, 128 - QH)))
    skip = jnp.repeat(head_own[2:3], HEAD_DIM, axis=1)

    small = (first_gain, second_gain, conv_own, head_rows, skip)
    wide_spread.place()
    w_wide = wide_spread.base.reshape(D, WIDE)

    tokens_sent, gate_piece = tie(tokens, gate_piece)
    tok_far = other_side(tokens_sent)
    cotangent_sent, tok_far = tie(cotangent, tok_far)
    tok_near_b, tok_far_b = other_core(tokens), other_core(tok_far)

    out_low = out_weight.astype(bf16)
    out_piece = in_order(
        core, columns_of(out_low, core), other_core(columns_of(out_low, 1 - core))
    )
    both_piece = jnp.stack([gate_piece, out_piece]).reshape(2, 2, chip_rows, QW)
    both_piece = after(both_piece, wide_hops[-1])

    def keep(base, piece, chip):
        return base + [(piece, chip)]

    both_spread = Spread(both_piece, groups, keep, [], (w_wide,))
    cot_far = other_side(cotangent_sent)
    cots = (cotangent, cot_far, other_core(cotangent), other_core(cot_far))

    start = (jnp.zeros((8, QC), f32), jnp.zeros((STATE, QW), f32))
    buffers, carried = None, start
    gain = first_gain
    for part in range(4):
        near, far = (tok_near_b, tok_far_b) if part >= 2 else (tokens, tok_far)
        *buffers, tail, state = run_forward(
            place, near, far, gain, w_wide, conv_own, head_rows, skip,
            carried if part % 2 else start, buffers, part,
        )
        carried = (tail, state)
        if both_spread.hop < groups - 1:
            moved = both_spread.step((buffers[0],), (buffers[0],))
            waits = [piece for piece, _ in both_spread.base[-2:]]
            gain = after(first_gain, moved, *waits)
    while both_spread.hop < groups - 1:
        both_spread.step()
    both_spread.place((buffers[0],))
    pieces, origins = zip(*both_spread.base)
    w_gate, w_own, w_send = run_assemble(
        jnp.concatenate([place, jnp.stack(origins).astype(jnp.int32)]), pieces
    )
    w_gate = w_gate.reshape(D, QW)
    w_out = (w_own.reshape(QW, QW), other_core(w_send).reshape(QW, QW))
    normed, normed_turned, proj, filtered, scanned, mem = buffers
    gate, grad_shaped, stats = run_gate(
        place, normed, w_gate, cots, w_out, second_gain, scanned
    )
    stats = stats + other_side(stats)
    swapped = other_core(stats)
    stats = stats + jnp.concatenate([swapped[:, ROWS:], swapped[:, :ROWS]], axis=1)
    shaped_turned, layer_a, layer_b, scan_grad, gate_grad, gain_grad = run_finish(
        place, stats, gate, grad_shaped, scanned, w_out, second_gain
    )

    layer_far = other_core(layer_b)
    out_grad = run_outer(shaped_turned, cots)
    layer_far, out_grad = tie(layer_far, out_grad)
    layer_send = (layer_a[HALF:].astype(f32) + layer_far[HALF:].astype(f32)).astype(bf16)
    layer_side = other_side(layer_send)

    split = (chips // 2, 2, chip_rows)
    out_far = other_core(columns_of(out_grad, 1 - core)).reshape(*split, QW)
    out_pieces = (out_grad.reshape(*split, D), out_far)
    both_pieces, gate_dots = run_pieces(
        place, normed_turned, after(gate_grad, layer_send), chips, w_gate, (0, 1), out_pieces
    )

    def blocks_of(pieces):
        return lambda chip: pick(pieces, chip, 0)

    both_sums = Collect(blocks_of(both_pieces), groups)

    waits = (both_pieces,)
    buffers, sums = (), []
    for sequence in (1, 0):
        carried = start
        for half in (1, 0):
            wide_grad, *part_sums, later, state = run_backward(
                place, sequence, half, proj, filtered, scanned, after(scan_grad, *waits), mem,
                conv_own, head_rows, skip, carried, buffers,
            )
            buffers, carried = (wide_grad,), (later, state)
            sums.append(part_sums)
            both_sum = both_sums.step(part_sums[0])
            waits = (both_sum,)
            if len(sums) == 2:
                waits = (both_sum, layer_side)
    both_sum = both_sums.rest() if groups > 4 else both_sum
    conv_grad, head_grad, skip_grad = (sum(parts[1:], parts[0]) for parts in zip(*sums))
    rest_pieces, rest_dots = run_pieces(
        place, normed_turned, after(wide_grad, both_sum), chips, w_wide, (0, 1, 2)
    )
    rest_sums = Collect(blocks_of(rest_pieces), groups)
    both_sum, wide_grad = tie(both_sum, wide_grad)
    gate_cores = from_cores(both_sum[0].reshape(2, 2, in_rows, QW), core)
    out_rows_sum = both_sum[1].reshape(2, out_rows, QW)
    out_rows_far = other_core(pick(out_rows_sum, 1 - core, 0))

    skip_grad = skip_grad[0].reshape(QH, HEAD_DIM).sum(axis=1)
    conv_all = jnp.concatenate(
        [
            lax.dynamic_update_slice(
                jnp.zeros((5, DI), f32), conv_grad[:5, :QW], (0, quarter * QW)
            ),
            conv_grad[:5, QW:],
        ],
        axis=1,
    )
    gains_all = jnp.concatenate(
        [
            (gate_dots + rest_dots)[0:1] / first_gain,
            lax.dynamic_update_slice(jnp.zeros((1, DI), f32), gain_grad[0:1], (0, quarter * QW)),
        ],
        axis=1,
    )
    heads_all = lax.dynamic_update_slice(
        jnp.zeros((3, HEADS), f32),
        jnp.concatenate([head_grad[0:2, :QH], skip_grad[None]], axis=0),
        (0, quarter * QH),
    )
    packed = jnp.concatenate(
        [
            conv_all.reshape(-1, 128),
            gains_all.reshape(-1, 128),
            jnp.pad(heads_all.reshape(-1), (0, 256 - 3 * HEADS)).reshape(2, 128),
        ],
        axis=0,
    )

    def input_rows(sequence, far, *waits):
        return run_input_grad(
            place, sequence, far, gate_grad, after(wide_grad, *waits), w_gate, w_wide
        )

    far_b = input_rows(1, True, rest_sums.first, packed, gate_cores, out_rows_far)
    far_core = other_core(far_b)
    packed = packed + after(other_side(packed), far_b)
    far_a = input_rows(0, True, packed)
    rest_sum = rest_sums.step(far_a)
    gate_sum = from_sides(gate_cores, side, rest_sum)
    packed = packed + after(other_core(packed), far_a)
    grad_send = (far_a.astype(f32) + far_core.astype(f32)).astype(bf16)
    near_b = input_rows(1, False, rest_sum, grad_send, packed, gate_sum)
    part = HALF // 4
    sides = [other_side(grad_send[:part])]
    near_core = other_core(near_b)
    sides[0], near_b = tie(sides[0], near_b)
    rest_sum = rest_sums.step(sides[0])
    near_a = input_rows(0, False, rest_sum)
    sides.append(other_side(grad_send[part : 2 * part]))
    sides.append(other_side(grad_send[2 * part : 3 * part]))
    sides[1], near_a = tie(sides[1], near_a)
    rest_sum = rest_sums.step(sides[1])
    out_rows_sum = after(out_rows_sum, rest_sum)
    layer_side = after(layer_side, rest_sum)
    layer_out = (
        tokens.astype(f32) + layer_a[:HALF].astype(f32) + layer_far[:HALF].astype(f32)
    ) + layer_side.astype(f32)
    sides[2], rest_sum, layer_out = tie(sides[2], rest_sum, layer_out)
    rest_sum = rest_sums.step(sides[2])
    if rest_sums.hop < groups:
        rest_sum = rest_sums.rest()
    sides.append(other_side(grad_send[3 * part :]))
    out_grad = in_order(core, pick(out_rows_sum, core, 0), out_rows_far, axis=1).astype(f32)

    both_group, rest_sum = tie(
        from_cores_shared(rest_sum.reshape(2, 2, in_rows, WIDE), core), rest_sum
    )
    packed = after(packed, rest_sum)
    packed = packed + after(flip(packed, 2), both_group)
    rest_sum, shared_sum = from_sides_shared(both_group, side)
    packed = packed + after(flip(packed, 4), rest_sum)
    tokens_grad = run_tokens_grad(
        tokens, cotangent, after(first_gain, rest_sum), near_a, near_core, sides
    )
    packed = sum_small(packed, 8, tokens_grad)
    conv_rows, gain_rows = 5 * CH // 128, (D + DI) // 128
    conv_sum = lax.dynamic_slice(
        packed[:conv_rows].reshape(5, CH), (0, number * conv_width), (5, conv_width)
    )
    gains_sum = lax.dynamic_slice(
        packed[conv_rows : conv_rows + gain_rows].reshape(-1), (number * gain_width,), (gain_width,)
    )
    head_sum = packed[conv_rows + gain_rows :].reshape(-1)[: 3 * HEADS].reshape(3, HEADS)

    in_grad = jnp.concatenate(
        [gate_sum.astype(f32), rest_sum.astype(f32), shared_sum[:, : 2 * STATE + HEADS]], axis=1
    )
    in_new = adamw_step(in_weight, in_moment, in_square, in_grad, rate_matrix, weight_decay)
    out_new = adamw_step(out_weight, out_moment, out_square, out_grad, rate_matrix, weight_decay)
    conv_new = adamw_step(conv_table, conv_moment, conv_square, conv_sum, rate_vector, 0.0)
    gains_new = adamw_step(norm_gains, gain_moment, gain_square, gains_sum, rate_vector, 0.0)
    head_new = adamw_step(head_table, head_moment, head_square, head_sum, rate_heads, 0.0)
    return (layer_out, tokens_grad, *in_new, *out_new, *conv_new, *gains_new, *head_new)


def solution(mesh):
    tokens = P(("dp", "seq"), None)
    rows = P(("seq", "dp"), None)
    columns = P(None, ("seq", "dp"))
    line = P(("seq", "dp"))
    return jax.shard_map(
        on_device,
        mesh=mesh,
        in_specs=(tokens,) * 2 + (rows,) * 6 + (columns,) * 3 + (line,) * 3 + (P(),) * 3,
        out_specs=(tokens,) * 2 + (rows,) * 6 + (columns,) * 3 + (line,) * 3 + (P(),) * 3,
        check_vma=False,
    )
```

```python
import functools

import jax
import jax.numpy as jnp
from jax import lax
from jax.experimental import pallas as pl
from jax.experimental.pallas import tpu as pltpu
from jax.sharding import PartitionSpec as P

D = 1536
HEADS = 48
HEAD_DIM = 64
STATE = 128
CONV = 4
STEP = 10
DI = 3072
CH = 3328

QUARTERS = 4
QH = HEADS // QUARTERS
QW = DI // QUARTERS
QC = QW + 2 * STATE
WIDE = QC + 128
GC = QW // 2
LEN = 256
ROWS = 1024
HALF = ROWS // 2
BLOCKS = ROWS // LEN

norm_epsilon = 1e-05
adam_epsilon = 1e-08
beta_first = 0.9
beta_second = 0.999
rate_matrix = 0.05
rate_vector = 0.5
rate_heads = 2.0
weight_decay = 0.1
LOG2E = 1.4426950408889634

f32 = jnp.float32
bf16 = jnp.bfloat16
NN = (((1,), (0,)), ((), ()))
NT = (((1,), (1,)), ((), ()))
TN = (((0,), (0,)), ((), ()))
MIB = 1024 * 1024


def mm(a, b, dims=NN):
    return lax.dot_general(a, b, dims, preferred_element_type=f32)


def mm_exact(a, b, dims=NN):
    return lax.dot_general(
        a, b, dims, precision=lax.Precision.HIGHEST, preferred_element_type=f32
    )


def spread_heads(columns, first_head, count):
    rows = columns.shape[0]
    low = lax.broadcasted_iota(jnp.int32, (rows, 128), 1) < HEAD_DIM
    parts = []
    for h in range(first_head, first_head + count, 2):
        first = jnp.broadcast_to(columns[:, h : h + 1], (rows, 128))
        second = jnp.broadcast_to(columns[:, h + 1 : h + 2], (rows, 128))
        parts.append(jnp.where(low, first, second))
    return jnp.concatenate(parts, axis=1)


def softplus(v):
    return jnp.maximum(v, 0.0) + jnp.log1p(jnp.exp(-jnp.abs(v)))


def triangle(lower):
    rows = lax.broadcasted_iota(jnp.int32, (LEN, LEN), 0)
    cols = lax.broadcasted_iota(jnp.int32, (LEN, LEN), 1)
    return rows >= cols if lower else rows <= cols


def halves(pair):
    low = lax.broadcasted_iota(jnp.int32, pair.shape, 1) < HEAD_DIM
    zero = jnp.zeros_like(pair)
    return jnp.where(low, pair, zero), jnp.where(low, zero, pair)


def parts_of(v):
    high = v.astype(bf16)
    return high, (v - high.astype(f32)).astype(bf16)


def affinity_of(first, second):
    both = jnp.concatenate(first, axis=1)
    high = jnp.concatenate([second[0], second[0]], axis=1)
    return mm(both, high, NT) + mm(first[0], second[1], NT)


def packed(v):
    high = v.astype(bf16).astype(f32)
    left = v - high
    middle = left.astype(bf16).astype(f32)
    parts = high + pltpu.roll(middle, 16, 1) + pltpu.roll(left - middle, 32, 1)
    return parts.astype(bf16)


def spread_product(v):
    lane = lax.broadcasted_iota(jnp.int32, v.shape, 1)
    row = lax.broadcasted_iota(jnp.int32, (128, QW), 0)
    column = lax.broadcasted_iota(jnp.int32, (128, QW), 1)
    ones = jnp.where((row % 16 == column // HEAD_DIM) & (row < 48), 1.0, 0.0)
    return mm(packed(jnp.where(lane < QH, v, 0.0)), ones.astype(bf16))


def running(mask, v):
    product = mm(mask.astype(f32).astype(bf16), packed(v))
    return product + pltpu.roll(product, 112, 1) + pltpu.roll(product, 96, 1)


def twice(pair):
    low = lax.broadcasted_iota(jnp.int32, pair.shape, 1) < HEAD_DIM
    turned = pltpu.roll(pair, HEAD_DIM, 1)
    return jnp.where(low, pair, turned).astype(bf16), jnp.where(low, turned, pair).astype(bf16)


def beside_rest(pair, rest):
    low = lax.broadcasted_iota(jnp.int32, pair.shape, 1) < HEAD_DIM
    turned = pltpu.roll(rest, HEAD_DIM, 1).astype(bf16)
    return jnp.where(low, pair, turned), jnp.where(low, turned, pair)


def filter_rows(ext, conv_ref):
    width = ext.shape[1]
    total = conv_ref[CONV : CONV + 1, :width]
    for k in range(CONV):
        total = total + conv_ref[k : k + 1, :width] * ext[5 + k : 5 + k + LEN, :]
    return total


def forward_kernel(
    half, place, near, far, gain, w, conv, head, skip, tail_in, state_in, *rest
):
    normed_out, turned_out, proj_out, filtered_out, scanned_out, mem_out = rest[-10:-4]
    tail_out, state_out, ext, mem = rest[-4:]
    j = pl.program_id(0)

    @pl.when(j == 0)
    def _():
        ext[0:8, :] = tail_in[...]
        mem[...] = state_in[...]

    wide = jnp.where(place[0] == half, near[...], far[...]).astype(f32)
    inv_one = lax.rsqrt(jnp.mean(wide * wide, axis=1, keepdims=True) + norm_epsilon)
    normed = (wide * inv_one * gain[...]).astype(bf16)
    normed_out[...] = normed
    turned_out[...] = normed.T
    proj = mm(normed, w[...])
    proj_out[...] = proj
    ext[8 : 8 + LEN, :] = proj[:, :QC]
    filtered = filter_rows(ext, conv)
    filtered_out[:, :QC] = filtered
    ext[0:8, :] = ext[LEN : LEN + 8, :]
    active = filtered * jax.nn.sigmoid(filtered)
    payload = active[:, :QW]
    writers = parts_of(active[:, QW : QW + STATE])
    readers = parts_of(active[:, QW + STATE :])
    writer = writers[0]

    steps = softplus(pltpu.roll(proj[:, QC:], place[2], 1) + head[1:2, :])
    rates = head[0:1, :] * steps
    causal = triangle(True)
    summed = running(causal, rates) * LOG2E
    across = summed.T
    affinity = jnp.where(causal, affinity_of(readers, writers), 0.0)

    dosed = payload * spread_product(steps)
    dosed_low = dosed.astype(bf16)
    state = mem[...]
    mem_out[0] = state
    summed_wide = spread_heads(summed, 0, QH)
    grown = jnp.exp2(summed_wide)
    state_low, state_rest = parts_of(state)
    carried = mm(jnp.concatenate(readers, axis=1), jnp.concatenate([state_low] * 2, axis=0))
    carried = (carried + mm(readers[0], state_rest)) * grown
    within = []
    for pair in range(QH // 2):
        weights = []
        for h in (2 * pair, 2 * pair + 1):
            gap = jnp.minimum(summed[:, h : h + 1] - across[h : h + 1, :], 0.0)
            weights.append((jnp.exp2(gap) * affinity).astype(bf16))
        first, second = halves(dosed_low[:, 128 * pair : 128 * pair + 128])
        within.append(
            mm(jnp.concatenate(weights, axis=1), jnp.concatenate([first, second], axis=0))
        )
    scanned_out[...] = jnp.concatenate(within, axis=1) + carried + payload * skip[...]

    last = summed[LEN - 1 : LEN, :]
    last_wide = spread_heads(last, 0, QH)
    remain = jnp.exp2(last_wide - summed_wide)
    added = mm(writer, (dosed * remain).astype(bf16), TN)
    mem[...] = state * jnp.exp2(last_wide) + added
    tail_out[...] = ext[0:8, :]
    state_out[...] = mem[...]


def by_core(core, own, other):
    first = core == 0
    return jnp.where(first, own, other), jnp.where(first, other, own)


def at_hand(side, near_a, far_a, near_b, far_b):
    j = pl.program_id(0)
    near = (j % BLOCKS) // (BLOCKS // 2) == side
    first = jnp.where(near, near_a[...], far_a[...])
    return jnp.where(j < BLOCKS, first, jnp.where(near, near_b[...], far_b[...]))


def gate_kernel(
    place, normed, w_gate, cot_na, cot_fa, cot_nb, cot_fb, w_own, w_other, gain, scanned,
    gate_out, shaped_grad_out, stats_out,
):
    gate = mm(normed[...], w_gate[...])
    cot = at_hand(place[0], cot_na, cot_fa, cot_nb, cot_fb)
    left, right = by_core(place[1], w_own[...], w_other[...])
    grad_shaped = mm(cot[:, :QW], left, NT) + mm(cot[:, QW:], right, NT)
    gate_out[...] = gate
    shaped_grad_out[...] = grad_shaped
    gated = scanned[...] * (gate * jax.nn.sigmoid(gate))
    squares = jnp.sum(gated * gated, axis=1, keepdims=True)
    inner = jnp.sum(grad_shaped * gain[...] * gated, axis=1, keepdims=True)
    lane = lax.broadcasted_iota(jnp.int32, (LEN, 128), 1)
    both = jnp.where(lane == 0, squares, jnp.where(lane == 1, inner, 0.0))
    stats_out[...] = both.T[0:8, :]


def finish_kernel(
    place, stats, gate_in, grad_shaped_in, scanned_in, w_own, w_other, gain,
    turned_out, layer_a_out, layer_b_out, scan_grad_out, gate_grad_out, gain_grad,
):
    j = pl.program_id(0)
    table = jnp.concatenate([stats[...], jnp.zeros((120, LEN), f32)], axis=0).T
    inv_two = lax.rsqrt(table[:, 0:1] / DI + norm_epsilon)
    mean = inv_two * table[:, 1:2] / DI
    gate = gate_in[...]
    scanned = scanned_in[...]
    grad_shaped = grad_shaped_in[...]
    sig = jax.nn.sigmoid(gate)
    lift = gate * sig
    unit = scanned * lift * inv_two
    shaped = (unit * gain[...]).astype(bf16)
    turned_out[...] = shaped.T
    left, right = by_core(place[1], w_own[...], w_other[...])
    layer = jnp.concatenate([mm(shaped, left), mm(shaped, right)], axis=1).astype(bf16)

    @pl.when(j < BLOCKS)
    def _():
        layer_a_out[...] = layer

    @pl.when(j >= BLOCKS)
    def _():
        layer_b_out[...] = layer

    grad_gated = inv_two * (grad_shaped * gain[...] - unit * mean)
    scan_grad_out[...] = grad_gated * lift
    gate_grad_out[...] = (grad_gated * scanned * sig * (1.0 + gate * (1.0 - sig))).astype(bf16)

    @pl.when(j == 0)
    def _():
        gain_grad[...] = jnp.zeros_like(gain_grad)

    gain_grad[0:1, :] += jnp.sum(grad_shaped * unit, axis=0, keepdims=True)


def backward_kernel(
    place, proj_in, filtered_in, scanned_in, grad_in, mem_in, conv, head, skip, later_in, state_in,
    *rest
):
    out, conv_grad, head_grad, skip_grad, later_out, state_out, later, grad_mem = rest[-8:]
    i = pl.program_id(0)

    @pl.when(i == 0)
    def _():
        later[LEN : LEN + 8, :] = later_in[...]
        grad_mem[...] = state_in[...]
        conv_grad[...] = jnp.zeros_like(conv_grad)
        head_grad[...] = jnp.zeros_like(head_grad)
        skip_grad[...] = jnp.zeros_like(skip_grad)

    @pl.when(i > 0)
    def _():
        later[LEN : LEN + 8, :] = later[0:8, :]

    conv_in = proj_in[:, :QC]
    filtered = filtered_in[:, :QC]
    sig = jax.nn.sigmoid(filtered)
    active = filtered * sig
    slope = sig * (1.0 + filtered * (1.0 - sig))
    payload = active[:, :QW]
    writers = parts_of(active[:, QW : QW + STATE])
    readers = parts_of(active[:, QW + STATE :])
    writer, reader = writers[0], readers[0]

    raw = pltpu.roll(proj_in[:, QC:], place[2], 1) + head[1:2, :]
    steps = softplus(raw)
    rates = head[0:1, :] * steps
    summed = running(triangle(True), rates) * LOG2E
    across = summed.T
    upper = triangle(False)
    affinity = jnp.where(upper, affinity_of(writers, readers), 0.0)

    grad = grad_in[...]
    grad_low = grad.astype(bf16)
    grad_rest = grad - grad_low.astype(f32)
    dose = spread_product(steps)
    dosed = payload * dose
    dosed_low = dosed.astype(bf16)
    state = mem_in[0]
    state_grad = grad_mem[...]
    state_grad_low = state_grad.astype(bf16)
    last = summed[LEN - 1 : LEN, :]
    last_wide = spread_heads(last, 0, QH)
    summed_wide = spread_heads(summed, 0, QH)
    remain = jnp.exp2(last_wide - summed_wide)
    from_state = mm(writer, state_grad_low) * remain

    mixed = jnp.zeros((LEN, LEN), f32)
    within = []
    for pair in range(QH // 2):
        lanes = slice(128 * pair, 128 * pair + 128)
        grads = halves(grad_low[:, lanes])
        doses = twice(dosed[:, lanes])
        parts = beside_rest(grad_low[:, lanes], grad_rest[:, lanes])
        weights = []
        for n in range(2):
            h = 2 * pair + n
            gap = jnp.minimum(across[h : h + 1, :] - summed[:, h : h + 1], 0.0)
            decay = jnp.exp2(gap)
            weights.append((decay * affinity).astype(bf16))
            mixed = mixed + decay * mm(doses[n], parts[n], NT)
        within.append(mm(jnp.concatenate(weights, axis=1), jnp.concatenate(grads, axis=0)))
    unit = jnp.concatenate(within, axis=1) + from_state

    payload_grad = dose * unit + skip[...] * grad
    core = scanned_in[...] - payload * skip[...]
    dosed_wide = dosed_low.astype(f32)
    balance = grad_low.astype(f32) * core - dosed_wide * unit
    high_part = balance.astype(bf16)
    low_part = (balance - high_part.astype(f32)).astype(bf16)
    decay_last = jnp.exp2(last_wide)
    at_end = jnp.sum(dosed_wide * from_state, axis=0, keepdims=True) + decay_last * jnp.sum(
        state_grad * state, axis=0, keepdims=True
    )
    end_high = at_end.astype(bf16).astype(f32)
    end_middle = (at_end - end_high).astype(bf16).astype(f32)
    row = lax.broadcasted_iota(jnp.int32, (16, QW), 0)
    end_parts = jnp.where(
        row == 0,
        end_high,
        jnp.where(row == 1, end_middle, jnp.where(row == 2, at_end - end_high - end_middle, 0.0)),
    ).astype(bf16)
    heads_of = (
        lax.broadcasted_iota(jnp.int32, (QW, 128), 0) // HEAD_DIM
        == lax.broadcasted_iota(jnp.int32, (QW, 128), 1)
    ).astype(f32)
    by_head = mm(
        jnp.concatenate([high_part, low_part, (payload * unit).astype(bf16), end_parts], axis=0),
        heads_of.astype(bf16),
    )
    balance_sum = by_head[:LEN] + by_head[LEN : 2 * LEN]
    direct = by_head[2 * LEN : 3 * LEN]
    end_sum = jnp.sum(by_head[3 * LEN :], axis=0, keepdims=True)
    rate_grad = running(upper, balance_sum) + end_sum
    step_grad = direct + head[0:1, :] * rate_grad
    raw_grad = step_grad * jax.nn.sigmoid(raw)
    head_grad[0:1, :] += jnp.sum(rate_grad * rates, axis=0, keepdims=True)
    head_grad[1:2, :] += jnp.sum(raw_grad, axis=0, keepdims=True)
    skip_grad[0:1, :] += jnp.sum(grad * payload, axis=0, keepdims=True)

    grown_wide = jnp.exp2(summed_wide) * grad
    grown_grad = grown_wide.astype(bf16)
    grown_rest = (grown_wide - grown_grad.astype(f32)).astype(bf16)
    kept = (remain * dosed).astype(bf16)
    mixed_low = jnp.where(upper, mixed, 0.0).astype(bf16)
    writer_grad = mm(mixed_low, reader) + mm(kept, state_grad_low, NT)
    state_low = state.astype(bf16)
    reader_grad = (
        mm(mixed_low, writer, TN) + mm(grown_grad, state_low, NT) + mm(grown_rest, state_low, NT)
    )
    grad_mem[...] = decay_last * state_grad + mm(reader, grown_grad, TN)

    filtered_grad = jnp.concatenate([payload_grad, writer_grad, reader_grad], axis=1) * slope
    later[0:LEN, :] = filtered_grad
    back = None
    sums = []
    for k in range(CONV):
        ahead = later[CONV - 1 - k : CONV - 1 - k + LEN, :]
        sums.append(jnp.sum(ahead * conv_in, axis=0, keepdims=True))
        term = conv[k : k + 1, :QC] * ahead
        back = term if back is None else back + term
    sums.append(jnp.sum(filtered_grad, axis=0, keepdims=True))
    conv_grad[...] += jnp.concatenate(sums + [jnp.zeros((7 - CONV, QC), f32)], axis=0)
    out[:, :QC] = back.astype(bf16)
    out[:, QC:] = pltpu.roll(raw_grad, place[3], 1).astype(bf16)
    later_out[...] = later[0:8, :]
    state_out[...] = grad_mem[...]


def outer_kernel(place, left, *rest):
    own, send = rest[-2:]
    total = None
    for n, right in enumerate(rest[:-2]):
        part = mm(left[:, n * HALF : (n + 1) * HALF], right[...])
        total = part if total is None else total + part
    total = total.astype(bf16)
    mine, other = by_core(place[1], total[:, :QW], total[:, QW:])
    own[...] = mine
    send[...] = other


def pieces_kernel(chip_rows, blocks, place, left, right, *rest):
    out, dots = rest[-2:]
    weights, others = rest[:blocks], rest[blocks:-2]
    tile = left.shape[0]
    i = pl.program_id(0)
    per = tile // chip_rows
    steps = out.shape[0] // per
    result = mm(left[...], right[...])
    sums = jnp.zeros((tile, 128), f32)
    for n, weight in enumerate(weights):
        product = result[:, n * GC : (n + 1) * GC] * weight[...].astype(f32)
        sums = sums + (product[:, :128] + product[:, 128:256] + product[:, 256:])
    dots[...] = jnp.broadcast_to(jnp.sum(sums.T, axis=0, keepdims=True), (8, tile))
    for n in range(per):
        part = result[n * chip_rows : (n + 1) * chip_rows].astype(bf16)
        if others:
            out[(i % steps) * per + n, 0, i // steps] = part
        else:
            out[(i % steps) * per + n, i // steps] = part
    if others:
        half = out.shape[0] // 2

        @pl.when(i == 0)
        def _():
            own, other = others
            core = place[1]
            out[pl.ds(core * half, half), 1] = own[...]
            out[pl.ds((1 - core) * half, half), 1] = other[...]


def input_grad(gate_grad, wide_grad, w_gate, w_wide):
    grad = mm(gate_grad[...], w_gate[...], NT) + mm(wide_grad[...], w_wide[...], NT)
    return grad.astype(bf16)


def input_grad_kernel(place, *refs):
    refs[-1][...] = input_grad(*refs[:-1])


def own_first(j, place):
    per = BLOCKS // 2
    half = j // per
    side = place[0]
    return (half + side - 2 * half * side) * per + j % per


def rows_of(width, first=0):
    return pl.BlockSpec((LEN, width), lambda j, *_: (j + first, 0))


def moved_columns(height):
    return pl.BlockSpec(
        (height, LEN),
        lambda j, place: (0, own_first(j % BLOCKS, place) + (j // BLOCKS) * BLOCKS),
    )


def first_rows(width):
    return pl.BlockSpec(
        (LEN, width), lambda j, place: (own_first(jnp.minimum(j, BLOCKS - 1), place), 0)
    )


def second_rows(width):
    return pl.BlockSpec(
        (LEN, width), lambda j, place: (own_first(jnp.maximum(j - BLOCKS, 0), place), 0)
    )


def whole(*shape):
    return pl.BlockSpec(shape, lambda j, *_: (0,) * len(shape))


def params():
    return pltpu.CompilerParams(
        vmem_limit_bytes=60 * MIB, dimension_semantics=("arbitrary",)
    )


def shape(dims, dtype):
    return jax.ShapeDtypeStruct(dims, dtype)


def cost(microseconds):
    return pl.CostEstimate(
        flops=int(microseconds * 1e9),
        bytes_accessed=int(microseconds * 3.5e6),
        transcendentals=0,
    )


def run_forward(place, near, far, gain, w, conv, head, skip, carried, buffers, part):
    per = BLOCKS // 2
    first = part * per
    if buffers is None:
        buffers = ()
    anywhere = pl.BlockSpec(memory_space=pl.ANY)
    return pl.pallas_call(
        functools.partial(forward_kernel, part % 2),
        grid_spec=pltpu.PrefetchScalarGridSpec(
            num_scalar_prefetch=1,
            grid=(per,),
            in_specs=[
                rows_of(D), rows_of(D), whole(1, D), whole(D, WIDE), whole(8, WIDE), whole(8, 128), whole(1, QW),
                whole(8, QC), whole(STATE, QW),
            ] + [anywhere] * len(buffers),
            out_specs=[
                rows_of(D, first), pl.BlockSpec((D, LEN), lambda j, *_: (0, j + first)),
                rows_of(WIDE, first), rows_of(WIDE, first), rows_of(QW, first),
                pl.BlockSpec((1, STATE, QW), lambda j, *_: (j + first, 0, 0)),
                whole(8, QC), whole(STATE, QW),
            ],
            scratch_shapes=[pltpu.VMEM((LEN + 8, QC), f32), pltpu.VMEM((STATE, QW), f32)],
        ),
        out_shape=[
            shape((2 * ROWS, D), bf16), shape((D, 2 * ROWS), bf16),
            shape((2 * ROWS, WIDE), f32), shape((2 * ROWS, WIDE), f32),
            shape((2 * ROWS, QW), f32), shape((2 * BLOCKS, STATE, QW), f32), shape((8, QC), f32), shape((STATE, QW), f32),
        ],
        input_output_aliases={10 + n: n for n in range(len(buffers))},
        compiler_params=params(),
        cost_estimate=cost(13),
        name="forward_scan",
    )(place, near, far, gain, w, conv, head, skip, *carried, *buffers)


def assemble_kernel(count, place, *refs):
    pieces, (gate, own, send) = refs[:count], refs[count:]
    half = count // 2
    for n, piece in enumerate(pieces):
        chip = place[4 + n]
        gate[0, chip] = piece[0, 0]
        gate[1, chip] = piece[0, 1]
        mine = chip // half == place[1]

        @pl.when(mine)
        def _():
            own[chip % half] = piece[1]

        @pl.when(jnp.logical_not(mine))
        def _():
            send[chip % half] = piece[1]


def run_assemble(place, pieces):
    count = len(pieces)
    _, _, rows, width = pieces[0].shape
    outs = [(2, count, rows, width)] + [(count // 2, 2, rows, width)] * 2
    return pl.pallas_call(
        functools.partial(assemble_kernel, count),
        grid_spec=pltpu.PrefetchScalarGridSpec(
            num_scalar_prefetch=1,
            grid=(1,),
            in_specs=[whole(2, 2, rows, width)] * count,
            out_specs=[whole(*dims) for dims in outs],
        ),
        out_shape=[shape(dims, bf16) for dims in outs],
        compiler_params=params(),
        cost_estimate=cost(3),
        name="assemble",
    )(place, *pieces)


def run_gate(place, normed, w_gate, cots, w_out, gain, scanned):
    per = BLOCKS // 2

    def half(sequence, far):
        def index(j, place):
            first = sequence * BLOCKS + (1 - place[0] if far else place[0]) * per
            return (jnp.clip(j - first, 0, per - 1), 0)

        return pl.BlockSpec((LEN, D), index)

    return pl.pallas_call(
        gate_kernel,
        grid_spec=pltpu.PrefetchScalarGridSpec(
            num_scalar_prefetch=1,
            grid=(2 * BLOCKS,),
            in_specs=[
                rows_of(D), whole(D, QW), half(0, False), half(0, True), half(1, False),
                half(1, True), whole(QW, QW), whole(QW, QW), whole(1, QW), rows_of(QW),
            ],
            out_specs=[
                rows_of(QW), rows_of(QW), pl.BlockSpec((8, LEN), lambda j, *_: (0, j)),
            ],
        ),
        out_shape=[
            shape((2 * ROWS, QW), f32), shape((2 * ROWS, QW), f32), shape((8, 2 * ROWS), f32),
        ],
        compiler_params=params(),
        cost_estimate=cost(2),
        name="gate_and_stats",
    )(place, normed, w_gate, *cots, *w_out, gain, scanned)


def run_finish(place, stats, gate, grad_shaped, scanned, w_out, gain):
    return pl.pallas_call(
        finish_kernel,
        grid_spec=pltpu.PrefetchScalarGridSpec(
            num_scalar_prefetch=1,
            grid=(2 * BLOCKS,),
            in_specs=[
                pl.BlockSpec((8, LEN), lambda j, *_: (0, j)), rows_of(QW), rows_of(QW),
                rows_of(QW), whole(QW, QW), whole(QW, QW), whole(1, QW),
            ],
            out_specs=[
                moved_columns(QW), first_rows(D), second_rows(D), rows_of(QW), rows_of(QW),
                whole(8, QW),
            ],
        ),
        out_shape=[
            shape((QW, 2 * ROWS), bf16), shape((ROWS, D), bf16), shape((ROWS, D), bf16),
            shape((2 * ROWS, QW), f32), shape((2 * ROWS, QW), bf16), shape((8, QW), f32),
        ],
        compiler_params=params(),
        cost_estimate=cost(2),
        name="finish",
    )(place, stats, gate, grad_shaped, scanned, *w_out, gain)


def run_backward(
    place, sequence, half, proj, filtered, scanned, grad, mem, conv, head, skip, carried, buffers
):
    per = BLOCKS // 2
    top = sequence * BLOCKS + (half + 1) * per - 1

    def back(width):
        return pl.BlockSpec((LEN, width), lambda i, *_: (top - i, 0))

    args = [place, proj, filtered, scanned, grad, mem, conv, head, skip, *carried]
    return pl.pallas_call(
        backward_kernel,
        grid_spec=pltpu.PrefetchScalarGridSpec(
            num_scalar_prefetch=1,
            grid=(per,),
            in_specs=[
                back(WIDE), back(WIDE), back(QW), back(QW),
                pl.BlockSpec((1, STATE, QW), lambda i, *_: (top - i, 0, 0)),
                whole(8, WIDE), whole(8, 128), whole(1, QW), whole(8, QC), whole(STATE, QW),
            ] + [pl.BlockSpec(memory_space=pl.ANY)] * len(buffers),
            out_specs=[
                back(WIDE), whole(8, QC), whole(8, 128), whole(8, QW), whole(8, QC),
                whole(STATE, QW),
            ],
            scratch_shapes=[pltpu.VMEM((LEN + 8, QC), f32), pltpu.VMEM((STATE, QW), f32)],
        ),
        out_shape=[
            shape((2 * ROWS, WIDE), bf16), shape((8, QC), f32), shape((8, 128), f32),
            shape((8, QW), f32), shape((8, QC), f32), shape((STATE, QW), f32),
        ],
        input_output_aliases={len(args) + n: n for n in range(len(buffers))},
        compiler_params=params(),
        cost_estimate=cost(2),
        name="backward_scan",
    )(*args, *buffers)


def run_outer(place, left, rights):
    tall, width = left.shape[0], rights[0].shape[1]
    tile = 384
    return pl.pallas_call(
        outer_kernel,
        grid_spec=pltpu.PrefetchScalarGridSpec(
            num_scalar_prefetch=1,
            grid=(tall // tile,),
            in_specs=[pl.BlockSpec((tile, 2 * ROWS), lambda i, *_: (i, 0))]
            + [whole(HALF, width) for _ in rights],
            out_specs=[pl.BlockSpec((tile, QW), lambda i, *_: (i, 0))] * 2,
        ),
        out_shape=[shape((tall, QW), bf16)] * 2,
        compiler_params=params(),
        cost_estimate=cost(1),
        name="weight_grad",
    )(place, left, *rights)


def run_pieces(place, left, right, chips, weights, columns, others=()):
    tall, width = left.shape[0], right.shape[1]
    tile = 384
    chip_rows = tall // (2 * chips)
    dims = (chips,) + (2,) * (2 if others else 1) + (chip_rows, width)

    def block(column):
        return pl.BlockSpec((tile, GC), lambda i, *_: (i, column))

    beside_specs = []
    if others:
        part = others[1].shape
        beside_specs = [
            whole(*part),
            whole(*part),
        ]
    return pl.pallas_call(
        functools.partial(pieces_kernel, chip_rows, len(columns)),
        grid_spec=pltpu.PrefetchScalarGridSpec(
            num_scalar_prefetch=1,
            grid=(tall // tile,),
            in_specs=[
                pl.BlockSpec((tile, 2 * ROWS), lambda i, *_: (i, 0)), whole(*right.shape),
            ] + [block(column) for column in columns] + beside_specs,
            out_specs=[whole(*dims), pl.BlockSpec((8, tile), lambda i, *_: (0, i))],
        ),
        out_shape=[shape(dims, bf16), shape((8, tall), f32)],
        compiler_params=params(),
        cost_estimate=cost(1),
        name="weight_grad",
    )(place, left, right, *([weights] * len(columns)), *others)


def tokens_grad_kernel(tok, cot, gain, near, core, *rest):
    sides, out = rest[:-1], rest[-1]
    i = pl.program_id(0)
    rows = out.shape[0]
    parts = [ref[n : n + rows, :] for ref in sides for n in range(0, ref.shape[0], rows)]
    side = parts[0]
    for n in range(1, len(parts)):
        side = jnp.where(i == n, parts[n], side)
    grad = near[...].astype(f32) + core[...].astype(f32) + side.astype(f32)
    wide = tok[...].astype(f32)
    inv_one = lax.rsqrt(jnp.mean(wide * wide, axis=1, keepdims=True) + norm_epsilon)
    unit = wide * inv_one
    lifted = grad * gain[...]
    mean = jnp.mean(lifted * unit, axis=1, keepdims=True)
    out[...] = cot[...].astype(f32) + inv_one * (lifted - unit * mean)


def run_tokens_grad(tokens, cotangent, gain, near, core, sides):
    rows = min(part.shape[0] for part in sides)
    block = pl.BlockSpec((rows, D), lambda i: (i, 0))
    return pl.pallas_call(
        tokens_grad_kernel,
        grid=(HALF // rows,),
        in_specs=[block, block, whole(1, D), block, block]
        + [whole(*part.shape) for part in sides],
        out_specs=block,
        out_shape=shape((HALF, D), f32),
        compiler_params=params(),
        cost_estimate=cost(4),
        name="tokens_grad",
    )(tokens, cotangent, gain, near, core, *sides)


def run_input_grad(place, sequence, far, gate_grad, wide_grad, w_gate, w_wide):
    per = BLOCKS // 2

    def rows(width):
        def index(j, place):
            half = 1 - place[0] if far else place[0]
            return (sequence * BLOCKS + half * per + j, 0)

        return pl.BlockSpec((LEN, width), index)

    return pl.pallas_call(
        input_grad_kernel,
        grid_spec=pltpu.PrefetchScalarGridSpec(
            num_scalar_prefetch=1,
            grid=(per,),
            in_specs=[rows(QW), rows(WIDE), whole(D, QW), whole(D, WIDE)],
            out_specs=rows_of(D),
        ),
        out_shape=shape((HALF, D), bf16),
        compiler_params=params(),
        cost_estimate=cost(1),
        name="input_grad",
    )(place, gate_grad, wide_grad, w_gate, w_wide)


def other_side(block):
    return lax.ppermute(block, "seq", [(0, 1), (1, 0)])


def after(block, *others):
    return lax.optimization_barrier((block, *others))[0]


def tie(*blocks):
    return lax.optimization_barrier(blocks)


def flip(block, bit):
    count = lax.axis_size("dp")
    return lax.ppermute(block, "dp", [(d, d ^ bit) for d in range(count)])


def other_core(block):
    return flip(block, 1)


def beside(block):
    return flip(block, 2)


def along(block):
    count = lax.axis_size("dp")
    return lax.ppermute(block, "dp", [(d, (d + 4) % count) for d in range(count)])


def in_order(place, own, received, axis=0):
    return jnp.where(
        place == 0,
        jnp.concatenate([own, received], axis=axis),
        jnp.concatenate([received, own], axis=axis),
    )


def pick(block, place, axis):
    return lax.dynamic_index_in_dim(block, place, axis, False)


class Spread:
    def __init__(self, piece, groups, put, base, hold=()):
        dp = lax.axis_index("dp")
        self.ring, self.beside_place = dp // 4, (dp // 2) % 2
        self.groups, self.put, self.base = groups, put, base
        self.hop, self.current = 0, piece
        self.neighbour = beside(after(piece, *hold) if hold else piece)

    def place(self, hold=()):
        origin = (self.ring + self.groups - self.hop) % self.groups
        current, neighbour = self.current, self.neighbour
        if hold:
            current, neighbour, *_ = tie(current, neighbour, *hold)
        self.base = self.put(self.base, current, 2 * origin + self.beside_place)
        self.base = self.put(self.base, neighbour, 2 * origin + 1 - self.beside_place)

    def step(self, hold=(), place_hold=()):
        moved = along(self.current)
        if hold:
            moved = after(moved, *hold)
        self.place(place_hold)
        self.hop, self.current, self.neighbour = self.hop + 1, moved, beside(moved)
        return moved


class Collect:
    def __init__(self, block_of, groups):
        dp = lax.axis_index("dp")
        self.ring, self.beside_place = dp // 4, (dp // 2) % 2
        self.block_of, self.groups = block_of, groups
        self.hop, self.total = 0, None
        self.first = self.block(1 - self.beside_place)
        self.received = beside(self.first)

    def block(self, place):
        target = (self.ring + 2 * self.groups - 1 - self.hop) % self.groups
        return self.block_of(2 * target + place)

    def step(self, *hold):
        received = after(self.received, *hold) if hold else self.received
        part = self.block(self.beside_place).astype(f32) + received.astype(f32)
        if self.hop:
            part = part + self.total.astype(f32)
        part = part.astype(bf16)
        self.hop += 1
        if self.hop < self.groups:
            part, following = tie(part, self.block(1 - self.beside_place))
            self.total = along(part)
            self.received = beside(following)
        return part

    def rest(self):
        part = None
        while self.hop < self.groups:
            part = self.step()
        return part


def gather_small(row, hold, later):
    dp = lax.axis_index("dp")
    block = row.reshape((1, 1) + row.shape)
    block = hold(in_order(lax.axis_index("seq"), block, other_side(block), axis=0))
    bit = 1
    while bit < lax.axis_size("dp"):
        received = flip(block, bit)
        if bit in later:
            received = after(received, later[bit])
        block = in_order((dp // bit) % 2, block, received, axis=1)
        bit *= 2
    return block.reshape((-1,) + row.shape)


def sum_small(block, bit, hold):
    while bit < lax.axis_size("dp"):
        block = block + after(flip(block, bit), hold)
        bit *= 2
    return block


def columns_of(block, half):
    return lax.dynamic_slice(block, (0, half * QW), (block.shape[0], QW))


def adamw_step(weight, moment, square, gradient, step_rate, decay_rate):
    moment_new = beta_first * moment + (1.0 - beta_first) * gradient
    square_new = beta_second * square + (1.0 - beta_second) * gradient * gradient
    first_fix = moment_new / (1.0 - beta_first**STEP)
    second_fix = square_new / (1.0 - beta_second**STEP)
    weight_new = weight - step_rate * (
        first_fix / (jnp.sqrt(second_fix) + adam_epsilon) + decay_rate * weight
    )
    return (weight_new, moment_new, square_new)


def to_side(halves_of, side):
    return in_order(side, halves_of(side)[None], other_side(halves_of(1 - side))[None])


def to_core(pair, quarter_of, core):
    return in_order(
        core, quarter_of(pair, core)[:, None], other_core(quarter_of(pair, 1 - core))[:, None], 1
    )


def from_cores(piece, core):
    return in_order(core, pick(piece, core, 1), other_core(pick(piece, 1 - core, 1)), 2)


def from_sides(cores, side, *hold):
    received = after(other_side(pick(cores, 1 - side, 0)), *hold)
    return in_order(side, pick(cores, side, 0), received, 1)


def from_cores_shared(piece, core):
    mine, got = pick(piece, core, 1), other_core(pick(piece, 1 - core, 1))
    cores = in_order(core, mine[:, :, :QW], got[:, :, :QW], 2)
    shared = (mine[:, :, QW:].astype(f32) + got[:, :, QW:].astype(f32)).astype(bf16)
    return jnp.concatenate([cores, shared], axis=2)


def from_sides_shared(both, side):
    mine, got = pick(both, side, 0), other_side(pick(both, 1 - side, 0))
    sides = in_order(side, mine[:, : 2 * QW], got[:, : 2 * QW], 1)
    return sides, mine[:, 2 * QW :].astype(f32) + got[:, 2 * QW :].astype(f32)


def on_device(
    tokens,
    cotangent,
    in_weight,
    in_moment,
    in_square,
    out_weight,
    out_moment,
    out_square,
    conv_table,
    conv_moment,
    conv_square,
    norm_gains,
    gain_moment,
    gain_square,
    head_table,
    head_moment,
    head_square,
):
    side = lax.axis_index("seq")
    dp = lax.axis_index("dp")
    core = dp % 2
    groups = lax.axis_size("dp") // 4
    chips = 2 * groups
    quarter = 2 * side + core
    number = side * lax.axis_size("dp") + dp
    turn = quarter * QH
    place = jnp.stack([side, core, 128 - turn, turn]).astype(jnp.int32)
    in_rows, out_rows = in_weight.shape[0], out_weight.shape[0]
    chip_rows = 2 * in_rows

    low = in_weight.astype(bf16)
    shared_own = jnp.pad(low[:, 2 * DI :], ((0, 0), (0, GC - 2 * STATE - HEADS)))

    def wide_half(side):
        own = lax.dynamic_slice(low, (0, DI + side * 2 * QW), (in_rows, 2 * QW))
        return jnp.concatenate([own, shared_own], axis=1)

    def wide_quarter(pair, core):
        own = lax.dynamic_slice(pair, (0, 0, core * QW), (2, in_rows, QW))
        return jnp.concatenate([own, pair[:, :, 2 * QW :]], axis=2)

    def gate_half(side):
        return lax.dynamic_slice(low, (0, side * 2 * QW), (in_rows, 2 * QW))

    def gate_quarter(pair, core):
        return lax.dynamic_slice(pair, (0, 0, core * QW), (2, in_rows, QW))

    wide_pair = to_side(wide_half, side)
    low, wide_pair = tie(low, wide_pair)
    gate_pair = to_side(gate_half, side)
    wide_piece = to_core(wide_pair, wide_quarter, core).reshape(2, chip_rows, WIDE)
    gate_piece = to_core(gate_pair, gate_quarter, core).reshape(4 * in_rows, QW)

    def put_in(base, piece, chip):
        return lax.dynamic_update_slice(base, piece[:, None], (0, chip, 0, 0))

    wide_spread = Spread(
        wide_piece, groups, put_in, jnp.zeros((2, chips, chip_rows, WIDE), bf16)
    )

    conv_width, gain_width = conv_table.shape[1], norm_gains.shape[0]
    small_size = 5 * conv_width + gain_width
    small_pad = -(-small_size // 128) * 128
    small_row = jnp.concatenate(
        [conv_table.astype(bf16).reshape(-1), norm_gains.astype(bf16)]
    )
    wide_hops = [wide_spread.step() for _ in range(groups - 1)]
    small_all = gather_small(
        jnp.pad(small_row, (0, small_pad - small_size)),
        lambda block: after(block, wide_hops[0]),
        {4: wide_hops[1]},
    )
    small_all = after(small_all, wide_hops[-1])
    devices = small_all.shape[0]
    conv_full = small_all[:, : 5 * conv_width].reshape(devices, 5, conv_width)
    conv_full = conv_full.transpose(1, 0, 2).reshape(5, CH).astype(f32)
    gains_full = small_all[:, 5 * conv_width : small_size].reshape(1, D + DI).astype(f32)
    first_gain = gains_full[:, :D]
    second_gain = lax.dynamic_slice(gains_full, (0, D + quarter * QW), (1, QW))
    conv_own = jnp.concatenate(
        [lax.dynamic_slice(conv_full, (0, quarter * QW), (5, QW)), conv_full[:, DI:]], axis=1
    )
    conv_own = jnp.pad(conv_own, ((0, 3), (0, WIDE - QC)))
    head_own = lax.dynamic_slice(head_table, (0, quarter * QH), (3, QH))
    head_rows = jnp.concatenate([-jnp.exp(head_own[0:1]), head_own[1:2]], axis=0)
    head_rows = jnp.pad(head_rows, ((0, 6), (0, 128 - QH)))
    skip = jnp.repeat(head_own[2:3], HEAD_DIM, axis=1)

    small = (first_gain, second_gain, conv_own, head_rows, skip)
    wide_spread.place()
    w_wide = wide_spread.base.reshape(D, WIDE)

    tokens_sent, gate_piece = tie(tokens, gate_piece)
    tok_far = other_side(tokens_sent)
    cotangent_sent, tok_far = tie(cotangent, tok_far)
    tok_near_b, tok_far_b = other_core(tokens), other_core(tok_far)

    out_low = out_weight.astype(bf16)
    out_piece = in_order(
        core, columns_of(out_low, core), other_core(columns_of(out_low, 1 - core))
    )
    both_piece = jnp.stack([gate_piece, out_piece]).reshape(2, 2, chip_rows, QW)
    both_piece = after(both_piece, wide_hops[-1])

    def keep(base, piece, chip):
        return base + [(piece, chip)]

    both_spread = Spread(both_piece, groups, keep, [], (w_wide,))
    cot_far = other_side(cotangent_sent)
    cots = (cotangent, cot_far, other_core(cotangent), other_core(cot_far))

    start = (jnp.zeros((8, QC), f32), jnp.zeros((STATE, QW), f32))
    buffers, carried = None, start
    gain = first_gain
    for part in range(4):
        near, far = (tok_near_b, tok_far_b) if part >= 2 else (tokens, tok_far)
        *buffers, tail, state = run_forward(
            place, near, far, gain, w_wide, conv_own, head_rows, skip,
            carried if part % 2 else start, buffers, part,
        )
        carried = (tail, state)
        if both_spread.hop < groups - 1:
            moved = both_spread.step((buffers[0],), (buffers[0],))
            waits = [piece for piece, _ in both_spread.base[-2:]]
            gain = after(first_gain, moved, *waits)
    while both_spread.hop < groups - 1:
        both_spread.step()
    both_spread.place((buffers[0],))
    pieces, origins = zip(*both_spread.base)
    w_gate, w_own, w_send = run_assemble(
        jnp.concatenate([place, jnp.stack(origins).astype(jnp.int32)]), pieces
    )
    w_gate = w_gate.reshape(D, QW)
    w_out = (w_own.reshape(QW, QW), other_core(w_send).reshape(QW, QW))
    normed, normed_turned, proj, filtered, scanned, mem = buffers
    gate, grad_shaped, stats = run_gate(
        place, normed, w_gate, cots, w_out, second_gain, scanned
    )
    stats = stats + other_side(stats)
    swapped = other_core(stats)
    stats = stats + jnp.concatenate([swapped[:, ROWS:], swapped[:, :ROWS]], axis=1)
    shaped_turned, layer_a, layer_b, scan_grad, gate_grad, gain_grad = run_finish(
        place, stats, gate, grad_shaped, scanned, w_out, second_gain
    )

    layer_far = other_core(layer_b)
    out_grad, out_send = run_outer(place, shaped_turned, cots)
    layer_far, out_grad = tie(layer_far, out_grad)
    layer_send = (layer_a[HALF:].astype(f32) + layer_far[HALF:].astype(f32)).astype(bf16)
    layer_side = other_side(layer_send)

    split = (chips // 2, 2, chip_rows)
    out_far = other_core(out_send).reshape(*split, QW)
    out_pieces = (out_grad.reshape(*split, QW), out_far)
    both_pieces, gate_dots = run_pieces(
        place, normed_turned, after(gate_grad, layer_send), chips, w_gate, (0, 1), out_pieces
    )

    def blocks_of(pieces):
        return lambda chip: pick(pieces, chip, 0)

    both_sums = Collect(blocks_of(both_pieces), groups)

    waits = (both_pieces,)
    buffers, sums = (), []
    for sequence in (1, 0):
        carried = start
        for half in (1, 0):
            wide_grad, *part_sums, later, state = run_backward(
                place, sequence, half, proj, filtered, scanned, after(scan_grad, *waits), mem,
                conv_own, head_rows, skip, carried, buffers,
            )
            buffers, carried = (wide_grad,), (later, state)
            sums.append(part_sums)
            both_sum = both_sums.step(part_sums[0])
            waits = (both_sum,)
            if len(sums) == 2:
                waits = (both_sum, layer_side)
    both_sum = both_sums.rest() if groups > 4 else both_sum
    conv_grad, head_grad, skip_grad = (sum(parts[1:], parts[0]) for parts in zip(*sums))
    rest_pieces, rest_dots = run_pieces(
        place, normed_turned, after(wide_grad, both_sum), chips, w_wide, (0, 1, 2)
    )
    rest_sums = Collect(blocks_of(rest_pieces), groups)
    both_sum, wide_grad = tie(both_sum, wide_grad)
    gate_cores = from_cores(both_sum[0].reshape(2, 2, in_rows, QW), core)
    out_rows_sum = both_sum[1].reshape(2, out_rows, QW)
    out_rows_far = other_core(pick(out_rows_sum, 1 - core, 0))

    skip_grad = skip_grad[0].reshape(QH, HEAD_DIM).sum(axis=1)
    conv_all = jnp.concatenate(
        [
            lax.dynamic_update_slice(
                jnp.zeros((5, DI), f32), conv_grad[:5, :QW], (0, quarter * QW)
            ),
            conv_grad[:5, QW:],
        ],
        axis=1,
    )
    gains_all = jnp.concatenate(
        [
            (gate_dots + rest_dots)[0:1] / first_gain,
            lax.dynamic_update_slice(jnp.zeros((1, DI), f32), gain_grad[0:1], (0, quarter * QW)),
        ],
        axis=1,
    )
    heads_all = lax.dynamic_update_slice(
        jnp.zeros((3, HEADS), f32),
        jnp.concatenate([head_grad[0:2, :QH], skip_grad[None]], axis=0),
        (0, quarter * QH),
    )
    packed = jnp.concatenate(
        [
            conv_all.reshape(-1, 128),
            gains_all.reshape(-1, 128),
            jnp.pad(heads_all.reshape(-1), (0, 256 - 3 * HEADS)).reshape(2, 128),
        ],
        axis=0,
    )

    def input_rows(sequence, far, *waits):
        return run_input_grad(
            place, sequence, far, gate_grad, after(wide_grad, *waits), w_gate, w_wide
        )

    far_b = input_rows(1, True, rest_sums.first, packed, gate_cores, out_rows_far)
    far_core = other_core(far_b)
    packed = packed + after(other_side(packed), far_b)
    far_a = input_rows(0, True, packed)
    rest_sum = rest_sums.step(far_a)
    gate_sum = from_sides(gate_cores, side, rest_sum)
    packed = packed + after(other_core(packed), far_a)
    grad_send = (far_a.astype(f32) + far_core.astype(f32)).astype(bf16)
    near_b = input_rows(1, False, rest_sum, grad_send, packed, gate_sum)
    part = HALF // 4
    sides = [other_side(grad_send[:part])]
    near_core = other_core(near_b)
    sides[0], near_b = tie(sides[0], near_b)
    rest_sum = rest_sums.step(sides[0])
    near_a = input_rows(0, False, rest_sum)
    sides.append(other_side(grad_send[part : 2 * part]))
    sides.append(other_side(grad_send[2 * part : 3 * part]))
    sides[1], near_a = tie(sides[1], near_a)
    rest_sum = rest_sums.step(sides[1])
    out_rows_sum = after(out_rows_sum, rest_sum)
    layer_side = after(layer_side, rest_sum)
    layer_out = (
        tokens.astype(f32) + layer_a[:HALF].astype(f32) + layer_far[:HALF].astype(f32)
    ) + layer_side.astype(f32)
    sides[2], rest_sum, layer_out = tie(sides[2], rest_sum, layer_out)
    rest_sum = rest_sums.step(sides[2])
    if rest_sums.hop < groups:
        rest_sum = rest_sums.rest()
    sides.append(other_side(grad_send[3 * part :]))
    out_grad = in_order(core, pick(out_rows_sum, core, 0), out_rows_far, axis=1).astype(f32)

    both_group, rest_sum = tie(
        from_cores_shared(rest_sum.reshape(2, 2, in_rows, WIDE), core), rest_sum
    )
    packed = after(packed, rest_sum)
    packed = packed + after(flip(packed, 2), both_group)
    rest_sum, shared_sum = from_sides_shared(both_group, side)
    packed = packed + after(flip(packed, 4), rest_sum)
    tokens_grad = run_tokens_grad(
        tokens, cotangent, after(first_gain, rest_sum), near_a, near_core, sides
    )
    packed = sum_small(packed, 8, tokens_grad)
    conv_rows, gain_rows = 5 * CH // 128, (D + DI) // 128
    conv_sum = lax.dynamic_slice(
        packed[:conv_rows].reshape(5, CH), (0, number * conv_width), (5, conv_width)
    )
    gains_sum = lax.dynamic_slice(
        packed[conv_rows : conv_rows + gain_rows].reshape(-1), (number * gain_width,), (gain_width,)
    )
    head_sum = packed[conv_rows + gain_rows :].reshape(-1)[: 3 * HEADS].reshape(3, HEADS)

    in_grad = jnp.concatenate(
        [gate_sum.astype(f32), rest_sum.astype(f32), shared_sum[:, : 2 * STATE + HEADS]], axis=1
    )
    in_new = adamw_step(in_weight, in_moment, in_square, in_grad, rate_matrix, weight_decay)
    out_new = adamw_step(out_weight, out_moment, out_square, out_grad, rate_matrix, weight_decay)
    conv_new = adamw_step(conv_table, conv_moment, conv_square, conv_sum, rate_vector, 0.0)
    gains_new = adamw_step(norm_gains, gain_moment, gain_square, gains_sum, rate_vector, 0.0)
    head_new = adamw_step(head_table, head_moment, head_square, head_sum, rate_heads, 0.0)
    return (layer_out, tokens_grad, *in_new, *out_new, *conv_new, *gains_new, *head_new)


def solution(mesh):
    tokens = P(("dp", "seq"), None)
    rows = P(("seq", "dp"), None)
    columns = P(None, ("seq", "dp"))
    line = P(("seq", "dp"))
    return jax.shard_map(
        on_device,
        mesh=mesh,
        in_specs=(tokens,) * 2 + (rows,) * 6 + (columns,) * 3 + (line,) * 3 + (P(),) * 3,
        out_specs=(tokens,) * 2 + (rows,) * 6 + (columns,) * 3 + (line,) * 3 + (P(),) * 3,
        check_vma=False,
    )
```
